32 devices in a mesh: pool: 2 (over x), dev: 16 (over z, y, core).
Axes of the slice: x: 2, y: 2, z: 4, core: 2. Of those that a mesh axis runs over, the one named last changes fastest.
Arguments:
- queries: bfloat16 [512, 4096], P(('pool', 'dev')), may hold values from -6 to 6
- new_kv: bfloat16 [512, 512], P(('pool', 'dev')), may hold values from -6 to 6
- kv_pages: bfloat16 [4096, 16, 512], P(('pool', 'dev')), may hold values from -6 to 6
- page_table: int32 [512, 16], P(('pool', 'dev')), may hold values from 0 to 143, as said below
- lengths: int32 [512], P(('pool', 'dev')), may hold values from 1 to 256, as said below
- shed_slots: int32 [512], P(('pool', 'dev')), may hold values from 0 to 127, as said below
- residual: bfloat16 [512, 4096], P(('pool', 'dev')), may hold values from -6 to 6
- norm_gain: float32 [4096], replicated, may hold values from 0.1 to 1.9
- expert_ids: int32 [512, 8], P(('pool', 'dev')), may hold values from 0 to 31, all different within a row; in each aligned block of 16 rows (0 to 15, 16 to 31, ...) at most 8 rows name the same one
- gate_weights: float32 [512, 8], P(('pool', 'dev')), may hold values from 0.05 to 0.6
- w_gate_up: bfloat16 [32, 4096, 1536], P(('pool', 'dev')), may hold values from -0.09375 to 0.09375
- w_down: bfloat16 [32, 768, 4096], P(('pool', 'dev')), may hold values from -0.21875 to 0.21875
Outputs:
- attended: bfloat16 [512, 4096], P(('pool', 'dev'))
- layer_out: bfloat16 [512, 4096], P(('pool', 'dev'))
The draws below stay inside these ranges and needn't reach their ends.
Inputs may be any that keep to these rules, and one draw needn't show every extreme that they name: `page_table`: entry p of request r is used for p < ceil(lengths[r] / 16) and is 0 otherwise. The used entries of one device's requests are distinct. Of two partners exactly one sheds: its used entries take every value from 0 to 143; the other's stay below 128. `lengths`: A device that sheds has a request of 256 tokens. `shed_slots`: for a device that sheds: distinct pages of the partner's block that no request of the partner uses. For the other device the list is not read. `expert_ids`: among the 16 requests of one device at most 8 name the same expert; the 8 experts of a request differ.
All inputs are finite; a program needn't handle non-finite values.
Results may differ from the reference program's by a relative error of at most 0.014.
Values may be sent and summed in bfloat16 or wider, within the bound.
No kernel may reach another device: no remote copies, remote signals or barrier semaphores. Data moves between devices by JAX's collectives and lax.ppermute only.
A program may use at most 128 MiB of HBM per device.

```python
import math
import jax
import jax.numpy as jnp
import numpy as np
from jax import lax

D = 4096
HEAD_DIMENSION = 128
TOPK = 8
HQ = 32
KEY_VALUE_HEADS = 2
MF = 768
PAGE = 16
MAXP = 16
R_DEV = 16
QUERY_GROUP_SIZE = 16
KVW = 512
PAGES_DEV = 128
SHED = 16
REQUESTS = 512
EXPERTS = 32
CAP = 8


def base_values(key, shape):
    return jnp.clip(jax.random.normal(key, shape, jnp.float32), -6.0, 6.0)


def page_plan(key):
    streams = jax.random.split(jax.random.fold_in(key, 4242), 6)
    device_count = REQUESTS // R_DEV
    half_count = device_count // 2
    pair_count = R_DEV // 2
    low_heavy = jax.random.randint(streams[0], (half_count,), 0, 2)
    heavy_mask = jnp.concatenate([low_heavy, 1 - low_heavy]) == 1
    heavy_pages = jax.random.randint(streams[1], (device_count, pair_count), 2, MAXP + 1)
    heavy_pages = heavy_pages.at[:, 0].set(MAXP)
    heavy_pages = jnp.stack([heavy_pages, MAXP + 2 - heavy_pages], axis=-1).reshape(device_count, R_DEV)
    light_pages = jax.random.randint(streams[2], (device_count, pair_count), 1, MAXP // 2 + 1)
    light_pages = jnp.stack([light_pages, MAXP // 2 + 1 - light_pages], axis=-1).reshape(device_count, R_DEV)
    page_counts = jnp.where(heavy_mask[:, None], heavy_pages, light_pages)
    last_fill = jax.random.randint(streams[3], (device_count, R_DEV), 1, PAGE + 1)
    length_rows = (page_counts - 1) * PAGE + last_fill
    length_rows = length_rows.at[:, 0].set(jnp.where(heavy_mask, MAXP * PAGE, length_rows[:, 0]))
    starts = jnp.cumsum(page_counts, axis=1) - page_counts
    column = jnp.arange(MAXP)
    flat_index = starts[:, :, None] + column[None, None, :]
    in_use = column[None, None, :] < page_counts[:, :, None]
    heavy_total = PAGES_DEV + SHED
    heavy_order = jax.vmap(lambda stream: jax.random.permutation(stream, heavy_total))(jax.random.split(streams[4], device_count))
    light_order = jax.vmap(lambda stream: jax.random.permutation(stream, PAGES_DEV))(jax.random.split(streams[5], device_count))
    light_padded = jnp.concatenate([light_order, jnp.zeros((device_count, SHED), light_order.dtype)], axis=1)
    page_order = jnp.where(heavy_mask[:, None], heavy_order, light_padded)
    clipped = jnp.clip(flat_index, 0, heavy_total - 1).reshape(device_count, R_DEV * MAXP)
    entries = jnp.take_along_axis(page_order, clipped, axis=1).reshape(device_count, R_DEV, MAXP)
    page_rows = jnp.where(in_use, entries, 0)
    light_used = pair_count * (MAXP // 2 + 1)
    spare_slots = light_order[:, light_used:light_used + SHED]
    partner = (jnp.arange(device_count) + half_count) % device_count
    unread_lists = jax.random.randint(jax.random.fold_in(key, 5151), (device_count, SHED), 0, PAGES_DEV)
    unread_lists = unread_lists.at[:, 0].set(0)
    unread_lists = unread_lists.at[:, SHED - 1].set(PAGES_DEV - 1)
    shed_rows = jnp.where(heavy_mask[:, None], spare_slots[partner], unread_lists)
    return (page_rows.reshape(REQUESTS, MAXP).astype(jnp.int32), length_rows.reshape(REQUESTS).astype(jnp.int32), shed_rows.reshape(device_count * SHED).astype(jnp.int32))


def draw_queries(key, part):
    base_rows = base_values(jax.random.fold_in(key, 1), (REQUESTS, HQ * HEAD_DIMENSION))
    return base_rows.astype(jnp.bfloat16)


def draw_new_kv(key, part):
    base_rows = base_values(jax.random.fold_in(key, 2), (REQUESTS, KVW))
    return base_rows.astype(jnp.bfloat16)


def draw_kv_pages(key, part):
    device_count = REQUESTS // R_DEV
    base_rows = base_values(jax.random.fold_in(key, 3), (device_count * PAGES_DEV, PAGE, KVW))
    return base_rows.astype(jnp.bfloat16)


def draw_page_table(key, part):
    return page_plan(key)[0]


def draw_lengths(key, part):
    return page_plan(key)[1]


def draw_shed_slots(key, part):
    return page_plan(key)[2]


def level_of(key, shape, pieces, smallest, top_value):
    factor_of = 1.0
    for dim, blocks in pieces:
        steps = jax.random.uniform(jax.random.fold_in(jax.random.fold_in(key, 6), dim), (blocks,), jnp.float32, smallest / len(pieces), top_value / len(pieces))
        factor_of = factor_of * jnp.repeat(jnp.exp(steps), shape[dim] // blocks).reshape((-1,) + (1,) * (len(shape) - 1 - dim))
    return factor_of


def deal_out(key, own, number, rows, count, top, most, slope):
    ranking = jax.random.permutation(key, count)
    crowded, common = portions_of(count, rows * top, most, slope, True), portions_of(count, rows * top, most, slope, False)
    places = jnp.arange(count)

    def named(sizes, turn):
        used = int((sizes > 0).sum())
        fixed = max(1, used // 4)
        moved = fixed + (places - fixed + turn * (used - fixed)) % max(1, count - fixed)
        return jnp.zeros((count,), jnp.int32).at[ranking[jnp.where(places < fixed, places, moved)]].set(jnp.asarray(sizes, jnp.int32))

    sizes = jnp.where(number % 4 == 0, named(crowded, number // 4), named(common, number - number // 4 - 1))
    mixed = jax.random.permutation(jax.random.fold_in(own, 3), count)
    source_of, taker = mixed[0:count // 2 * 2:2], mixed[1:count // 2 * 2:2]
    room = jnp.minimum(sizes[source_of] - 1, most - sizes[taker]) // 2
    room = jnp.where((source_of == ranking[0]) | (taker == ranking[0]) | (sizes[taker] == 0), 0, jnp.maximum(room, 0))
    moved = jax.random.randint(jax.random.fold_in(own, 4), (count // 2,), 0, 1 << 20) % (room + 1)
    sizes = sizes.at[source_of].add(-moved).at[taker].add(moved)
    members = jnp.searchsorted(jnp.cumsum(sizes), jnp.arange(rows * top), side="right").astype(jnp.int32)
    listing = members.reshape(top, rows).T
    listing = listing[jax.random.permutation(jax.random.fold_in(own, 1), rows)]
    turn = jax.random.randint(jax.random.fold_in(own, 2), (rows, 1), 0, top)
    return jnp.take_along_axis(listing, (jnp.arange(top)[None, :] + turn) % top, axis=1)


def portions_of(count, total, bound, lean, full):
    portions = [(1 << 20) // math.isqrt(grade ** lean) + 1 for grade in range(1, count + 1)]
    largest = bound if full else min(bound, max(-(-total // count), total * portions[0] // sum(portions)))
    least = 1 if total - largest >= count - 1 else 0
    counts, spare = [largest] + [least] * (count - 1), total - largest - least * (count - 1)
    while spare > 0:
        free = [i for i in range(1, count) if counts[i] < largest] or [i for i in range(1, count) if counts[i] < bound]
        mass, left = sum([portions[i] for i in free]), spare
        for i in free:
            addition = min(bound - counts[i], max(1, left * portions[i] // mass), spare)
            counts[i] = counts[i] + addition
            spare = spare - addition
    return np.array(counts)


def noise(stream_key, shape, scale, reach, cuts=(), kind=jnp.bfloat16):
    level = level_of(stream_key, shape, cuts, -0.22, 0.18) if cuts else 1.0
    array = jax.random.normal(stream_key, shape, jnp.float32) * scale * level
    return jnp.minimum(jnp.maximum(array, -reach), reach).astype(kind)


def setup_inputs(seed: int = 0) -> dict:
    seeds = jax.random.split(jax.random.key(seed), 13)
    queries = draw_queries(jax.random.fold_in(seeds[12], 71), 0)
    new_kv = draw_new_kv(jax.random.fold_in(seeds[12], 71), 0)
    kv_pages = draw_kv_pages(jax.random.fold_in(seeds[12], 71), 0)
    page_table = draw_page_table(jax.random.fold_in(seeds[12], 71), 0)
    lengths = draw_lengths(jax.random.fold_in(seeds[12], 71), 0)
    shed_slots = draw_shed_slots(jax.random.fold_in(seeds[12], 71), 0)
    residual = noise(seeds[6], (REQUESTS, D), 1.0, 6.0, ((0, 32),))
    norm_gain = jnp.clip(1.0 + 0.18 * jax.random.normal(seeds[7], (D,), jnp.float32), 0.1, 1.9)
    expert_ids_keys = jax.random.split(jax.random.fold_in(seeds[8], 1), REQUESTS // R_DEV)
    expert_ids_turns = jax.random.permutation(jax.random.fold_in(seeds[8], 3), REQUESTS // R_DEV)
    expert_ids = jax.vmap(lambda own, number: deal_out(jax.random.fold_in(seeds[8], 2), own, number, R_DEV, EXPERTS, TOPK, CAP, 2))(expert_ids_keys, expert_ids_turns).reshape((REQUESTS, TOPK))
    gate_weights = jnp.clip(jnp.exp(math.log(0.6) - 2.4849067 * jax.random.uniform(seeds[9], (REQUESTS, TOPK), jnp.float32) ** level_of(seeds[9], (REQUESTS, TOPK), ((0, 32),), -0.2, 0.2)), 0.05, 0.6)
    w_gate_up = noise(seeds[10], (EXPERTS, D, 2 * MF), D ** -0.5, 0.09375, ((0, 32),))
    w_down = noise(seeds[11], (EXPERTS, MF, D), MF ** -0.5, 0.21875, ((0, 32),))
    return dict(queries=queries, new_kv=new_kv, kv_pages=kv_pages, page_table=page_table, lengths=lengths, shed_slots=shed_slots, residual=residual, norm_gain=norm_gain, expert_ids=expert_ids, gate_weights=gate_weights, w_gate_up=w_gate_up, w_down=w_down)


masked_score = -1e+30
epsilon = 1e-06
highest = lax.Precision.HIGHEST

def attend_rows(source, table_rows, length_rows, query_entries, incoming_rows):
    count_of_rows = table_rows.shape[0]
    key_row_width = incoming_rows.shape[-1] // 2
    collected_rows = jnp.take(source, table_rows, axis=0).reshape(count_of_rows, -1, source.shape[-1])
    key_entries = collected_rows[:, :, :key_row_width].reshape(count_of_rows, -1, KEY_VALUE_HEADS, HEAD_DIMENSION).astype(jnp.float32)
    value_entries = collected_rows[:, :, key_row_width:].reshape(count_of_rows, -1, KEY_VALUE_HEADS, HEAD_DIMENSION).astype(jnp.float32)
    query_head_block = query_entries.reshape(count_of_rows, KEY_VALUE_HEADS, QUERY_GROUP_SIZE, HEAD_DIMENSION).astype(jnp.float32)
    scaling = 1.0 / math.sqrt(HEAD_DIMENSION)
    scores = jnp.einsum('rkgd,rlkd->rkgl', query_head_block, key_entries, precision=highest) * scaling
    positions = jnp.arange(key_entries.shape[1], dtype=jnp.int32)
    allowed = positions[None, :] < length_rows[:, None]
    scores = jnp.where(allowed[:, None, None, :], scores, masked_score)
    incoming_keys = incoming_rows[:, :key_row_width].reshape(count_of_rows, KEY_VALUE_HEADS, HEAD_DIMENSION).astype(jnp.float32)
    incoming_values = incoming_rows[:, key_row_width:].reshape(count_of_rows, KEY_VALUE_HEADS, HEAD_DIMENSION).astype(jnp.float32)
    fresh_score = jnp.einsum('rkgd,rkd->rkg', query_head_block, incoming_keys, precision=highest) * scaling
    largest = jnp.maximum(lax.optimization_barrier(jnp.max(scores, axis=-1)), fresh_score)
    weights = jnp.exp(scores - largest[..., None])
    fresh_weight = jnp.exp(fresh_score - largest)
    denominator = lax.optimization_barrier(jnp.sum(weights, axis=-1)) + fresh_weight
    weights_low = lax.optimization_barrier(weights.astype(jnp.bfloat16)).astype(jnp.float32)
    fresh_low = lax.optimization_barrier(fresh_weight.astype(jnp.bfloat16)).astype(jnp.float32)
    summed = jnp.einsum('rkgl,rlkd->rkgd', weights_low, value_entries, precision=highest)
    summed = summed + fresh_low[..., None] * incoming_values[:, :, None, :]
    return (summed / denominator[..., None]).reshape(count_of_rows, -1).astype(jnp.bfloat16)

def expert_rows(tokens, gate_up, down_proj):
    hidden_dim = down_proj.shape[0]
    product = jnp.dot(tokens, gate_up, preferred_element_type=jnp.float32)
    hidden = (jax.nn.silu(product[:, :hidden_dim]) * product[:, hidden_dim:]).astype(jnp.bfloat16)
    return jnp.dot(hidden, down_proj, preferred_element_type=jnp.float32).astype(jnp.bfloat16)

def reference(queries, new_kv, kv_pages, page_table, lengths, shed_slots, residual, norm_gain, expert_ids, gate_weights, w_gate_up, w_down):
    device_count = REQUESTS // R_DEV

    def per_device(device_index):
        row_start = (device_index * R_DEV).astype(jnp.int32)
        partner = ((device_index + device_count // 2) % device_count).astype(jnp.int32)
        own_pages = lax.dynamic_slice_in_dim(kv_pages, (device_index * PAGES_DEV).astype(jnp.int32), PAGES_DEV, 0)
        other_pages = lax.dynamic_slice_in_dim(kv_pages, (partner * PAGES_DEV).astype(jnp.int32), PAGES_DEV, 0)
        hosted = lax.dynamic_slice_in_dim(shed_slots, (device_index * SHED).astype(jnp.int32), SHED, 0)
        combined = jnp.concatenate([own_pages, jnp.take(other_pages, hosted, axis=0)], axis=0)
        table_rows = lax.dynamic_slice_in_dim(page_table, row_start, R_DEV, 0)
        length_rows = lax.dynamic_slice_in_dim(lengths, row_start, R_DEV, 0)
        query_entries = lax.dynamic_slice_in_dim(queries, row_start, R_DEV, 0)
        incoming_rows = lax.dynamic_slice_in_dim(new_kv, row_start, R_DEV, 0)
        return attend_rows(combined, table_rows, length_rows, query_entries, incoming_rows)
    attended = lax.map(per_device, jnp.arange(device_count, dtype=jnp.int32)).reshape(REQUESTS, D)
    merged = (residual.astype(jnp.float32) + attended.astype(jnp.float32)).astype(jnp.bfloat16)
    merged_wide = merged.astype(jnp.float32)
    normed = (merged_wide * lax.rsqrt(lax.optimization_barrier(jnp.mean(merged_wide * merged_wide, axis=-1, keepdims=True)) + epsilon) * norm_gain).astype(jnp.bfloat16)
    limit_rows = CAP * device_count

    def add_expert(running, inputs):
        gate_up, down_proj, expert = inputs
        matches = expert_ids == expert
        chosen = jnp.any(matches, axis=1)
        weight_rows = lax.optimization_barrier(jnp.sum(jnp.where(matches, gate_weights, 0.0), axis=1))
        selected = jnp.argsort(jnp.where(chosen, 0, 1).astype(jnp.int32), stable=True)[:limit_rows]
        output_rows = expert_rows(normed[selected], gate_up, down_proj).astype(jnp.float32)
        scaled = (weight_rows[selected] * chosen[selected].astype(jnp.float32))[:, None] * output_rows
        return (running.at[selected].add(scaled), None)
    expert_sum, ignored = lax.scan(add_expert, jnp.zeros((REQUESTS, D), jnp.float32), (w_gate_up, w_down, jnp.arange(EXPERTS, dtype=jnp.int32)))
    layer_out = (merged_wide + expert_sum).astype(jnp.bfloat16)
    return (attended, layer_out)
```

```python
import math

import jax
import jax.numpy as jnp
from jax import lax
from jax.sharding import PartitionSpec as P

HEAD_DIMENSION = 128
KEY_VALUE_HEADS = 2
QUERY_GROUP_SIZE = 16


masked_score = -1e30
epsilon = 1e-06


def from_behind(value, axis, by):
    length = lax.axis_size(axis)
    return lax.ppermute(value, axis, [(i, (i + by) % length) for i in range(length)])


def cache_scores(source, index_table, allowed, query_head_block, scaling):
    count_of_rows = index_table.shape[0]
    collected_rows = jnp.take(source, index_table, axis=0).reshape(
        count_of_rows, -1, source.shape[-1]
    )
    key_row_width = source.shape[-1] // 2
    group_heads = query_head_block.shape[1]
    head_size = query_head_block.shape[3]
    key_entries = collected_rows[:, :, :key_row_width].reshape(
        count_of_rows, -1, group_heads, head_size
    )
    value_entries = collected_rows[:, :, key_row_width:].reshape(
        count_of_rows, -1, group_heads, head_size
    )
    scores = (
        jnp.einsum(
            "rkgd,rlkd->rkgl", query_head_block, key_entries, preferred_element_type=jnp.float32
        )
        * scaling
    )
    scores = jnp.where(allowed[:, None, None, :], scores, masked_score)
    return (scores, value_entries)


def finish_attention(score_list, value_list, query_head_block, incoming_rows, scaling):
    count_of_rows = incoming_rows.shape[0]
    key_row_width = incoming_rows.shape[-1] // 2
    group_heads = query_head_block.shape[1]
    head_size = query_head_block.shape[3]
    incoming_keys = incoming_rows[:, :key_row_width].reshape(count_of_rows, group_heads, head_size)
    incoming_values = incoming_rows[:, key_row_width:].reshape(
        count_of_rows, group_heads, head_size
    )
    fresh_score = (
        jnp.einsum(
            "rkgd,rkd->rkg", query_head_block, incoming_keys, preferred_element_type=jnp.float32
        )
        * scaling
    )
    largest = fresh_score
    for scores in score_list:
        largest = jnp.maximum(largest, jnp.max(scores, axis=-1))
    fresh_weight = jnp.exp(fresh_score - largest)
    denominator = fresh_weight
    fresh_low = lax.optimization_barrier(fresh_weight.astype(jnp.bfloat16)).astype(jnp.float32)
    summed = fresh_low[..., None] * incoming_values.astype(jnp.float32)[:, :, None, :]
    for scores, value_entries in zip(score_list, value_list):
        weights = jnp.exp(scores - largest[..., None])
        denominator = denominator + jnp.sum(weights, axis=-1)
        summed = summed + jnp.einsum(
            "rkgl,rlkd->rkgd",
            weights.astype(jnp.bfloat16),
            value_entries,
            preferred_element_type=jnp.float32,
        )
    return (summed / denominator[..., None]).reshape(count_of_rows, -1).astype(jnp.bfloat16)


def expert_block(tokens, gate_up, down_proj):
    hidden_dim = down_proj.shape[0]
    product = jnp.dot(tokens, gate_up, preferred_element_type=jnp.float32)
    hidden = (jax.nn.silu(product[:, :hidden_dim]) * product[:, hidden_dim:]).astype(jnp.bfloat16)
    return jnp.dot(hidden, down_proj, preferred_element_type=jnp.float32).astype(jnp.bfloat16)


def local(
    queries,
    new_kv,
    kv_pages,
    page_table,
    lengths,
    shed_slots,
    residual,
    norm_gain,
    expert_ids,
    gate_weights,
    w_gate_up,
    w_down,
):
    count_of_rows, model_dim = queries.shape
    pages_own, page_len, kv_width = kv_pages.shape
    table_width = page_table.shape[1]
    query_head_block = queries.reshape(
        count_of_rows, KEY_VALUE_HEADS, QUERY_GROUP_SIZE, HEAD_DIMENSION
    )
    scaling = 1.0 / math.sqrt(HEAD_DIMENSION)
    positions = jnp.arange(table_width * page_len, dtype=jnp.int32)
    allowed = positions[None, :] < lengths[:, None]
    requested = from_behind(shed_slots, "pool", 1)
    fetched = from_behind(jnp.take(kv_pages, requested, axis=0), "pool", 1)
    combined = jnp.concatenate([kv_pages, fetched], axis=0)
    scores, value_entries = cache_scores(combined, page_table, allowed, query_head_block, scaling)
    attended = finish_attention([scores], [value_entries], query_head_block, new_kv, scaling)
    merged = (residual.astype(jnp.float32) + attended.astype(jnp.float32)).astype(jnp.bfloat16)
    merged_wide = merged.astype(jnp.float32)
    normed = (
        merged_wide
        * lax.rsqrt(jnp.mean(merged_wide * merged_wide, axis=-1, keepdims=True) + epsilon)
        * norm_gain
    ).astype(jnp.bfloat16)
    axes = ("pool", "dev")
    expert = lax.axis_index(axes)
    weight_here = lax.all_gather(
        jnp.concatenate([expert_ids.astype(jnp.float32), gate_weights], axis=1),
        axes,
        axis=0,
        tiled=True,
    )
    top_count = expert_ids.shape[1]
    matches = weight_here[:, :top_count] == expert.astype(jnp.float32)
    row_weight = jnp.sum(jnp.where(matches, weight_here[:, top_count:], 0.0), axis=1)
    gathered = lax.all_gather(normed, axes, axis=0, tiled=True)
    finished = expert_block(gathered, w_gate_up[0], w_down[0])
    partial = (finished.astype(jnp.float32) * row_weight[:, None]).astype(jnp.bfloat16)
    expert_sum = lax.psum_scatter(partial, axes, scatter_dimension=0, tiled=True)
    layer_out = (merged_wide + expert_sum.astype(jnp.float32)).astype(jnp.bfloat16)
    return (attended, layer_out)


def solution(mesh):
    return jax.shard_map(
        local,
        mesh=mesh,
        in_specs=(
            P(("pool", "dev"), None),
            P(("pool", "dev"), None),
            P(("pool", "dev"), None, None),
            P(("pool", "dev"), None),
            P(("pool", "dev")),
            P(("pool", "dev")),
            P(("pool", "dev"), None),
            P(),
            P(("pool", "dev"), None),
            P(("pool", "dev"), None),
            P(("pool", "dev"), None, None),
            P(("pool", "dev"), None, None),
        ),
        out_specs=(P(("pool", "dev"), None), P(("pool", "dev"), None)),
        check_vma=False,
    )
```

```python
import math

import jax
import jax.numpy as jnp
from jax import lax
from jax.sharding import PartitionSpec as P

HEAD_DIMENSION = 128
KEY_VALUE_HEADS = 2
QUERY_GROUP_SIZE = 16


masked_score = -1e30
epsilon = 1e-06
AXES = ("pool", "dev")


def from_behind(value, axis, by):
    length = lax.axis_size(axis)
    return lax.ppermute(value, axis, [(i, (i + by) % length) for i in range(length)])


def cache_scores(source, index_table, allowed, query_head_block, scaling):
    count_of_rows = index_table.shape[0]
    collected_rows = jnp.take(source, index_table, axis=0).reshape(
        count_of_rows, -1, source.shape[-1]
    )
    key_row_width = source.shape[-1] // 2
    group_heads = query_head_block.shape[1]
    head_size = query_head_block.shape[3]
    key_entries = collected_rows[:, :, :key_row_width].reshape(
        count_of_rows, -1, group_heads, head_size
    )
    value_entries = collected_rows[:, :, key_row_width:].reshape(
        count_of_rows, -1, group_heads, head_size
    )
    scores = (
        jnp.einsum(
            "rkgd,rlkd->rkgl", query_head_block, key_entries, preferred_element_type=jnp.float32
        )
        * scaling
    )
    scores = jnp.where(allowed[:, None, None, :], scores, masked_score)
    return (scores, value_entries)


def finish_attention(score_list, value_list, query_head_block, incoming_rows, scaling):
    count_of_rows = incoming_rows.shape[0]
    key_row_width = incoming_rows.shape[-1] // 2
    group_heads = query_head_block.shape[1]
    head_size = query_head_block.shape[3]
    incoming_keys = incoming_rows[:, :key_row_width].reshape(count_of_rows, group_heads, head_size)
    incoming_values = incoming_rows[:, key_row_width:].reshape(
        count_of_rows, group_heads, head_size
    )
    fresh_score = (
        jnp.einsum(
            "rkgd,rkd->rkg", query_head_block, incoming_keys, preferred_element_type=jnp.float32
        )
        * scaling
    )
    largest = fresh_score
    for scores in score_list:
        largest = jnp.maximum(largest, jnp.max(scores, axis=-1))
    fresh_weight = jnp.exp(fresh_score - largest)
    denominator = fresh_weight
    fresh_low = lax.optimization_barrier(fresh_weight.astype(jnp.bfloat16)).astype(jnp.float32)
    summed = fresh_low[..., None] * incoming_values.astype(jnp.float32)[:, :, None, :]
    for scores, value_entries in zip(score_list, value_list):
        weights = jnp.exp(scores - largest[..., None])
        denominator = denominator + jnp.sum(weights, axis=-1)
        summed = summed + jnp.einsum(
            "rkgl,rlkd->rkgd",
            weights.astype(jnp.bfloat16),
            value_entries,
            preferred_element_type=jnp.float32,
        )
    return (summed / denominator[..., None]).reshape(count_of_rows, -1).astype(jnp.bfloat16)


def expert_block(tokens, gate_up, down_proj):
    hidden_dim = down_proj.shape[0]
    product = jnp.dot(tokens, gate_up, preferred_element_type=jnp.float32)
    hidden = (jax.nn.silu(product[:, :hidden_dim]) * product[:, hidden_dim:]).astype(jnp.bfloat16)
    return jnp.dot(hidden, down_proj, preferred_element_type=jnp.float32).astype(jnp.bfloat16)


class Layout:
    def __init__(self, pool, dev):
        self.pool, self.dev = pool, dev
        self.inner = math.gcd(dev, 4)
        self.planes = dev // self.inner
        self.members = pool * self.inner
        self.groups = [
            [self.linear(member, plane) for member in range(self.members)]
            for plane in range(self.planes)
        ]

    def linear(self, member, plane):
        return member // self.inner * self.dev + plane * self.inner + member % self.inner

    def shifted(self, value, by):
        if by == 0:
            return value
        pairs = [
            (self.linear(m, z), self.linear(m, (z + by) % self.planes))
            for z in range(self.planes)
            for m in range(self.members)
        ]
        return lax.ppermute(value, AXES, pairs)

    def swapped(self, value, mask):
        if mask == 0:
            return value
        pairs = [
            (self.linear(m, z), self.linear(m ^ mask, z))
            for z in range(self.planes)
            for m in range(self.members)
        ]
        return lax.ppermute(value, AXES, pairs)


def slot_choice(ids, experts, capacity):
    match = jnp.any(ids[:, :, None, :] == experts[None, None, :, None], axis=-1)
    rank = jnp.cumsum(match.astype(jnp.int32), axis=1) - 1
    slots = jnp.arange(capacity, dtype=jnp.int32)
    chosen = match[..., None] & (rank[..., None] == slots)
    return jnp.transpose(chosen, (2, 0, 3, 1)).astype(jnp.float32)


def spread(choice):
    members, blocks, capacity, rows = choice.shape
    own = jnp.eye(blocks, dtype=choice.dtype)
    full = choice[:, :, :, None, :] * own[None, :, None, :, None]
    return full.reshape(members * blocks * capacity, blocks * rows)


def local(
    queries,
    new_kv,
    kv_pages,
    page_table,
    lengths,
    shed_slots,
    residual,
    norm_gain,
    expert_ids,
    gate_weights,
    w_gate_up,
    w_down,
):
    count_of_rows, model_dim = queries.shape
    pages_own, page_len, kv_width = kv_pages.shape
    table_width = page_table.shape[1]
    top_count = expert_ids.shape[1]
    layout = Layout(lax.axis_size("pool"), lax.axis_size("dev"))
    inner = layout.inner
    capacity = 2 * count_of_rows * top_count // (layout.pool * layout.dev)
    routing = jnp.concatenate([expert_ids.astype(jnp.float32), gate_weights], axis=1)
    routing = jnp.stack([layout.shifted(routing, s) for s in range(layout.planes)])
    ids = routing[:, :, :top_count].astype(jnp.int32)
    gates = routing[:, :, top_count:]
    query_head_block = queries.reshape(
        count_of_rows, KEY_VALUE_HEADS, QUERY_GROUP_SIZE, HEAD_DIMENSION
    )
    scaling = 1.0 / math.sqrt(HEAD_DIMENSION)
    positions = jnp.arange(table_width * page_len, dtype=jnp.int32)
    allowed = positions[None, :] < lengths[:, None]
    requested = from_behind(shed_slots, "pool", 1)
    fetched = from_behind(jnp.take(kv_pages, requested, axis=0), "pool", 1)
    combined = jnp.concatenate([kv_pages, fetched], axis=0)
    scores, value_entries = cache_scores(combined, page_table, allowed, query_head_block, scaling)
    attended = finish_attention([scores], [value_entries], query_head_block, new_kv, scaling)
    merged = (residual.astype(jnp.float32) + attended.astype(jnp.float32)).astype(jnp.bfloat16)
    merged_wide = merged.astype(jnp.float32)
    normed = (
        merged_wide
        * lax.rsqrt(jnp.mean(merged_wide * merged_wide, axis=-1, keepdims=True) + epsilon)
        * norm_gain
    ).astype(jnp.bfloat16)
    place = lax.axis_index("pool") * inner + lax.axis_index("dev") % inner
    plane = lax.axis_index("dev") // inner
    members = jnp.arange(layout.members, dtype=jnp.int32)
    experts_absolute = layout.linear(members, plane)
    experts_relative = layout.linear(members ^ place, plane)
    send = slot_choice(ids, experts_absolute, capacity)
    back = slot_choice(ids, experts_relative, capacity)
    gate_of = jnp.sum(
        jnp.where(
            ids[:, :, None, :] == experts_relative[None, None, :, None], gates[:, :, None, :], 0.0
        ),
        axis=-1,
    )
    blocks = jnp.concatenate([layout.shifted(normed, s) for s in range(layout.planes)], axis=0)
    outgoing = jnp.dot(spread(send).astype(jnp.bfloat16), blocks, preferred_element_type=jnp.float32).astype(jnp.bfloat16)
    arrived = lax.all_to_all(
        outgoing, AXES, 0, 0, axis_index_groups=layout.groups, tiled=True
    )
    finished = expert_block(arrived, w_gate_up[0], w_down[0])
    share = finished.shape[0] // layout.members
    returned = [
        layout.swapped(lax.dynamic_slice_in_dim(finished, (place ^ m) * share, share, 0), m)
        for m in range(layout.members)
    ]
    mixing = spread(back * gate_of.transpose(2, 0, 1)[:, :, None, :])
    coarse = lax.reduce_precision(mixing, 8, 7)
    rest = mixing - coarse
    both = jnp.concatenate([coarse, rest], axis=1).astype(jnp.bfloat16)
    summed = lax.dot_general(
        both,
        jnp.concatenate(returned, axis=0),
        (((0,), (0,)), ((), ())),
        preferred_element_type=jnp.float32,
    )
    half = summed.shape[0] // 2
    summed = (summed[:half] + summed[half:]).astype(jnp.bfloat16)
    expert_sum = sum(
        layout.shifted(summed[s * count_of_rows : (s + 1) * count_of_rows], -s).astype(jnp.float32)
        for s in range(layout.planes)
    )
    layer_out = (merged_wide + expert_sum).astype(jnp.bfloat16)
    return (attended, layer_out)


def solution(mesh):
    return jax.shard_map(
        local,
        mesh=mesh,
        in_specs=(
            P(("pool", "dev"), None),
            P(("pool", "dev"), None),
            P(("pool", "dev"), None, None),
            P(("pool", "dev"), None),
            P(("pool", "dev")),
            P(("pool", "dev")),
            P(("pool", "dev"), None),
            P(),
            P(("pool", "dev"), None),
            P(("pool", "dev"), None),
            P(("pool", "dev"), None, None),
            P(("pool", "dev"), None, None),
        ),
        out_specs=(P(("pool", "dev"), None), P(("pool", "dev"), None)),
        check_vma=False,
    )
```

```python
import math

import jax
import jax.numpy as jnp
from jax import lax
from jax.experimental import pallas as pl
from jax.experimental.pallas import tpu as pltpu
from jax.sharding import PartitionSpec as P

HEAD_DIMENSION = 128
KEY_VALUE_HEADS = 2
QUERY_GROUP_SIZE = 16
HEADS = KEY_VALUE_HEADS * QUERY_GROUP_SIZE

masked_score = -1e30
epsilon = 1e-06
AXES = ("pool", "dev")
VMEM = pl.BlockSpec(memory_space=pltpu.VMEM)
MEBI = 1 << 20


class Layout:
    def __init__(self, pool, dev):
        self.pool, self.dev = pool, dev
        self.inner = math.gcd(dev, 4)
        self.planes = dev // self.inner
        self.members = pool * self.inner
        self.groups = [
            [self.linear(member, plane) for member in range(self.members)]
            for plane in range(self.planes)
        ]

    def linear(self, member, plane):
        return member // self.inner * self.dev + plane * self.inner + member % self.inner

    def shifted(self, value, by):
        if by == 0:
            return value
        pairs = [
            (self.linear(m, z), self.linear(m, (z + by) % self.planes))
            for z in range(self.planes)
            for m in range(self.members)
        ]
        return lax.ppermute(value, AXES, pairs)

    def exchanged(self, value):
        return lax.all_to_all(value, AXES, 0, 0, axis_index_groups=self.groups, tiled=True)


def from_behind(value, axis, by):
    length = lax.axis_size(axis)
    return lax.ppermute(value, axis, [(i, (i + by) % length) for i in range(length)])


def pick_pages(slots, pages):
    count = slots.shape[0]
    last = pages.shape[0] - 1

    def kernel(slots_ref, pages_ref, out_ref, sems):
        copies = []
        for i in range(count):
            page = jnp.clip(slots_ref[i], 0, last)
            copies.append(pltpu.make_async_copy(pages_ref.at[page], out_ref.at[i], sems.at[i]))
            copies[-1].start()
        for copy in copies:
            copy.wait()

    return pl.pallas_call(
        kernel,
        out_shape=jax.ShapeDtypeStruct((count,) + pages.shape[1:], pages.dtype),
        in_specs=[
            pl.BlockSpec(memory_space=pltpu.SMEM),
            pl.BlockSpec(memory_space=pl.ANY),
        ],
        out_specs=pl.BlockSpec(memory_space=pl.ANY),
        scratch_shapes=[pltpu.SemaphoreType.DMA((count,))],
        cost_estimate=pl.CostEstimate(flops=0, bytes_accessed=4 * MEBI, transcendentals=0),
        name="pick_pages",
    )(slots, pages)


def head_blocks(query):
    rows = query.shape[0]
    head = lax.broadcasted_iota(jnp.int32, (rows, HEAD_DIMENSION), 0) % HEADS
    nothing = jnp.zeros_like(query)
    low = head < QUERY_GROUP_SIZE
    return jnp.concatenate([jnp.where(low, query, nothing), jnp.where(low, nothing, query)], axis=1)


def own_head(both):
    rows = both.shape[0]
    head = lax.broadcasted_iota(jnp.int32, (rows, HEAD_DIMENSION), 0) % HEADS
    return jnp.where(
        head < QUERY_GROUP_SIZE, both[:, :HEAD_DIMENSION], both[:, HEAD_DIMENSION:]
    )


def tokens_of_pages(table, lengths, first, page_len):
    count_of_rows, width = table.shape
    page = lax.broadcasted_iota(jnp.int32, (count_of_rows, 128), 1) + first
    held = jnp.zeros((count_of_rows, 128), jnp.float32)
    for p in range(width):
        filled = jnp.clip(lengths - p * page_len, 0, page_len).astype(jnp.float32)
        held = held + jnp.where(table[:, p : p + 1] == page, filled, 0.0)
    return held


def token_bias(held, first_page, tokens, page_len):
    page = lax.broadcasted_iota(jnp.int32, (128, tokens), 0)
    token = lax.broadcasted_iota(jnp.int32, (128, tokens), 1)
    widen = (page == token // page_len + first_page).astype(jnp.bfloat16)
    limit = jnp.dot(held.astype(jnp.bfloat16), widen, preferred_element_type=jnp.float32)
    inside = (token[: held.shape[0]] % page_len).astype(jnp.float32)
    return jnp.where(inside < limit, 0.0, masked_score)


def masked_scores(blocks, keys, bias, scaling):
    scores = lax.dot_general(
        blocks, keys, (((1,), (1,)), ((), ())), preferred_element_type=jnp.float32
    )
    requests, tokens = bias.shape
    return (
        (scores * scaling).reshape(requests, HEADS, tokens) + bias[:, None, :]
    ).reshape(requests * HEADS, tokens)


def narrowed(value, join):
    result = value[:, :128]
    for start in range(128, value.shape[1], 128):
        result = join(result, value[:, start : start + 128])
    return result


def own_attention(query, new_kv, pages, table, lengths):
    page_count, page_len, kv_width = pages.shape
    rows = query.shape[0]
    requests = new_kv.shape[0]
    half = kv_width // 2
    chunk_pages = 128 * (page_count // 128) // 4
    chunk = chunk_pages * page_len
    chunks = page_count // chunk_pages
    scaling = 1.0 / math.sqrt(HEAD_DIMENSION)

    def kernel(q_ref, new_ref, pages_ref, table_ref, lengths_ref, out_ref, top_ref, sum_ref, s_ref, fresh_ref):
        blocks = head_blocks(q_ref[...])
        held = tokens_of_pages(table_ref[...], lengths_ref[...], 0, page_len)
        fresh_ref[...] = jnp.zeros_like(fresh_ref)
        fresh_ref[0:requests] = new_ref[...]
        lane = lax.broadcasted_iota(jnp.int32, (requests, 128), 1)
        own = lax.broadcasted_iota(jnp.int32, (requests, 128), 0)
        fresh_bias = jnp.where(lane == own, 0.0, masked_score)
        fresh = masked_scores(blocks, fresh_ref[:, :half], fresh_bias, scaling)
        s_ref[:, chunks * chunk :] = fresh
        top = fresh
        for c in range(chunks):
            keys = pages_ref[c * chunk_pages : (c + 1) * chunk_pages, :, :half].reshape(chunk, half)
            bias = token_bias(held, c * chunk_pages, chunk, page_len)
            scores = masked_scores(blocks, keys, bias, scaling)
            s_ref[:, c * chunk : (c + 1) * chunk] = scores
            top = jnp.maximum(top, narrowed(scores, jnp.maximum))
        top = jnp.max(top, axis=1, keepdims=True)
        weights = jnp.exp(s_ref[:, chunks * chunk :] - top)
        total = weights
        summed = jnp.dot(
            weights.astype(jnp.bfloat16), fresh_ref[:, half:], preferred_element_type=jnp.float32
        )
        for c in range(chunks):
            values = pages_ref[c * chunk_pages : (c + 1) * chunk_pages, :, half:].reshape(chunk, half)
            weights = jnp.exp(s_ref[:, c * chunk : (c + 1) * chunk] - top)
            total = total + narrowed(weights, jnp.add)
            summed = summed + jnp.dot(
                weights.astype(jnp.bfloat16), values, preferred_element_type=jnp.float32
            )
        out_ref[...] = own_head(summed)
        top_ref[...] = jnp.broadcast_to(top, top_ref.shape)
        sum_ref[...] = jnp.broadcast_to(jnp.sum(total, axis=1, keepdims=True), sum_ref.shape)

    shape = jax.ShapeDtypeStruct((rows, 128), jnp.float32)
    return pl.pallas_call(
        kernel,
        out_shape=(shape, shape, shape),
        in_specs=[VMEM] * 5,
        out_specs=(VMEM,) * 3,
        scratch_shapes=[
            pltpu.VMEM((rows, chunks * chunk + 128), jnp.float32),
            pltpu.VMEM((128, kv_width), jnp.bfloat16),
        ],
        compiler_params=pltpu.CompilerParams(vmem_limit_bytes=24 * MEBI),
        cost_estimate=pl.CostEstimate(
            flops=4 * rows * half * chunks * chunk,
            bytes_accessed=16 * MEBI,
            transcendentals=rows * chunks * chunk,
        ),
        name="own_attention",
    )(query, new_kv, pages, table, lengths)


def finish_attention(query, fetched, table, lengths, partial, residual, gain, pages_own):
    count, page_len, kv_width = fetched.shape
    half = kv_width // 2
    tokens = count * page_len
    requests, model_dim = residual.shape
    rows = query.shape[0]
    scaling = 1.0 / math.sqrt(HEAD_DIMENSION)

    def kernel(q_ref, fetched_ref, table_ref, lengths_ref, sum_ref, top_ref, total_ref, residual_ref, gain_ref, attended_ref, merged_ref, normed_ref, heads_ref):
        blocks = head_blocks(q_ref[...])
        held = tokens_of_pages(table_ref[...], lengths_ref[...], pages_own, page_len)
        bias = token_bias(held, 0, tokens, page_len)
        keys = fetched_ref[:, :, :half].reshape(tokens, half)
        values = fetched_ref[:, :, half:].reshape(tokens, half)
        scores = masked_scores(blocks, keys, bias, scaling)
        before = top_ref[...]
        shed_top = jnp.max(narrowed(scores, jnp.maximum), axis=1, keepdims=True)
        top = jnp.maximum(before, shed_top)
        kept = jnp.exp(before - top)
        weights = jnp.exp(scores - jnp.concatenate([top] * (tokens // 128), axis=1))
        added = jnp.sum(narrowed(weights, jnp.add), axis=1, keepdims=True)
        total = total_ref[...] * kept + added
        summed = own_head(
            jnp.dot(weights.astype(jnp.bfloat16), values, preferred_element_type=jnp.float32)
        )
        heads_ref[...] = (sum_ref[...] * kept + summed) / total
        square = jnp.zeros((requests, 128), jnp.float32)
        for h in range(HEADS):
            columns = slice(h * 128, (h + 1) * 128)
            attended = heads_ref[pl.ds(h, requests, stride=HEADS), :].astype(jnp.bfloat16)
            attended_ref[:, columns] = attended
            merged = (
                residual_ref[:, columns].astype(jnp.float32) + attended.astype(jnp.float32)
            ).astype(jnp.bfloat16)
            merged_ref[:, columns] = merged
            wide = merged.astype(jnp.float32)
            square = square + wide * wide
        mean = jnp.sum(square, axis=1, keepdims=True) * (1.0 / model_dim)
        inverse = lax.rsqrt(mean + epsilon)
        normed_ref[...] = (
            merged_ref[...].astype(jnp.float32) * inverse * gain_ref[...]
        ).astype(jnp.bfloat16)

    shape = jax.ShapeDtypeStruct((requests, model_dim), jnp.bfloat16)
    return pl.pallas_call(
        kernel,
        out_shape=(shape, shape, shape),
        in_specs=[VMEM] * 9,
        out_specs=(VMEM,) * 3,
        scratch_shapes=[pltpu.VMEM((rows, 128), jnp.float32)],
        compiler_params=pltpu.CompilerParams(vmem_limit_bytes=16 * MEBI),
        cost_estimate=pl.CostEstimate(
            flops=4 * rows * half * tokens, bytes_accessed=4 * MEBI, transcendentals=rows * tokens
        ),
        name="finish_attention",
    )(query, fetched, table, lengths, *partial, residual, gain)


def expert_block(tokens, gate_up, down_proj):
    hidden_dim = down_proj.shape[0]
    product = jnp.dot(tokens, gate_up, preferred_element_type=jnp.float32)
    hidden = (jax.nn.silu(product[:, :hidden_dim]) * product[:, hidden_dim:]).astype(jnp.bfloat16)
    return jnp.dot(hidden, down_proj, preferred_element_type=jnp.float32).astype(jnp.bfloat16)


def slot_choice(ids, experts, capacity):
    match = jnp.any(ids[:, :, None, :] == experts[None, None, :, None], axis=-1)
    rank = jnp.cumsum(match.astype(jnp.int32), axis=1) - 1
    slots = jnp.arange(capacity, dtype=jnp.int32)
    chosen = match[..., None] & (rank[..., None] == slots)
    return jnp.transpose(chosen, (2, 0, 3, 1)).astype(jnp.float32)


def spread(choice):
    members, blocks, capacity, rows = choice.shape
    own = jnp.eye(blocks, dtype=choice.dtype)
    full = choice[:, :, :, None, :] * own[None, :, None, :, None]
    return full.reshape(members * blocks * capacity, blocks * rows)


def local(
    queries,
    new_kv,
    kv_pages,
    page_table,
    lengths,
    shed_slots,
    residual,
    norm_gain,
    expert_ids,
    gate_weights,
    w_gate_up,
    w_down,
):
    count_of_rows, model_dim = queries.shape
    top_count = expert_ids.shape[1]
    layout = Layout(lax.axis_size("pool"), lax.axis_size("dev"))
    capacity = 2 * count_of_rows * top_count // (layout.pool * layout.dev)
    planes = layout.planes

    requested = from_behind(shed_slots, "pool", 1)
    fetched = from_behind(pick_pages(requested, kv_pages), "pool", 1)

    routing = jnp.concatenate([expert_ids.astype(jnp.float32), gate_weights], axis=1)
    routing, requested = lax.optimization_barrier((routing, requested))
    routing = jnp.stack([layout.shifted(routing, s) for s in range(planes)])
    ids = routing[:, :, :top_count].astype(jnp.int32)
    gates = routing[:, :, top_count:]
    plane = lax.axis_index("dev") // layout.inner
    experts = layout.linear(jnp.arange(layout.members, dtype=jnp.int32), plane)
    choice = slot_choice(ids, experts, capacity)
    gate_of = jnp.sum(
        jnp.where(ids[:, :, None, :] == experts[None, None, :, None], gates[:, :, None, :], 0.0),
        axis=-1,
    )
    mixing = choice * gate_of.transpose(2, 0, 1)[:, :, None, :]

    query = queries.reshape(count_of_rows * HEADS, HEAD_DIMENSION)
    lengths_column = lengths.reshape(count_of_rows, 1)
    partial = own_attention(query, new_kv, kv_pages, page_table, lengths_column)
    attended, merged, normed = finish_attention(
        query,
        fetched,
        page_table,
        lengths_column,
        partial,
        residual,
        norm_gain.reshape(1, model_dim),
        kv_pages.shape[0],
    )

    first = max(1, planes // 4)
    groups = [range(0, first), range(first, 2 * first), range(2 * first, planes)]
    blocks = [layout.shifted(normed, s) for s in range(planes)]
    arrived = []
    for group in groups:
        rows = jnp.concatenate([blocks[s] for s in group], axis=0)
        pick = spread(choice[:, group.start : group.stop]).astype(jnp.bfloat16)
        outgoing = jnp.dot(pick, rows, preferred_element_type=jnp.float32).astype(jnp.bfloat16)
        arrived.append(layout.exchanged(outgoing))
    finished = expert_block(jnp.concatenate(arrived, axis=0), w_gate_up[0], w_down[0])
    pieces, start = [], 0
    for part in arrived:
        pieces.append(finished[start : start + part.shape[0]])
        start += part.shape[0]
    sums = []
    for group, piece in list(zip(groups, pieces))[::-1]:
        returned = layout.exchanged(piece)
        mix = spread(mixing[:, group.start : group.stop])
        coarse = lax.reduce_precision(mix, 8, 7)
        both = jnp.concatenate([coarse, mix - coarse], axis=1).astype(jnp.bfloat16)
        summed = lax.dot_general(
            both, returned, (((0,), (0,)), ((), ())), preferred_element_type=jnp.float32
        )
        half = summed.shape[0] // 2
        summed = (summed[:half] + summed[half:]).astype(jnp.bfloat16)
        for i, s in enumerate(group):
            sums.append(layout.shifted(summed[i * count_of_rows : (i + 1) * count_of_rows], -s))
    expert_sum = sum(part.astype(jnp.float32) for part in sums)
    layer_out = (merged.astype(jnp.float32) + expert_sum).astype(jnp.bfloat16)
    return (attended, layer_out)


def solution(mesh):
    return jax.shard_map(
        local,
        mesh=mesh,
        in_specs=(
            P(("pool", "dev"), None),
            P(("pool", "dev"), None),
            P(("pool", "dev"), None, None),
            P(("pool", "dev"), None),
            P(("pool", "dev")),
            P(("pool", "dev")),
            P(("pool", "dev"), None),
            P(),
            P(("pool", "dev"), None),
            P(("pool", "dev"), None),
            P(("pool", "dev"), None, None),
            P(("pool", "dev"), None, None),
        ),
        out_specs=(P(("pool", "dev"), None), P(("pool", "dev"), None)),
        check_vma=False,
    )
```

```python
import math

import jax
import jax.numpy as jnp
from jax import lax
from jax.experimental import pallas as pl
from jax.experimental.pallas import tpu as pltpu
from jax.sharding import PartitionSpec as P

HEAD_DIMENSION = 128
KEY_VALUE_HEADS = 2
QUERY_GROUP_SIZE = 16
HEADS = KEY_VALUE_HEADS * QUERY_GROUP_SIZE

masked_score = -1e30
epsilon = 1e-06
AXES = ("pool", "dev")
VMEM = pl.BlockSpec(memory_space=pltpu.VMEM)
SMEM = pl.BlockSpec(memory_space=pltpu.SMEM)
MEBI = 1 << 20


class Layout:
    def __init__(self, pool, dev):
        self.pool, self.dev = pool, dev
        self.inner = math.gcd(dev, 4)
        self.planes = dev // self.inner
        self.members = pool * self.inner
        self.groups = [
            [self.linear(member, plane) for member in range(self.members)]
            for plane in range(self.planes)
        ]

    def linear(self, member, plane):
        return member // self.inner * self.dev + plane * self.inner + member % self.inner

    def shifted(self, value, by):
        if by == 0:
            return value
        pairs = [
            (self.linear(m, z), self.linear(m, z ^ by))
            for z in range(self.planes)
            for m in range(self.members)
        ]
        return lax.ppermute(value, AXES, pairs)

    def swapped(self, value, by):
        if by == 0:
            return value
        pairs = [
            (self.linear(m, z), self.linear(m ^ by, z))
            for z in range(self.planes)
            for m in range(self.members)
        ]
        return lax.ppermute(value, AXES, pairs)


def from_behind(value, axis, by):
    length = lax.axis_size(axis)
    return lax.ppermute(value, axis, [(i, (i + by) % length) for i in range(length)])


def pick_pages(slots, pages):
    count = slots.shape[0]
    last = pages.shape[0] - 1

    def kernel(slots_ref, pages_ref, out_ref):
        for i in range(count):
            out_ref[i] = pages_ref[jnp.clip(slots_ref[i], 0, last)]

    return pl.pallas_call(
        kernel,
        out_shape=jax.ShapeDtypeStruct((count,) + pages.shape[1:], pages.dtype),
        in_specs=[SMEM, VMEM],
        out_specs=VMEM,
        compiler_params=pltpu.CompilerParams(vmem_limit_bytes=8 * MEBI),
        cost_estimate=pl.CostEstimate(flops=0, bytes_accessed=2 * MEBI, transcendentals=0),
        name="pick_pages",
    )(slots, pages)


def head_blocks(query):
    rows = query.shape[0]
    head = lax.broadcasted_iota(jnp.int32, (rows, HEAD_DIMENSION), 0) % HEADS
    nothing = jnp.zeros_like(query)
    low = head < QUERY_GROUP_SIZE
    return jnp.concatenate([jnp.where(low, query, nothing), jnp.where(low, nothing, query)], axis=1)


def own_head(both):
    rows = both.shape[0]
    head = lax.broadcasted_iota(jnp.int32, (rows, HEAD_DIMENSION), 0) % HEADS
    return jnp.where(
        head < QUERY_GROUP_SIZE, both[:, :HEAD_DIMENSION], both[:, HEAD_DIMENSION:]
    )


def tokens_of_pages(table, lengths_ref, first, page_len):
    count_of_rows, width = table.shape
    page = lax.broadcasted_iota(jnp.int32, (count_of_rows, 128), 1) + first
    row = lax.broadcasted_iota(jnp.int32, (count_of_rows, 128), 0)
    lengths = jnp.zeros((count_of_rows, 128), jnp.int32)
    for r in range(count_of_rows):
        lengths = jnp.where(row == r, lengths_ref[r], lengths)
    held = jnp.zeros((count_of_rows, 128), jnp.float32)
    for p in range(width):
        filled = jnp.clip(lengths - p * page_len, 0, page_len).astype(jnp.float32)
        held = held + jnp.where(table[:, p : p + 1] == page, filled, 0.0)
    return held


def token_bias(held, first_page, tokens, page_len):
    page = lax.broadcasted_iota(jnp.int32, (128, tokens), 0)
    token = lax.broadcasted_iota(jnp.int32, (128, tokens), 1)
    widen = (page == token // page_len + first_page).astype(jnp.bfloat16)
    limit = jnp.dot(held.astype(jnp.bfloat16), widen, preferred_element_type=jnp.float32)
    inside = (token[: held.shape[0]] % page_len).astype(jnp.float32)
    return jnp.where(inside < limit, 0.0, masked_score)


def masked_scores(blocks, keys, bias, scaling):
    scores = lax.dot_general(
        blocks, keys, (((1,), (1,)), ((), ())), preferred_element_type=jnp.float32
    )
    requests, tokens = bias.shape
    return (
        (scores * scaling).reshape(requests, HEADS, tokens) + bias[:, None, :]
    ).reshape(requests * HEADS, tokens)


def narrowed(value, join):
    result = value[:, :128]
    for start in range(128, value.shape[1], 128):
        result = join(result, value[:, start : start + 128])
    return result


def own_attention(query, new_kv, pages, table, lengths):
    page_count, page_len, kv_width = pages.shape
    rows = query.shape[0]
    requests = new_kv.shape[0]
    half = kv_width // 2
    chunk_pages = 128 * (page_count // 128) // 4
    chunk = chunk_pages * page_len
    chunks = page_count // chunk_pages
    scaling = 1.0 / math.sqrt(HEAD_DIMENSION)

    def kernel(q_ref, new_ref, pages_ref, table_ref, lengths_ref, out_ref, top_ref, sum_ref, s_ref, fresh_ref):
        blocks = head_blocks(q_ref[...])
        held = tokens_of_pages(table_ref[...], lengths_ref, 0, page_len)
        fresh_ref[...] = jnp.zeros_like(fresh_ref)
        fresh_ref[0:requests] = new_ref[...]
        lane = lax.broadcasted_iota(jnp.int32, (requests, 128), 1)
        own = lax.broadcasted_iota(jnp.int32, (requests, 128), 0)
        fresh_bias = jnp.where(lane == own, 0.0, masked_score)
        fresh = masked_scores(blocks, fresh_ref[:, :half], fresh_bias, scaling)
        s_ref[:, chunks * chunk :] = fresh
        top = fresh
        for c in range(chunks):
            keys = pages_ref[c * chunk_pages : (c + 1) * chunk_pages, :, :half].reshape(chunk, half)
            bias = token_bias(held, c * chunk_pages, chunk, page_len)
            scores = masked_scores(blocks, keys, bias, scaling)
            s_ref[:, c * chunk : (c + 1) * chunk] = scores
            top = jnp.maximum(top, narrowed(scores, jnp.maximum))
        top = jnp.max(top, axis=1, keepdims=True)
        weights = jnp.exp(s_ref[:, chunks * chunk :] - top)
        total = weights
        summed = jnp.dot(
            weights.astype(jnp.bfloat16), fresh_ref[:, half:], preferred_element_type=jnp.float32
        )
        for c in range(chunks):
            values = pages_ref[c * chunk_pages : (c + 1) * chunk_pages, :, half:].reshape(chunk, half)
            weights = jnp.exp(s_ref[:, c * chunk : (c + 1) * chunk] - top)
            total = total + narrowed(weights, jnp.add)
            summed = summed + jnp.dot(
                weights.astype(jnp.bfloat16), values, preferred_element_type=jnp.float32
            )
        out_ref[...] = own_head(summed)
        top_ref[...] = jnp.broadcast_to(top, top_ref.shape)
        sum_ref[...] = jnp.broadcast_to(jnp.sum(total, axis=1, keepdims=True), sum_ref.shape)

    shape = jax.ShapeDtypeStruct((rows, 128), jnp.float32)
    return pl.pallas_call(
        kernel,
        out_shape=(shape, shape, shape),
        in_specs=[VMEM] * 4 + [SMEM],
        out_specs=(VMEM,) * 3,
        scratch_shapes=[
            pltpu.VMEM((rows, chunks * chunk + 128), jnp.float32),
            pltpu.VMEM((128, kv_width), jnp.bfloat16),
        ],
        compiler_params=pltpu.CompilerParams(vmem_limit_bytes=24 * MEBI),
        cost_estimate=pl.CostEstimate(
            flops=4 * rows * half * chunks * chunk,
            bytes_accessed=16 * MEBI,
            transcendentals=rows * chunks * chunk,
        ),
        name="own_attention",
    )(query, new_kv, pages, table, lengths)


def routing_columns(ids, gates):
    top_count = ids.shape[1]
    high = gates.astype(jnp.bfloat16)
    rest = gates - high.astype(jnp.float32)
    middle = rest.astype(jnp.bfloat16)
    low = (rest - middle.astype(jnp.float32)).astype(jnp.bfloat16)
    source = lax.broadcasted_iota(jnp.int32, (top_count, 128), 0)
    lane = lax.broadcasted_iota(jnp.int32, (top_count, 128), 1)
    columns = 0.0
    for i, part in enumerate((ids.astype(jnp.float32).astype(jnp.bfloat16), high, middle, low)):
        place = (lane == source + i * top_count).astype(jnp.bfloat16)
        columns = columns + jnp.dot(part, place, preferred_element_type=jnp.float32)
    return columns.astype(jnp.bfloat16)


def chosen_slots(routing, experts_ref, blocks, members, capacity, top_count, rows_each, gated):
    rows = routing.shape[0]
    row = lax.broadcasted_iota(jnp.int32, (rows, 128), 0)
    lane = lax.broadcasted_iota(jnp.int32, (rows, 128), 1)
    expert = jnp.full((rows, 128), -1, jnp.int32)
    for m in range(members):
        expert = jnp.where(lane // (blocks * capacity) == m, experts_ref[m], expert)
    same_block = lane // capacity % blocks == row // rows_each
    expert = jnp.where(same_block, expert, -1).astype(jnp.float32)
    match = jnp.zeros((rows, 128), jnp.float32)
    gate = jnp.zeros((rows, 128), jnp.float32)
    for k in range(top_count):
        hit = routing[:, k : k + 1] == expert
        match = jnp.where(hit, 1.0, match)
        if gated:
            parts = [routing[:, i * top_count + k : i * top_count + k + 1] for i in (1, 2, 3)]
            gate = jnp.where(hit, parts[0] + (parts[1] + parts[2]), gate)
    earlier = (
        lax.broadcasted_iota(jnp.int32, (rows, rows), 0)
        > lax.broadcasted_iota(jnp.int32, (rows, rows), 1)
    ).astype(jnp.bfloat16)
    rank = jnp.dot(earlier, match.astype(jnp.bfloat16), preferred_element_type=jnp.float32)
    wanted = (lane % capacity).astype(jnp.float32)
    return jnp.where(rank == wanted, gate if gated else match, 0.0)


def stacked(parts):
    if len(parts) == 1:
        return parts[0]
    return jnp.concatenate(parts, axis=0)


def select_rows(blocks, experts, capacity, top_count):
    count = len(blocks)
    members = experts.shape[0]
    rows_each = blocks[0].shape[0]
    model_dim = blocks[0].shape[1] - 128
    share = count * capacity

    def kernel(experts_ref, *refs):
        block_refs, out_refs = refs[:count], refs[count:]
        routing = stacked([ref[:, model_dim:].astype(jnp.float32) for ref in block_refs])
        choice = chosen_slots(
            routing, experts_ref, count, members, capacity, top_count, rows_each, False
        )
        pick = choice.T[: members * share].astype(jnp.bfloat16)
        step = model_dim // 4
        for start in range(0, model_dim, step):
            rows = stacked([ref[:, start : start + step] for ref in block_refs])
            picked = jnp.dot(pick, rows, preferred_element_type=jnp.float32).astype(jnp.bfloat16)
            for m in range(members):
                out_refs[m][:, start : start + step] = picked[m * share : (m + 1) * share]

    shape = jax.ShapeDtypeStruct((share, model_dim), jnp.bfloat16)
    return pl.pallas_call(
        kernel,
        out_shape=(shape,) * members,
        in_specs=[SMEM] + [VMEM] * count,
        out_specs=(VMEM,) * members,
        compiler_params=pltpu.CompilerParams(vmem_limit_bytes=16 * MEBI),
        cost_estimate=pl.CostEstimate(flops=0, bytes_accessed=3 * MEBI, transcendentals=0),
        name="select_rows",
    )(experts, *blocks)


def run_experts(groups, gate_up, down_proj):
    members = len(groups[0])
    shares = [group[0].shape[0] for group in groups]
    share = sum(shares)
    rows = members * share
    model_dim, double = gate_up.shape[1:]
    hidden_dim = double // 2
    width = 256
    out_width = 1024

    def kernel(*refs):
        inputs, rest = refs[: members * len(groups)], refs[members * len(groups) :]
        up_ref, down_ref = rest[0], rest[1]
        outputs = rest[2 : 2 + members * len(groups)]
        tokens_ref, hidden_ref = rest[2 + members * len(groups) :]
        for m in range(members):
            mine = [inputs[g * members + m][...].astype(jnp.float32) for g in range(len(groups))]
            tokens_ref[m * share : (m + 1) * share] = stacked(mine).astype(jnp.bfloat16)

        @pl.loop(0, hidden_dim // width)
        def _(c):
            start = pl.multiple_of(c * width, width)
            tokens = tokens_ref[...]
            gate = jnp.dot(
                tokens, up_ref[0, :, pl.ds(start, width)], preferred_element_type=jnp.float32
            )
            up = jnp.dot(
                tokens,
                up_ref[0, :, pl.ds(hidden_dim + start, width)],
                preferred_element_type=jnp.float32,
            )
            hidden_ref[:, pl.ds(start, width)] = (gate / (1.0 + jnp.exp(-gate)) * up).astype(
                jnp.bfloat16
            )

        for start in range(0, model_dim, out_width):
            columns = slice(start, start + out_width)
            result = jnp.dot(
                hidden_ref[...], down_ref[0, :, columns], preferred_element_type=jnp.float32
            )
            for m in range(members):
                offset = m * share
                for g in range(len(groups)):
                    outputs[g * members + m][:, columns] = result[
                        offset : offset + shares[g]
                    ].astype(jnp.bfloat16)
                    offset += shares[g]

    flat = [part for group in groups for part in group]
    results = pl.pallas_call(
        kernel,
        out_shape=tuple(jax.ShapeDtypeStruct(part.shape, jnp.bfloat16) for part in flat),
        in_specs=[VMEM] * (len(flat) + 2),
        out_specs=(VMEM,) * len(flat),
        scratch_shapes=[
            pltpu.VMEM((rows, model_dim), jnp.bfloat16),
            pltpu.VMEM((rows, hidden_dim), jnp.bfloat16),
        ],
        compiler_params=pltpu.CompilerParams(vmem_limit_bytes=36 * MEBI),
        cost_estimate=pl.CostEstimate(
            flops=6 * rows * model_dim * hidden_dim,
            bytes_accessed=20 * MEBI,
            transcendentals=rows * hidden_dim,
        ),
        name="run_experts",
    )(*flat, gate_up, down_proj)
    return [results[g * members : (g + 1) * members] for g in range(len(groups))]


def combine_rows(returned, blocks, experts, capacity, top_count, merged=None, others=()):
    count = len(blocks)
    members = experts.shape[0]
    rows_each = blocks[0].shape[0]
    model_dim = blocks[0].shape[1] - 128
    share = count * capacity
    rows = count * rows_each
    final = merged is not None

    def kernel(experts_ref, *refs):
        block_refs, refs = refs[:count], refs[count:]
        part_refs, refs = refs[:members], refs[members:]
        extra_refs, out_refs = refs[: len(extra)], refs[len(extra) :]
        routing = stacked([ref[:, model_dim:].astype(jnp.float32) for ref in block_refs])
        mixing = chosen_slots(
            routing, experts_ref, count, members, capacity, top_count, rows_each, True
        )
        coarse = mixing.astype(jnp.bfloat16)
        fine = (mixing - coarse.astype(jnp.float32)).astype(jnp.bfloat16)
        both = jnp.concatenate([coarse, fine], axis=0)[:, : members * share]
        step = model_dim // 4
        for start in range(0, model_dim, step):
            columns = slice(start, start + step)
            parts = jnp.concatenate(
                [ref[:, columns].astype(jnp.float32) for ref in part_refs], axis=0
            ).astype(jnp.bfloat16)
            summed = jnp.dot(both, parts, preferred_element_type=jnp.float32)
            summed = summed[:rows] + summed[rows:]
            for ref in extra_refs:
                summed = summed + ref[:, columns].astype(jnp.float32)
            for i in range(count):
                out_refs[i][:, columns] = summed[i * rows_each : (i + 1) * rows_each].astype(
                    jnp.bfloat16
                )

    extra = [merged, *others] if final else []
    shape = jax.ShapeDtypeStruct((rows_each, model_dim), jnp.bfloat16)
    return pl.pallas_call(
        kernel,
        out_shape=(shape,) * count,
        in_specs=[SMEM] + [VMEM] * (count + members + len(extra)),
        out_specs=(VMEM,) * count,
        compiler_params=pltpu.CompilerParams(vmem_limit_bytes=16 * MEBI),
        cost_estimate=pl.CostEstimate(flops=0, bytes_accessed=3 * MEBI, transcendentals=0),
        name="combine_rows",
    )(experts, *blocks, *returned, *extra)


def finish_attention(
    query, fetched, table, lengths, partial, residual, gain, ids, gates, pages_own
):
    count, page_len, kv_width = fetched.shape
    half = kv_width // 2
    tokens = count * page_len
    requests, model_dim = residual.shape
    rows = query.shape[0]
    scaling = 1.0 / math.sqrt(HEAD_DIMENSION)

    def kernel(q_ref, fetched_ref, table_ref, lengths_ref, sum_ref, top_ref, total_ref, residual_ref, gain_ref, ids_ref, gates_ref, attended_ref, merged_ref, normed_ref, heads_ref):
        blocks = head_blocks(q_ref[...])
        held = tokens_of_pages(table_ref[...], lengths_ref, pages_own, page_len)
        bias = token_bias(held, 0, tokens, page_len)
        keys = fetched_ref[:, :, :half].reshape(tokens, half)
        values = fetched_ref[:, :, half:].reshape(tokens, half)
        scores = masked_scores(blocks, keys, bias, scaling)
        before = top_ref[...]
        shed_top = jnp.max(narrowed(scores, jnp.maximum), axis=1, keepdims=True)
        top = jnp.maximum(before, shed_top)
        kept = jnp.exp(before - top)
        weights = jnp.exp(scores - jnp.concatenate([top] * (tokens // 128), axis=1))
        added = jnp.sum(narrowed(weights, jnp.add), axis=1, keepdims=True)
        total = total_ref[...] * kept + added
        summed = own_head(
            jnp.dot(weights.astype(jnp.bfloat16), values, preferred_element_type=jnp.float32)
        )
        heads_ref[...] = (sum_ref[...] * kept + summed) / total
        square = jnp.zeros((requests, 128), jnp.float32)
        for h in range(HEADS):
            columns = slice(h * 128, (h + 1) * 128)
            attended = heads_ref[pl.ds(h, requests, stride=HEADS), :].astype(jnp.bfloat16)
            attended_ref[:, columns] = attended
            merged = (
                residual_ref[:, columns].astype(jnp.float32) + attended.astype(jnp.float32)
            ).astype(jnp.bfloat16)
            merged_ref[:, columns] = merged
            wide = merged.astype(jnp.float32)
            square = square + wide * wide
        mean = jnp.sum(square, axis=1, keepdims=True) * (1.0 / model_dim)
        inverse = lax.rsqrt(mean + epsilon)
        normed_ref[:, model_dim:] = routing_columns(ids_ref[...], gates_ref[...])
        normed_ref[:, :model_dim] = (
            merged_ref[...].astype(jnp.float32) * inverse * gain_ref[...]
        ).astype(jnp.bfloat16)

    shape = jax.ShapeDtypeStruct((requests, model_dim), jnp.bfloat16)
    return pl.pallas_call(
        kernel,
        out_shape=(shape, shape, jax.ShapeDtypeStruct((requests, model_dim + 128), jnp.bfloat16)),
        in_specs=[VMEM] * 3 + [SMEM] + [VMEM] * 7,
        out_specs=(VMEM,) * 3,
        scratch_shapes=[pltpu.VMEM((rows, 128), jnp.float32)],
        compiler_params=pltpu.CompilerParams(vmem_limit_bytes=16 * MEBI),
        cost_estimate=pl.CostEstimate(
            flops=4 * rows * half * tokens, bytes_accessed=4 * MEBI, transcendentals=rows * tokens
        ),
        name="finish_attention",
    )(query, fetched, table, lengths, *partial, residual, gain, ids, gates)


def local(
    queries,
    new_kv,
    kv_pages,
    page_table,
    lengths,
    shed_slots,
    residual,
    norm_gain,
    expert_ids,
    gate_weights,
    w_gate_up,
    w_down,
):
    count_of_rows, model_dim = queries.shape
    top_count = expert_ids.shape[1]
    layout = Layout(lax.axis_size("pool"), lax.axis_size("dev"))
    capacity = 2 * count_of_rows * top_count // (layout.pool * layout.dev)
    planes = layout.planes

    requested = from_behind(shed_slots, "pool", 1)
    picked = pick_pages(requested, kv_pages)
    fetched = from_behind(picked, "pool", 1)
    queries, expert_ids, picked = lax.optimization_barrier((queries, expert_ids, picked))

    inner = layout.inner
    place = lax.axis_index("pool") * inner + lax.axis_index("dev") % inner
    plane = lax.axis_index("dev") // inner
    experts = layout.linear(jnp.arange(layout.members, dtype=jnp.int32) ^ place, plane)

    query = queries.reshape(count_of_rows * HEADS, HEAD_DIMENSION)
    partial = own_attention(query, new_kv, kv_pages, page_table, lengths)
    attended, merged, normed = finish_attention(
        query,
        fetched,
        page_table,
        lengths,
        partial,
        residual,
        norm_gain.reshape(1, model_dim),
        expert_ids,
        gate_weights,
        kv_pages.shape[0],
    )

    first = max(1, planes // 4)
    groups = [range(0, first), range(first, 2 * first), range(2 * first, planes)]
    masks = range(layout.members)
    blocks = [layout.shifted(normed, s) for s in range(planes)]
    arrived = []
    for group in groups:
        outgoing = select_rows([blocks[s] for s in group], experts, capacity, top_count)
        arrived.append([layout.swapped(outgoing[m], m) for m in masks])
    near = run_experts(arrived[:2], w_gate_up, w_down)
    far = run_experts(arrived[2:], w_gate_up, w_down)
    others = []
    for group, finished in ((groups[2], far[0]), (groups[1], near[1])):
        returned = [layout.swapped(finished[m], m) for m in masks]
        sums = combine_rows(returned, [blocks[s] for s in group], experts, capacity, top_count)
        others += [layout.shifted(part, s) for part, s in zip(sums, group)]
    returned = [layout.swapped(near[0][m], m) for m in masks]
    mine = [blocks[s] for s in groups[0]]
    if len(mine) == 1:
        layer_out = combine_rows(returned, mine, experts, capacity, top_count, merged, others)[0]
    else:
        sums = combine_rows(returned, mine, experts, capacity, top_count)
        others += [layout.shifted(part, s) for part, s in zip(sums, groups[0])]
        total = merged.astype(jnp.float32) + sum(part.astype(jnp.float32) for part in others)
        layer_out = total.astype(jnp.bfloat16)
    return (attended, layer_out)


def solution(mesh):
    return jax.shard_map(
        local,
        mesh=mesh,
        in_specs=(
            P(("pool", "dev"), None),
            P(("pool", "dev"), None),
            P(("pool", "dev"), None, None),
            P(("pool", "dev"), None),
            P(("pool", "dev")),
            P(("pool", "dev")),
            P(("pool", "dev"), None),
            P(),
            P(("pool", "dev"), None),
            P(("pool", "dev"), None),
            P(("pool", "dev"), None, None),
            P(("pool", "dev"), None, None),
        ),
        out_specs=(P(("pool", "dev"), None), P(("pool", "dev"), None)),
        check_vma=False,
    )
```

```python
import math

import jax
import jax.numpy as jnp
from jax import lax
from jax.experimental import pallas as pl
from jax.experimental.pallas import tpu as pltpu
from jax.sharding import PartitionSpec as P

HEAD_DIMENSION = 128
KEY_VALUE_HEADS = 2
QUERY_GROUP_SIZE = 16
HEADS = KEY_VALUE_HEADS * QUERY_GROUP_SIZE

masked_score = -1e30
epsilon = 1e-06
AXES = ("pool", "dev")
VMEM = pl.BlockSpec(memory_space=pltpu.VMEM)
SMEM = pl.BlockSpec(memory_space=pltpu.SMEM)
HBM = pl.BlockSpec(memory_space=pltpu.HBM)
MEBI = 1 << 20


def in_hbm(value):
    return pltpu.with_memory_space_constraint(value, pltpu.HBM)


class Layout:
    def __init__(self, pool, dev):
        self.pool, self.dev = pool, dev
        self.inner = math.gcd(dev, 4)
        self.planes = dev // self.inner
        self.members = pool * self.inner
        self.groups = [
            [self.linear(member, plane) for member in range(self.members)]
            for plane in range(self.planes)
        ]

    def linear(self, member, plane):
        return member // self.inner * self.dev + plane * self.inner + member % self.inner

    def shifted(self, value, by):
        if by == 0:
            return value
        pairs = [
            (self.linear(m, z), self.linear(m, z ^ by))
            for z in range(self.planes)
            for m in range(self.members)
        ]
        return lax.ppermute(value, AXES, pairs)

    def swapped(self, value, by):
        if by == 0:
            return value
        pairs = [
            (self.linear(m, z), self.linear(m ^ by, z))
            for z in range(self.planes)
            for m in range(self.members)
        ]
        return lax.ppermute(value, AXES, pairs)


def from_behind(value, axis, by):
    length = lax.axis_size(axis)
    return lax.ppermute(value, axis, [(i, (i + by) % length) for i in range(length)])


def pick_pages(slots, pages):
    count = slots.shape[0]
    last = pages.shape[0] - 1

    def kernel(slots_ref, pages_ref, out_ref, sems):
        copies = []
        for i in range(count):
            page = jnp.clip(slots_ref[i], 0, last)
            copies.append(pltpu.make_async_copy(pages_ref.at[page], out_ref.at[i], sems.at[i]))
            copies[-1].start()
        for copy in copies:
            copy.wait()

    return pl.pallas_call(
        kernel,
        out_shape=jax.ShapeDtypeStruct((count,) + pages.shape[1:], pages.dtype),
        in_specs=[SMEM, HBM],
        out_specs=VMEM,
        scratch_shapes=[pltpu.SemaphoreType.DMA((count,))],
        compiler_params=pltpu.CompilerParams(vmem_limit_bytes=4 * MEBI),
        cost_estimate=pl.CostEstimate(flops=0, bytes_accessed=MEBI, transcendentals=0),
        name="pick_pages",
    )(slots, in_hbm(pages))


def head_blocks(query):
    rows = query.shape[0]
    head = lax.broadcasted_iota(jnp.int32, (rows, HEAD_DIMENSION), 0) % HEADS
    nothing = jnp.zeros_like(query)
    low = head < QUERY_GROUP_SIZE
    return jnp.concatenate([jnp.where(low, query, nothing), jnp.where(low, nothing, query)], axis=1)


def own_head(both):
    rows = both.shape[0]
    head = lax.broadcasted_iota(jnp.int32, (rows, HEAD_DIMENSION), 0) % HEADS
    return jnp.where(
        head < QUERY_GROUP_SIZE, both[:, :HEAD_DIMENSION], both[:, HEAD_DIMENSION:]
    )


def tokens_of_pages(table, lengths_ref, first, page_len):
    count_of_rows, width = table.shape
    page = lax.broadcasted_iota(jnp.int32, (count_of_rows, 128), 1) + first
    row = lax.broadcasted_iota(jnp.int32, (count_of_rows, 128), 0)
    lengths = jnp.zeros((count_of_rows, 128), jnp.int32)
    for r in range(count_of_rows):
        lengths = jnp.where(row == r, lengths_ref[r], lengths)
    held = jnp.zeros((count_of_rows, 128), jnp.float32)
    for p in range(width):
        filled = jnp.clip(lengths - p * page_len, 0, page_len).astype(jnp.float32)
        held = held + jnp.where(table[:, p : p + 1] == page, filled, 0.0)
    return held


def token_bias(held, first_page, tokens, page_len):
    page = lax.broadcasted_iota(jnp.int32, (128, tokens), 0)
    token = lax.broadcasted_iota(jnp.int32, (128, tokens), 1)
    widen = (page == token // page_len + first_page).astype(jnp.bfloat16)
    limit = jnp.dot(held.astype(jnp.bfloat16), widen, preferred_element_type=jnp.float32)
    inside = (token[: held.shape[0]] % page_len).astype(jnp.float32)
    return jnp.where(inside < limit, 0.0, masked_score)


def masked_scores(blocks, keys, bias, scaling):
    scores = lax.dot_general(
        blocks, keys, (((1,), (1,)), ((), ())), preferred_element_type=jnp.float32
    )
    requests, tokens = bias.shape
    return (
        (scores * scaling).reshape(requests, HEADS, tokens) + bias[:, None, :]
    ).reshape(requests * HEADS, tokens)


def narrowed(value, join):
    result = value[:, :128]
    for start in range(128, value.shape[1], 128):
        result = join(result, value[:, start : start + 128])
    return result


def own_attention(queries, new_kv, pages, table, lengths):
    page_count, page_len, kv_width = pages.shape
    requests = new_kv.shape[0]
    rows = requests * HEADS
    half = kv_width // 2
    chunk_pages = 128 * (page_count // 128) // 4
    chunk = chunk_pages * page_len
    chunks = page_count // chunk_pages
    scaling = 1.0 / math.sqrt(HEAD_DIMENSION)

    def kernel(
        queries_hbm,
        new_hbm,
        pages_hbm,
        table_hbm,
        lengths_hbm,
        out_ref,
        top_ref,
        sum_ref,
        query_ref,
        s_ref,
        fresh_ref,
        heads_ref,
        flat_ref,
        pages_ref,
        table_ref,
        lengths_ref,
        sems,
    ):
        page_copies = [
            pltpu.make_async_copy(
                pages_hbm.at[pl.ds(c * chunk_pages, chunk_pages)],
                pages_ref.at[pl.ds(c * chunk_pages, chunk_pages)],
                sems.at[4 + c],
            )
            for c in range(chunks)
        ]
        copies = [
            pltpu.make_async_copy(queries_hbm, flat_ref, sems.at[0]),
            pltpu.make_async_copy(table_hbm, table_ref, sems.at[1]),
            pltpu.make_async_copy(lengths_hbm, lengths_ref, sems.at[2]),
            pltpu.make_async_copy(new_hbm, fresh_ref.at[pl.ds(0, requests)], sems.at[3]),
        ]
        fresh_ref[requests:] = jnp.zeros_like(fresh_ref[requests:])
        for copy in copies + page_copies:
            copy.start()
        for copy in copies:
            copy.wait()
        for h in range(HEADS):
            heads_ref[pl.ds(h, requests, stride=HEADS), :] = flat_ref[
                :, h * 128 : (h + 1) * 128
            ].astype(jnp.float32)
        query = heads_ref[...].astype(jnp.bfloat16)
        query_ref[...] = query
        blocks = head_blocks(query)
        held = tokens_of_pages(table_ref[...], lengths_ref, 0, page_len)
        lane = lax.broadcasted_iota(jnp.int32, (requests, 128), 1)
        own = lax.broadcasted_iota(jnp.int32, (requests, 128), 0)
        fresh_bias = jnp.where(lane == own, 0.0, masked_score)
        fresh = masked_scores(blocks, fresh_ref[:, :half], fresh_bias, scaling)
        s_ref[:, chunks * chunk :] = fresh
        top = fresh
        for c in range(chunks):
            page_copies[c].wait()
            keys = pages_ref[c * chunk_pages : (c + 1) * chunk_pages, :, :half].reshape(chunk, half)
            bias = token_bias(held, c * chunk_pages, chunk, page_len)
            scores = masked_scores(blocks, keys, bias, scaling)
            s_ref[:, c * chunk : (c + 1) * chunk] = scores
            top = jnp.maximum(top, narrowed(scores, jnp.maximum))
        top = jnp.max(top, axis=1, keepdims=True)
        weights = jnp.exp(s_ref[:, chunks * chunk :] - top)
        total = weights
        summed = jnp.dot(
            weights.astype(jnp.bfloat16), fresh_ref[:, half:], preferred_element_type=jnp.float32
        )
        for c in range(chunks):
            values = pages_ref[c * chunk_pages : (c + 1) * chunk_pages, :, half:].reshape(chunk, half)
            weights = jnp.exp(s_ref[:, c * chunk : (c + 1) * chunk] - top)
            total = total + narrowed(weights, jnp.add)
            summed = summed + jnp.dot(
                weights.astype(jnp.bfloat16), values, preferred_element_type=jnp.float32
            )
        out_ref[...] = own_head(summed)
        top_ref[...] = jnp.broadcast_to(top, top_ref.shape)
        sum_ref[...] = jnp.broadcast_to(jnp.sum(total, axis=1, keepdims=True), sum_ref.shape)

    shape = jax.ShapeDtypeStruct((rows, 128), jnp.float32)
    return pl.pallas_call(
        kernel,
        out_shape=(shape, shape, shape, jax.ShapeDtypeStruct((rows, 128), jnp.bfloat16)),
        in_specs=[HBM] * 5,
        out_specs=(VMEM,) * 4,
        scratch_shapes=[
            pltpu.VMEM((rows, chunks * chunk + 128), jnp.float32),
            pltpu.VMEM((128, kv_width), jnp.bfloat16),
            pltpu.VMEM((rows, 128), jnp.float32),
            pltpu.VMEM(queries.shape, jnp.bfloat16),
            pltpu.VMEM(pages.shape, jnp.bfloat16),
            pltpu.VMEM(table.shape, jnp.int32),
            pltpu.SMEM(lengths.shape, jnp.int32),
            pltpu.SemaphoreType.DMA((4 + chunks,)),
        ],
        compiler_params=pltpu.CompilerParams(vmem_limit_bytes=24 * MEBI),
        cost_estimate=pl.CostEstimate(
            flops=4 * rows * half * chunks * chunk,
            bytes_accessed=16 * MEBI,
            transcendentals=rows * chunks * chunk,
        ),
        name="own_attention",
    )(*[in_hbm(value) for value in (queries, new_kv, pages, table, lengths)])


def routing_columns(ids, gates):
    top_count = ids.shape[0]
    high = gates.astype(jnp.bfloat16)
    rest = gates - high.astype(jnp.float32)
    middle = rest.astype(jnp.bfloat16)
    low = (rest - middle.astype(jnp.float32)).astype(jnp.bfloat16)
    source = lax.broadcasted_iota(jnp.int32, (top_count, 128), 0)
    lane = lax.broadcasted_iota(jnp.int32, (top_count, 128), 1)
    columns = 0.0
    for i, part in enumerate((ids.astype(jnp.float32).astype(jnp.bfloat16), high, middle, low)):
        place = (lane == source + i * top_count).astype(jnp.bfloat16)
        columns = columns + lax.dot_general(
            part, place, (((0,), (0,)), ((), ())), preferred_element_type=jnp.float32
        )
    return columns.astype(jnp.bfloat16)


def stacked(parts):
    if len(parts) == 1:
        return parts[0]
    return jnp.concatenate(parts, axis=0)


def run_experts(groups, others, gate_up, down_proj, expert, top_count, slots):
    model_dim, double = gate_up.shape[1:]
    hidden_dim = double // 2
    chips = len(groups[0])
    flat = [part for group in groups for chip in group for part in chip]
    shares = [sum(part.shape[0] for part in group[0]) for group in groups]
    rows = sum(part.shape[0] for part in flat) + sum(other.shape[0] for other in others)
    width = 256
    up_steps = hidden_dim // width
    out_width = 1024 if rows <= 512 else 512
    out_steps = model_dim // out_width
    strip = 256

    def kernel(expert_ref, *refs):
        own_refs, refs = refs[: len(flat)], refs[len(flat) :]
        other_refs, refs = refs[: len(others)], refs[len(others) :]
        up_hbm, down_hbm, refs = refs[0], refs[1], refs[2:]
        out_refs, refs = refs[: chips * len(groups)], refs[chips * len(groups) :]
        over_refs, refs = refs[: len(groups)], refs[len(groups) :]
        up_ref, down_ref, tokens_ref, hidden_ref, sems = refs
        up_copies, down_copies = [], []
        for c in range(up_steps):
            pair = []
            for half in range(2):
                columns = pl.ds(half * hidden_dim + c * width, width)
                pair.append(
                    pltpu.make_async_copy(
                        up_hbm.at[0, :, columns], up_ref.at[:, columns], sems.at[2 * c + half]
                    )
                )
                pair[-1].start()
            up_copies.append(pair)
        for c in range(out_steps):
            columns = pl.ds(c * out_width, out_width)
            down_copies.append(
                pltpu.make_async_copy(
                    down_hbm.at[0, :, columns], down_ref.at[:, columns], sems.at[2 * up_steps + c]
                )
            )
            down_copies[-1].start()

        token_refs = list(own_refs) + list(other_refs)
        routing = stacked([ref[:, model_dim:] for ref in token_refs]).astype(jnp.float32)
        wanted = expert_ref[0].astype(jnp.float32)
        match = jnp.zeros((rows, 1), jnp.float32)
        gates = [jnp.zeros((rows, 1), jnp.float32)] * 3
        for k in range(top_count):
            hit = routing[:, k : k + 1] == wanted
            match = jnp.where(hit, 1.0, match)
            gates = [
                jnp.where(hit, routing[:, i * top_count + k : i * top_count + k + 1], gate)
                for i, gate in enumerate(gates, 1)
            ]
        lane = lax.broadcasted_iota(jnp.int32, (rows, slots), 1)
        match = jnp.broadcast_to(match, (rows, slots))
        earlier = (
            lax.broadcasted_iota(jnp.int32, (strip, strip), 0)
            > lax.broadcasted_iota(jnp.int32, (strip, strip), 1)
        ).astype(jnp.bfloat16)
        ranks, before = [], jnp.zeros((1, slots), jnp.float32)
        for start in range(0, rows, strip):
            piece = match[start : start + strip]
            ranks.append(
                before
                + jnp.dot(earlier, piece.astype(jnp.bfloat16), preferred_element_type=jnp.float32)
            )
            before = before + jnp.sum(piece, axis=0, keepdims=True)
        rank = stacked(ranks)
        choice = jnp.where(rank == lane.astype(jnp.float32), match, 0.0)
        pick = choice.T.astype(jnp.bfloat16)
        place = choice.astype(jnp.bfloat16)
        gate_columns = jnp.where(
            lane == 0, gates[0], jnp.where(lane == 1, gates[1], jnp.where(lane == 2, gates[2], 0.0))
        ).astype(jnp.bfloat16)
        gate = jnp.sum(
            jnp.dot(pick, gate_columns, preferred_element_type=jnp.float32), axis=1, keepdims=True
        )
        for start in range(0, model_dim, out_width):
            columns = slice(start, start + out_width)
            tokens = stacked([ref[:, columns] for ref in token_refs])
            tokens_ref[:, columns] = jnp.dot(
                pick, tokens, preferred_element_type=jnp.float32
            ).astype(jnp.bfloat16)

        for c in range(up_steps):
            for copy in up_copies[c]:
                copy.wait()
            start = c * width
            tokens = tokens_ref[...]
            gated = jnp.dot(
                tokens, up_ref[:, start : start + width], preferred_element_type=jnp.float32
            )
            up = jnp.dot(
                tokens,
                up_ref[:, hidden_dim + start : hidden_dim + start + width],
                preferred_element_type=jnp.float32,
            )
            hidden_ref[:, start : start + width] = (gated / (1.0 + jnp.exp(-gated)) * up).astype(
                jnp.bfloat16
            )

        for c in range(out_steps):
            down_copies[c].wait()
            columns = slice(c * out_width, (c + 1) * out_width)
            result = jnp.dot(
                hidden_ref[...], down_ref[:, columns], preferred_element_type=jnp.float32
            )
            result = (result * gate).astype(jnp.bfloat16)
            sums = jnp.dot(place, result, preferred_element_type=jnp.float32).astype(jnp.bfloat16)
            offset = 0
            for i, ref in enumerate([*out_refs, *over_refs]):
                cut = ref.shape[0]
                ref[:, columns] = sums[offset : offset + cut]
                offset += cut

    shapes = [(share, model_dim) for share in shares for _ in range(chips)]
    shapes += [(other.shape[0], model_dim) for other in others]
    results = pl.pallas_call(
        kernel,
        out_shape=tuple(jax.ShapeDtypeStruct(shape, jnp.bfloat16) for shape in shapes),
        in_specs=[SMEM] + [VMEM] * (len(flat) + len(others)) + [HBM] * 2,
        out_specs=(VMEM,) * len(shapes),
        scratch_shapes=[
            pltpu.VMEM((model_dim, double), jnp.bfloat16),
            pltpu.VMEM((hidden_dim, model_dim), jnp.bfloat16),
            pltpu.VMEM((slots, model_dim), jnp.bfloat16),
            pltpu.VMEM((slots, hidden_dim), jnp.bfloat16),
            pltpu.SemaphoreType.DMA((2 * up_steps + out_steps,)),
        ],
        compiler_params=pltpu.CompilerParams(vmem_limit_bytes=38 * MEBI),
        cost_estimate=pl.CostEstimate(
            flops=6 * slots * model_dim * hidden_dim,
            bytes_accessed=20 * MEBI,
            transcendentals=slots * hidden_dim,
        ),
        name="run_experts",
    )(expert, *flat, *others, in_hbm(gate_up), in_hbm(down_proj))
    mine = [results[g * chips : (g + 1) * chips] for g in range(len(groups))]
    return mine, results[chips * len(groups) :]


def add_up(parts, cuts, name):
    rows = sum(cuts)
    model_dim = parts[0][0].shape[1]
    counts = [len(part) for part in parts]
    flat = [piece for part in parts for piece in part]

    def kernel(*refs):
        in_refs, out_refs = refs[: len(flat)], refs[len(flat) :]
        step = 1024
        for start in range(0, model_dim, step):
            columns = slice(start, start + step)
            offset = 0
            for i, (out_ref, cut) in enumerate(zip(out_refs, cuts)):
                total = 0.0
                first = 0
                for count in counts:
                    pieces = in_refs[first : first + count]
                    first += count
                    if count > 1:
                        piece = pieces[i][:, columns]
                    else:
                        piece = pieces[0][offset : offset + cut, columns]
                    total = total + piece.astype(jnp.float32)
                out_ref[:, columns] = total.astype(jnp.bfloat16)
                offset += cut

    return pl.pallas_call(
        kernel,
        out_shape=tuple(jax.ShapeDtypeStruct((cut, model_dim), jnp.bfloat16) for cut in cuts),
        in_specs=[VMEM] * len(flat),
        out_specs=(VMEM,) * len(cuts),
        compiler_params=pltpu.CompilerParams(vmem_limit_bytes=12 * MEBI),
        cost_estimate=pl.CostEstimate(
            flops=rows * model_dim, bytes_accessed=2 * rows * model_dim, transcendentals=0
        ),
        name=name,
    )(*flat)


def finish_attention(
    query, fetched, table, lengths, partial, residual, gain, ids, gates, pages_own
):
    count, page_len, kv_width = fetched.shape
    half = kv_width // 2
    tokens = count * page_len
    requests, model_dim = residual.shape
    rows = query.shape[0]
    scaling = 1.0 / math.sqrt(HEAD_DIMENSION)

    def kernel(q_ref, fetched_ref, table_ref, lengths_ref, sum_ref, top_ref, total_ref, residual_ref, gain_ref, ids_ref, gates_ref, attended_ref, merged_ref, normed_ref, heads_ref):
        blocks = head_blocks(q_ref[...])
        held = tokens_of_pages(table_ref[...], lengths_ref, pages_own, page_len)
        bias = token_bias(held, 0, tokens, page_len)
        keys = fetched_ref[:, :, :half].reshape(tokens, half)
        values = fetched_ref[:, :, half:].reshape(tokens, half)
        scores = masked_scores(blocks, keys, bias, scaling)
        before = top_ref[...]
        shed_top = jnp.max(narrowed(scores, jnp.maximum), axis=1, keepdims=True)
        top = jnp.maximum(before, shed_top)
        kept = jnp.exp(before - top)
        weights = jnp.exp(scores - jnp.concatenate([top] * (tokens // 128), axis=1))
        added = jnp.sum(narrowed(weights, jnp.add), axis=1, keepdims=True)
        total = total_ref[...] * kept + added
        summed = own_head(
            jnp.dot(weights.astype(jnp.bfloat16), values, preferred_element_type=jnp.float32)
        )
        heads_ref[...] = (sum_ref[...] * kept + summed) / total
        square = jnp.zeros((requests, 128), jnp.float32)
        for h in range(HEADS):
            columns = slice(h * 128, (h + 1) * 128)
            attended = heads_ref[pl.ds(h, requests, stride=HEADS), :].astype(jnp.bfloat16)
            attended_ref[:, columns] = attended
            merged = (
                residual_ref[:, columns].astype(jnp.float32) + attended.astype(jnp.float32)
            ).astype(jnp.bfloat16)
            merged_ref[:, columns] = merged
            wide = merged.astype(jnp.float32)
            square = square + wide * wide
        mean = jnp.sum(square, axis=1, keepdims=True) * (1.0 / model_dim)
        inverse = lax.rsqrt(mean + epsilon)
        normed_ref[:, model_dim:] = routing_columns(ids_ref[...], gates_ref[...])
        normed_ref[:, :model_dim] = (
            merged_ref[...].astype(jnp.float32) * inverse * gain_ref[...]
        ).astype(jnp.bfloat16)

    shape = jax.ShapeDtypeStruct((requests, model_dim), jnp.bfloat16)
    return pl.pallas_call(
        kernel,
        out_shape=(shape, shape, jax.ShapeDtypeStruct((requests, model_dim + 128), jnp.bfloat16)),
        in_specs=[VMEM] * 3 + [SMEM] + [VMEM] * 7,
        out_specs=(VMEM,) * 3,
        scratch_shapes=[pltpu.VMEM((rows, 128), jnp.float32)],
        compiler_params=pltpu.CompilerParams(vmem_limit_bytes=16 * MEBI),
        cost_estimate=pl.CostEstimate(
            flops=4 * rows * half * tokens, bytes_accessed=4 * MEBI, transcendentals=rows * tokens
        ),
        name="finish_attention",
    )(query, fetched, table, lengths, *partial, residual, gain, ids, gates)


def local(
    queries,
    new_kv,
    kv_pages,
    page_table,
    lengths,
    shed_slots,
    residual,
    norm_gain,
    expert_ids,
    gate_weights,
    w_gate_up,
    w_down,
):
    count_of_rows, model_dim = queries.shape
    top_count = expert_ids.shape[1]
    layout = Layout(lax.axis_size("pool"), lax.axis_size("dev"))
    capacity = 2 * count_of_rows * top_count // (layout.pool * layout.dev)
    planes = layout.planes

    requested = from_behind(shed_slots, "pool", 1)
    picked = pick_pages(requested, kv_pages)
    fetched = from_behind(picked, "pool", 1)
    queries, expert_ids, picked = lax.optimization_barrier((queries, expert_ids, picked))

    expert = (lax.axis_index("pool") * layout.dev + lax.axis_index("dev")).reshape(1)
    *partial, query = own_attention(queries, new_kv, kv_pages, page_table, lengths)
    attended, merged, normed = finish_attention(
        query,
        fetched,
        page_table,
        lengths,
        partial,
        residual,
        norm_gain.reshape(1, model_dim),
        expert_ids.T,
        gate_weights.T,
        kv_pages.shape[0],
    )

    first = max(1, planes // 4)
    groups = [range(0, first), range(first, 2 * first), range(2 * first, planes)]
    chips = range(0, layout.members, 2)
    blocks = [layout.shifted(normed, s) for s in range(planes)]
    arrived = []
    for group in groups:
        rows = stacked([blocks[s] for s in group])
        arrived.append([layout.swapped(rows, chip) for chip in chips])
    rows = [
        [[arrived[0][c], arrived[1][c]] for c in range(len(chips))],
        [[arrived[2][c]] for c in range(len(chips))],
    ]
    others = [layout.swapped(stacked([part for chip in own for part in chip]), 1) for own in rows]
    mine, over = [], []
    for some in ((0, 1),) if planes <= 4 else ((0,), (1,)):
        slots = capacity * sum(
            part.shape[0] for g in some for chip in rows[g] for part in chip
        ) * 2 // count_of_rows
        results = run_experts(
            [rows[g] for g in some],
            [others[g] for g in some],
            w_gate_up,
            w_down,
            expert,
            top_count,
            slots,
        )
        mine += results[0]
        over += results[1]
    finished = []
    for parts, sent in zip(mine, over):
        back = layout.swapped(sent, 1)
        sums = add_up([parts, [back]], [part.shape[0] for part in parts], "add_cores")
        finished.append([layout.swapped(part, chip) for part, chip in zip(sums, chips)])
    near, far = finished
    others = []
    for parts, shifts in ((far, groups[2]), (near, [*groups[0], *groups[1]])):
        cuts = [count_of_rows] * len(shifts)
        sums = add_up([[part] for part in parts], cuts, "add_chips")
        others += [layout.shifted(part, s) for part, s in zip(sums, shifts)]
    total = merged.astype(jnp.float32) + sum(part.astype(jnp.float32) for part in others)
    layer_out = total.astype(jnp.bfloat16)
    return (attended, layer_out)


def solution(mesh):
    return jax.shard_map(
        local,
        mesh=mesh,
        in_specs=(
            P(("pool", "dev"), None),
            P(("pool", "dev"), None),
            P(("pool", "dev"), None, None),
            P(("pool", "dev"), None),
            P(("pool", "dev")),
            P(("pool", "dev")),
            P(("pool", "dev"), None),
            P(),
            P(("pool", "dev"), None),
            P(("pool", "dev"), None),
            P(("pool", "dev"), None, None),
            P(("pool", "dev"), None, None),
        ),
        out_specs=(P(("pool", "dev"), None), P(("pool", "dev"), None)),
        check_vma=False,
    )
```

```python
import math

import jax
import jax.numpy as jnp
from jax import lax
from jax.experimental import pallas as pl
from jax.experimental.pallas import tpu as pltpu
from jax.sharding import PartitionSpec as P

HEAD_DIMENSION = 128
KEY_VALUE_HEADS = 2
QUERY_GROUP_SIZE = 16
HEADS = KEY_VALUE_HEADS * QUERY_GROUP_SIZE

masked_score = -1e30
epsilon = 1e-06
AXES = ("pool", "dev")
VMEM = pl.BlockSpec(memory_space=pltpu.VMEM)
SMEM = pl.BlockSpec(memory_space=pltpu.SMEM)
HBM = pl.BlockSpec(memory_space=pltpu.HBM)
MEBI = 1 << 20


def in_hbm(value):
    return pltpu.with_memory_space_constraint(value, pltpu.HBM)


class Layout:
    def __init__(self, pool, dev):
        self.pool, self.dev = pool, dev
        self.inner = math.gcd(dev, 4)
        self.planes = dev // self.inner
        self.members = pool * self.inner
        self.groups = [
            [self.linear(member, plane) for member in range(self.members)]
            for plane in range(self.planes)
        ]

    def linear(self, member, plane):
        return member // self.inner * self.dev + plane * self.inner + member % self.inner

    def shifted(self, value, by):
        if by == 0:
            return value
        pairs = [
            (self.linear(m, z), self.linear(m, z ^ by))
            for z in range(self.planes)
            for m in range(self.members)
        ]
        with jax.named_scope(f"plane_{by}"):
            return lax.ppermute(value, AXES, pairs)

    def swapped(self, value, by):
        if by == 0:
            return value
        pairs = [
            (self.linear(m, z), self.linear(m ^ by, z))
            for z in range(self.planes)
            for m in range(self.members)
        ]
        with jax.named_scope(f"member_{by}"):
            return lax.ppermute(value, AXES, pairs)


def from_behind(value, axis, by):
    length = lax.axis_size(axis)
    return lax.ppermute(value, axis, [(i, (i + by) % length) for i in range(length)])


def pick_pages(slots, pages):
    count = slots.shape[0]
    last = pages.shape[0] - 1

    def kernel(slots_ref, pages_ref, out_ref, sems):
        copies = []
        for i in range(count):
            page = jnp.clip(slots_ref[i], 0, last)
            copies.append(pltpu.make_async_copy(pages_ref.at[page], out_ref.at[i], sems.at[i]))
            copies[-1].start()
        for copy in copies:
            copy.wait()

    return pl.pallas_call(
        kernel,
        out_shape=jax.ShapeDtypeStruct((count,) + pages.shape[1:], pages.dtype),
        in_specs=[SMEM, HBM],
        out_specs=VMEM,
        scratch_shapes=[pltpu.SemaphoreType.DMA((count,))],
        compiler_params=pltpu.CompilerParams(vmem_limit_bytes=4 * MEBI),
        cost_estimate=pl.CostEstimate(flops=0, bytes_accessed=MEBI, transcendentals=0),
        name="pick_pages",
    )(slots, in_hbm(pages))


def head_blocks(query):
    rows = query.shape[0]
    head = lax.broadcasted_iota(jnp.int32, (rows, HEAD_DIMENSION), 0) % HEADS
    nothing = jnp.zeros_like(query)
    low = head < QUERY_GROUP_SIZE
    return jnp.concatenate([jnp.where(low, query, nothing), jnp.where(low, nothing, query)], axis=1)


def own_head(both):
    rows = both.shape[0]
    head = lax.broadcasted_iota(jnp.int32, (rows, HEAD_DIMENSION), 0) % HEADS
    return jnp.where(
        head < QUERY_GROUP_SIZE, both[:, :HEAD_DIMENSION], both[:, HEAD_DIMENSION:]
    )


def tokens_of_pages(table, lengths_ref, first, page_len):
    count_of_rows, width = table.shape
    page = lax.broadcasted_iota(jnp.int32, (count_of_rows, 128), 1) + first
    row = lax.broadcasted_iota(jnp.int32, (count_of_rows, 128), 0)
    lengths = jnp.zeros((count_of_rows, 128), jnp.int32)
    for r in range(count_of_rows):
        lengths = jnp.where(row == r, lengths_ref[r], lengths)
    held = jnp.zeros((count_of_rows, 128), jnp.float32)
    for p in range(width):
        filled = jnp.clip(lengths - p * page_len, 0, page_len).astype(jnp.float32)
        held = held + jnp.where(table[:, p : p + 1] == page, filled, 0.0)
    return held


def token_bias(held, first_page, tokens, page_len):
    page = lax.broadcasted_iota(jnp.int32, (128, tokens), 0)
    token = lax.broadcasted_iota(jnp.int32, (128, tokens), 1)
    widen = (page == token // page_len + first_page).astype(jnp.bfloat16)
    limit = jnp.dot(held.astype(jnp.bfloat16), widen, preferred_element_type=jnp.float32)
    inside = (token[: held.shape[0]] % page_len).astype(jnp.float32)
    return jnp.where(inside < limit, 0.0, masked_score)


def masked_scores(blocks, keys, bias, scaling):
    scores = lax.dot_general(
        blocks, keys, (((1,), (1,)), ((), ())), preferred_element_type=jnp.float32
    )
    requests, tokens = bias.shape
    return (
        (scores * scaling).reshape(requests, HEADS, tokens) + bias[:, None, :]
    ).reshape(requests * HEADS, tokens)


def narrowed(value, join):
    result = value[:, :128]
    for start in range(128, value.shape[1], 128):
        result = join(result, value[:, start : start + 128])
    return result


def own_attention(queries, new_kv, pages, table, lengths):
    page_count, page_len, kv_width = pages.shape
    requests = new_kv.shape[0]
    rows = requests * HEADS
    half = kv_width // 2
    chunk_pages = 128 * (page_count // 128) // 4
    chunk = chunk_pages * page_len
    chunks = page_count // chunk_pages
    scaling = 1.0 / math.sqrt(HEAD_DIMENSION)

    def kernel(
        queries_hbm,
        new_hbm,
        pages_hbm,
        table_hbm,
        lengths_hbm,
        out_ref,
        top_ref,
        sum_ref,
        query_ref,
        s_ref,
        fresh_ref,
        heads_ref,
        flat_ref,
        pages_ref,
        table_ref,
        lengths_ref,
        sems,
    ):
        page_copies = [
            pltpu.make_async_copy(
                pages_hbm.at[pl.ds(c * chunk_pages, chunk_pages)],
                pages_ref.at[pl.ds(c * chunk_pages, chunk_pages)],
                sems.at[4 + c],
            )
            for c in range(chunks)
        ]
        copies = [
            pltpu.make_async_copy(queries_hbm, flat_ref, sems.at[0]),
            pltpu.make_async_copy(table_hbm, table_ref, sems.at[1]),
            pltpu.make_async_copy(lengths_hbm, lengths_ref, sems.at[2]),
            pltpu.make_async_copy(new_hbm, fresh_ref.at[pl.ds(0, requests)], sems.at[3]),
        ]
        fresh_ref[requests:] = jnp.zeros_like(fresh_ref[requests:])
        for copy in copies + page_copies:
            copy.start()
        for copy in copies:
            copy.wait()
        for h in range(HEADS):
            heads_ref[pl.ds(h, requests, stride=HEADS), :] = flat_ref[
                :, h * 128 : (h + 1) * 128
            ].astype(jnp.float32)
        query = heads_ref[...].astype(jnp.bfloat16)
        query_ref[...] = query
        blocks = head_blocks(query)
        held = tokens_of_pages(table_ref[...], lengths_ref, 0, page_len)
        lane = lax.broadcasted_iota(jnp.int32, (requests, 128), 1)
        own = lax.broadcasted_iota(jnp.int32, (requests, 128), 0)
        fresh_bias = jnp.where(lane == own, 0.0, masked_score)
        fresh = masked_scores(blocks, fresh_ref[:, :half], fresh_bias, scaling)
        s_ref[:, chunks * chunk :] = fresh
        top = fresh
        for c in range(chunks):
            page_copies[c].wait()
            keys = pages_ref[c * chunk_pages : (c + 1) * chunk_pages, :, :half].reshape(chunk, half)
            bias = token_bias(held, c * chunk_pages, chunk, page_len)
            scores = masked_scores(blocks, keys, bias, scaling)
            s_ref[:, c * chunk : (c + 1) * chunk] = scores
            top = jnp.maximum(top, narrowed(scores, jnp.maximum))
        top = jnp.max(top, axis=1, keepdims=True)
        weights = jnp.exp(s_ref[:, chunks * chunk :] - top)
        total = weights
        summed = jnp.dot(
            weights.astype(jnp.bfloat16), fresh_ref[:, half:], preferred_element_type=jnp.float32
        )
        for c in range(chunks):
            values = pages_ref[c * chunk_pages : (c + 1) * chunk_pages, :, half:].reshape(chunk, half)
            weights = jnp.exp(s_ref[:, c * chunk : (c + 1) * chunk] - top)
            total = total + narrowed(weights, jnp.add)
            summed = summed + jnp.dot(
                weights.astype(jnp.bfloat16), values, preferred_element_type=jnp.float32
            )
        out_ref[...] = own_head(summed)
        top_ref[...] = jnp.broadcast_to(top, top_ref.shape)
        sum_ref[...] = jnp.broadcast_to(jnp.sum(total, axis=1, keepdims=True), sum_ref.shape)

    shape = jax.ShapeDtypeStruct((rows, 128), jnp.float32)
    return pl.pallas_call(
        kernel,
        out_shape=(shape, shape, shape, jax.ShapeDtypeStruct((rows, 128), jnp.bfloat16)),
        in_specs=[HBM] * 5,
        out_specs=(VMEM,) * 4,
        scratch_shapes=[
            pltpu.VMEM((rows, chunks * chunk + 128), jnp.float32),
            pltpu.VMEM((128, kv_width), jnp.bfloat16),
            pltpu.VMEM((rows, 128), jnp.float32),
            pltpu.VMEM(queries.shape, jnp.bfloat16),
            pltpu.VMEM(pages.shape, jnp.bfloat16),
            pltpu.VMEM(table.shape, jnp.int32),
            pltpu.SMEM(lengths.shape, jnp.int32),
            pltpu.SemaphoreType.DMA((4 + chunks,)),
        ],
        compiler_params=pltpu.CompilerParams(vmem_limit_bytes=24 * MEBI),
        cost_estimate=pl.CostEstimate(
            flops=4 * rows * half * chunks * chunk,
            bytes_accessed=16 * MEBI,
            transcendentals=rows * chunks * chunk,
        ),
        name="own_attention",
    )(*[in_hbm(value) for value in (queries, new_kv, pages, table, lengths)])


def routing_columns(ids, gates):
    top_count = ids.shape[0]
    high = gates.astype(jnp.bfloat16)
    rest = gates - high.astype(jnp.float32)
    middle = rest.astype(jnp.bfloat16)
    low = (rest - middle.astype(jnp.float32)).astype(jnp.bfloat16)
    source = lax.broadcasted_iota(jnp.int32, (top_count, 128), 0)
    lane = lax.broadcasted_iota(jnp.int32, (top_count, 128), 1)
    columns = 0.0
    for i, part in enumerate((ids.astype(jnp.float32).astype(jnp.bfloat16), high, middle, low)):
        place = (lane == source + i * top_count).astype(jnp.bfloat16)
        columns = columns + lax.dot_general(
            part, place, (((0,), (0,)), ((), ())), preferred_element_type=jnp.float32
        )
    return columns.astype(jnp.bfloat16)


def stacked(parts):
    if len(parts) == 1:
        return parts[0]
    return jnp.concatenate(parts, axis=0)


def packed(parts, work=0):
    if len(parts) == 1 and not work:
        return parts[0]
    rows = sum(part.shape[0] for part in parts)
    columns = parts[0].shape[1]

    def kernel(*refs):
        out_ref, offset = refs[-1], 0
        for ref in refs[:-1]:
            out_ref[offset : offset + ref.shape[0]] = ref[...]
            offset += ref.shape[0]

    return pl.pallas_call(
        kernel,
        out_shape=jax.ShapeDtypeStruct((rows, columns), parts[0].dtype),
        in_specs=[VMEM] * len(parts),
        out_specs=VMEM,
        compiler_params=pltpu.CompilerParams(vmem_limit_bytes=12 * MEBI),
        cost_estimate=pl.CostEstimate(flops=work, bytes_accessed=0, transcendentals=0),
        name="packed",
    )(*parts)


def after(value, *others):
    return lax.optimization_barrier((value, *others))[0]


def run_experts(groups, others, gate_up, down_proj, expert, top_count, slots):
    model_dim, double = gate_up.shape[1:]
    hidden_dim = double // 2
    chips = len(groups[0])
    flat = [part for group in groups for chip in group for part in chip]
    shares = [sum(part.shape[0] for part in group[0]) for group in groups]
    rows = sum(part.shape[0] for part in flat) + sum(other.shape[0] for other in others)
    width = 256
    up_steps = hidden_dim // width
    out_width = 1024 if rows <= 512 else 512
    out_steps = model_dim // out_width
    strip = 256

    def kernel(expert_ref, *refs):
        own_refs, refs = refs[: len(flat)], refs[len(flat) :]
        other_refs, refs = refs[: len(others)], refs[len(others) :]
        up_hbm, down_hbm, refs = refs[0], refs[1], refs[2:]
        out_refs, refs = refs[: chips * len(groups)], refs[chips * len(groups) :]
        over_refs, refs = refs[: len(groups)], refs[len(groups) :]
        up_ref, down_ref, tokens_ref, hidden_ref, sems = refs
        up_copies, down_copies = [], []
        for c in range(up_steps):
            pair = []
            for half in range(2):
                columns = pl.ds(half * hidden_dim + c * width, width)
                pair.append(
                    pltpu.make_async_copy(
                        up_hbm.at[0, :, columns], up_ref.at[:, columns], sems.at[2 * c + half]
                    )
                )
                pair[-1].start()
            up_copies.append(pair)
        for c in range(out_steps):
            columns = pl.ds(c * out_width, out_width)
            down_copies.append(
                pltpu.make_async_copy(
                    down_hbm.at[0, :, columns], down_ref.at[:, columns], sems.at[2 * up_steps + c]
                )
            )
            down_copies[-1].start()

        token_refs = list(own_refs) + list(other_refs)
        routing = stacked([ref[:, model_dim:] for ref in token_refs]).astype(jnp.float32)
        wanted = expert_ref[0].astype(jnp.float32)
        match = jnp.zeros((rows, 1), jnp.float32)
        gates = [jnp.zeros((rows, 1), jnp.float32)] * 3
        for k in range(top_count):
            hit = routing[:, k : k + 1] == wanted
            match = jnp.where(hit, 1.0, match)
            gates = [
                jnp.where(hit, routing[:, i * top_count + k : i * top_count + k + 1], gate)
                for i, gate in enumerate(gates, 1)
            ]
        lane = lax.broadcasted_iota(jnp.int32, (rows, slots), 1)
        match = jnp.broadcast_to(match, (rows, slots))
        earlier = (
            lax.broadcasted_iota(jnp.int32, (strip, strip), 0)
            > lax.broadcasted_iota(jnp.int32, (strip, strip), 1)
        ).astype(jnp.bfloat16)
        ranks, before = [], jnp.zeros((1, slots), jnp.float32)
        for start in range(0, rows, strip):
            piece = match[start : start + strip]
            ranks.append(
                before
                + jnp.dot(earlier, piece.astype(jnp.bfloat16), preferred_element_type=jnp.float32)
            )
            before = before + jnp.sum(piece, axis=0, keepdims=True)
        rank = stacked(ranks)
        choice = jnp.where(rank == lane.astype(jnp.float32), match, 0.0)
        pick = choice.T.astype(jnp.bfloat16)
        place = choice.astype(jnp.bfloat16)
        gate_columns = jnp.where(
            lane == 0, gates[0], jnp.where(lane == 1, gates[1], jnp.where(lane == 2, gates[2], 0.0))
        ).astype(jnp.bfloat16)
        gate = jnp.sum(
            jnp.dot(pick, gate_columns, preferred_element_type=jnp.float32), axis=1, keepdims=True
        )
        for start in range(0, model_dim, out_width):
            columns = slice(start, start + out_width)
            tokens = stacked([ref[:, columns] for ref in token_refs])
            tokens_ref[:, columns] = jnp.dot(
                pick, tokens, preferred_element_type=jnp.float32
            ).astype(jnp.bfloat16)

        for c in range(up_steps):
            for copy in up_copies[c]:
                copy.wait()
            start = c * width
            tokens = tokens_ref[...]
            gated = jnp.dot(
                tokens, up_ref[:, start : start + width], preferred_element_type=jnp.float32
            )
            up = jnp.dot(
                tokens,
                up_ref[:, hidden_dim + start : hidden_dim + start + width],
                preferred_element_type=jnp.float32,
            )
            hidden_ref[:, start : start + width] = (gated / (1.0 + jnp.exp(-gated)) * up).astype(
                jnp.bfloat16
            )

        for c in range(out_steps):
            down_copies[c].wait()
            columns = slice(c * out_width, (c + 1) * out_width)
            result = jnp.dot(
                hidden_ref[...], down_ref[:, columns], preferred_element_type=jnp.float32
            )
            result = (result * gate).astype(jnp.bfloat16)
            sums = jnp.dot(place, result, preferred_element_type=jnp.float32).astype(jnp.bfloat16)
            offset = 0
            for i, ref in enumerate([*out_refs, *over_refs]):
                cut = ref.shape[0]
                ref[:, columns] = sums[offset : offset + cut]
                offset += cut

    shapes = [(share, model_dim) for share in shares for _ in range(chips)]
    shapes += [(other.shape[0], model_dim) for other in others]
    results = pl.pallas_call(
        kernel,
        out_shape=tuple(jax.ShapeDtypeStruct(shape, jnp.bfloat16) for shape in shapes),
        in_specs=[SMEM] + [VMEM] * (len(flat) + len(others)) + [HBM] * 2,
        out_specs=(VMEM,) * len(shapes),
        scratch_shapes=[
            pltpu.VMEM((model_dim, double), jnp.bfloat16),
            pltpu.VMEM((hidden_dim, model_dim), jnp.bfloat16),
            pltpu.VMEM((slots, model_dim), jnp.bfloat16),
            pltpu.VMEM((slots, hidden_dim), jnp.bfloat16),
            pltpu.SemaphoreType.DMA((2 * up_steps + out_steps,)),
        ],
        compiler_params=pltpu.CompilerParams(vmem_limit_bytes=28 * MEBI),
        cost_estimate=pl.CostEstimate(
            flops=6 * slots * model_dim * hidden_dim,
            bytes_accessed=20 * MEBI,
            transcendentals=slots * hidden_dim,
        ),
        name="run_experts",
    )(expert, *flat, *others, in_hbm(gate_up), in_hbm(down_proj))
    mine = [results[g * chips : (g + 1) * chips] for g in range(len(groups))]
    return mine, results[chips * len(groups) :]


def add_up(parts, cuts, name):
    rows = sum(cuts)
    model_dim = parts[0][0].shape[1]
    flat = [piece for part in parts for piece in part]
    places = []
    for part in parts:
        start = 0
        for piece in part:
            places.append((start, start + piece.shape[0]))
            start += piece.shape[0]

    def kernel(*refs):
        in_refs, out_refs = refs[: len(flat)], refs[len(flat) :]
        step = 1024
        for start in range(0, model_dim, step):
            columns = slice(start, start + step)
            offset = 0
            for out_ref, cut in zip(out_refs, cuts):
                total = 0.0
                for ref, (low, high) in zip(in_refs, places):
                    if low <= offset and offset + cut <= high:
                        rows_of = slice(offset - low, offset - low + cut)
                        total = total + ref[rows_of, columns].astype(jnp.float32)
                out_ref[:, columns] = total.astype(jnp.bfloat16)
                offset += cut

    return pl.pallas_call(
        kernel,
        out_shape=tuple(jax.ShapeDtypeStruct((cut, model_dim), jnp.bfloat16) for cut in cuts),
        in_specs=[VMEM] * len(flat),
        out_specs=(VMEM,) * len(cuts),
        compiler_params=pltpu.CompilerParams(vmem_limit_bytes=12 * MEBI),
        cost_estimate=pl.CostEstimate(
            flops=0, bytes_accessed=0, transcendentals=0
        ),
        name=name,
    )(*flat)


def finish_attention(
    query, fetched, table, lengths, partial, residual, gain, ids, gates, pages_own
):
    count, page_len, kv_width = fetched.shape
    half = kv_width // 2
    tokens = count * page_len
    requests, model_dim = residual.shape
    rows = query.shape[0]
    scaling = 1.0 / math.sqrt(HEAD_DIMENSION)

    def kernel(q_ref, fetched_ref, table_ref, lengths_ref, sum_ref, top_ref, total_ref, residual_ref, gain_ref, ids_ref, gates_ref, attended_ref, merged_ref, normed_ref, heads_ref):
        blocks = head_blocks(q_ref[...])
        held = tokens_of_pages(table_ref[...], lengths_ref, pages_own, page_len)
        bias = token_bias(held, 0, tokens, page_len)
        keys = fetched_ref[:, :, :half].reshape(tokens, half)
        values = fetched_ref[:, :, half:].reshape(tokens, half)
        scores = masked_scores(blocks, keys, bias, scaling)
        before = top_ref[...]
        shed_top = jnp.max(narrowed(scores, jnp.maximum), axis=1, keepdims=True)
        top = jnp.maximum(before, shed_top)
        kept = jnp.exp(before - top)
        weights = jnp.exp(scores - jnp.concatenate([top] * (tokens // 128), axis=1))
        added = jnp.sum(narrowed(weights, jnp.add), axis=1, keepdims=True)
        total = total_ref[...] * kept + added
        summed = own_head(
            jnp.dot(weights.astype(jnp.bfloat16), values, preferred_element_type=jnp.float32)
        )
        heads_ref[...] = (sum_ref[...] * kept + summed) / total
        square = jnp.zeros((requests, 128), jnp.float32)
        for h in range(HEADS):
            columns = slice(h * 128, (h + 1) * 128)
            attended = heads_ref[pl.ds(h, requests, stride=HEADS), :].astype(jnp.bfloat16)
            attended_ref[:, columns] = attended
            merged = (
                residual_ref[:, columns].astype(jnp.float32) + attended.astype(jnp.float32)
            ).astype(jnp.bfloat16)
            merged_ref[:, columns] = merged
            wide = merged.astype(jnp.float32)
            square = square + wide * wide
        mean = jnp.sum(square, axis=1, keepdims=True) * (1.0 / model_dim)
        inverse = lax.rsqrt(mean + epsilon)
        normed_ref[:, model_dim:] = routing_columns(ids_ref[...], gates_ref[...])
        normed_ref[:, :model_dim] = (
            merged_ref[...].astype(jnp.float32) * inverse * gain_ref[...]
        ).astype(jnp.bfloat16)

    shape = jax.ShapeDtypeStruct((requests, model_dim), jnp.bfloat16)
    return pl.pallas_call(
        kernel,
        out_shape=(shape, shape, jax.ShapeDtypeStruct((requests, model_dim + 128), jnp.bfloat16)),
        in_specs=[VMEM] * 3 + [SMEM] + [VMEM] * 7,
        out_specs=(VMEM,) * 3,
        scratch_shapes=[pltpu.VMEM((rows, 128), jnp.float32)],
        compiler_params=pltpu.CompilerParams(vmem_limit_bytes=16 * MEBI),
        cost_estimate=pl.CostEstimate(
            flops=4 * rows * half * tokens, bytes_accessed=4 * MEBI, transcendentals=rows * tokens
        ),
        name="finish_attention",
    )(query, fetched, table, lengths, *partial, residual, gain, ids, gates)


def local(
    queries,
    new_kv,
    kv_pages,
    page_table,
    lengths,
    shed_slots,
    residual,
    norm_gain,
    expert_ids,
    gate_weights,
    w_gate_up,
    w_down,
):
    count_of_rows, model_dim = queries.shape
    top_count = expert_ids.shape[1]
    layout = Layout(lax.axis_size("pool"), lax.axis_size("dev"))
    capacity = 2 * count_of_rows * top_count // (layout.pool * layout.dev)
    planes = layout.planes

    requested = from_behind(shed_slots, "pool", 1)
    picked = pick_pages(requested, kv_pages)
    fetched = from_behind(picked, "pool", 1)
    queries, expert_ids, picked = lax.optimization_barrier((queries, expert_ids, picked))

    expert = (lax.axis_index("pool") * layout.dev + lax.axis_index("dev")).reshape(1)
    *partial, query = own_attention(queries, new_kv, kv_pages, page_table, lengths)
    attended, merged, normed = finish_attention(
        query,
        fetched,
        page_table,
        lengths,
        partial,
        residual,
        norm_gain.reshape(1, model_dim),
        expert_ids.T,
        gate_weights.T,
        kv_pages.shape[0],
    )

    first = max(1, planes // 4)
    groups = [range(0, first), range(first, 2 * first), range(2 * first, planes)]
    chips = range(0, layout.members, 2)
    blocks = [layout.shifted(normed, s) for s in range(planes)]
    arrived = []
    for g, group in enumerate(groups):
        rows = packed([blocks[s] for s in group])
        sent = []
        for c, chip in enumerate(chips):
            ready = rows
            if g == 1:
                ready = after(rows, arrived[0][c])
            sent.append(layout.swapped(ready, chip))
        arrived.append(sent)
    arrived[0][0] = after(arrived[0][0], arrived[2][0])

    def to_experts(members, tie):
        own = [[arrived[g][c] for g in members] for c in range(len(chips))]
        pieces = [part for chip in own for part in chip]
        if tie is not None:
            pieces[0] = after(pieces[0], tie)
        other = layout.swapped(packed(pieces), 1)
        slots = layout.members * sum(len(groups[g]) for g in members) * capacity
        return own, other, slots

    def from_experts(own, other, slots):
        (mine,), (over,) = run_experts(
            [own], [other], w_gate_up, w_down, expert, top_count, slots
        )
        return mine, over

    def add_cores(mine, over):
        back = layout.swapped(over, 1)
        cuts = [count_of_rows] * (sum(part.shape[0] for part in mine) // count_of_rows)
        return add_up([mine, [back]], cuts, "add_cores")

    def to_owners(sums, i):
        pieces = len(sums) // len(chips)
        return [layout.swapped(sums[c * pieces + i], chip) for c, chip in enumerate(chips)]

    def from_owners(parts, by):
        total = add_up([[part] for part in parts], [count_of_rows], "add_chips")[0]
        return layout.shifted(total, by)

    near = [s for g in (0, 1) for s in groups[g]]
    mine, over = from_experts(*to_experts((0, 1), None))
    far_own, far_other, slots = to_experts((2,), over)
    near_sums = add_cores(mine, over)
    mine, over = from_experts(far_own, after(far_other, near_sums[0]), slots)
    early = [(to_owners(near_sums, i), near[i]) for i in range(1, len(near))]
    over = after(over, *[part for parts, _ in early for part in parts[1:]])
    far_sums = add_cores(mine, over)
    late = [(to_owners(far_sums, i), s) for i, s in enumerate(groups[2])]
    late.append((to_owners(near_sums, 0), near[0]))
    others = [from_owners(parts, s) for parts, s in early + late]
    total = merged.astype(jnp.float32) + sum(part.astype(jnp.float32) for part in others)
    layer_out = total.astype(jnp.bfloat16)
    return (attended, layer_out)


def solution(mesh):
    return jax.shard_map(
        local,
        mesh=mesh,
        in_specs=(
            P(("pool", "dev"), None),
            P(("pool", "dev"), None),
            P(("pool", "dev"), None, None),
            P(("pool", "dev"), None),
            P(("pool", "dev")),
            P(("pool", "dev")),
            P(("pool", "dev"), None),
            P(),
            P(("pool", "dev"), None),
            P(("pool", "dev"), None),
            P(("pool", "dev"), None, None),
            P(("pool", "dev"), None, None),
        ),
        out_specs=(P(("pool", "dev"), None), P(("pool", "dev"), None)),
        check_vma=False,
    )
```

```python
import math

import jax
import jax.numpy as jnp
from jax import lax
from jax.experimental import pallas as pl
from jax.experimental.pallas import tpu as pltpu
from jax.sharding import PartitionSpec as P

HEAD_DIMENSION = 128
KEY_VALUE_HEADS = 2
QUERY_GROUP_SIZE = 16
HEADS = KEY_VALUE_HEADS * QUERY_GROUP_SIZE

masked_score = -1e30
epsilon = 1e-06
AXES = ("pool", "dev")
VMEM = pl.BlockSpec(memory_space=pltpu.VMEM)
SMEM = pl.BlockSpec(memory_space=pltpu.SMEM)
HBM = pl.BlockSpec(memory_space=pltpu.HBM)
MEBI = 1 << 20
EXPERT_LIMIT = 16 * MEBI


def in_hbm(value):
    return pltpu.with_memory_space_constraint(value, pltpu.HBM)


class Layout:
    def __init__(self, pool, dev):
        self.pool, self.dev = pool, dev
        self.inner = math.gcd(dev, 4)
        self.planes = dev // self.inner
        self.members = pool * self.inner
        self.groups = [
            [self.linear(member, plane) for member in range(self.members)]
            for plane in range(self.planes)
        ]

    def linear(self, member, plane):
        return member // self.inner * self.dev + plane * self.inner + member % self.inner

    def shifted(self, value, by):
        if by == 0:
            return value
        pairs = [
            (self.linear(m, z), self.linear(m, z ^ by))
            for z in range(self.planes)
            for m in range(self.members)
        ]
        with jax.named_scope(f"plane_{by}"):
            return lax.ppermute(value, AXES, pairs)

    def swapped(self, value, by):
        if by == 0:
            return value
        pairs = [
            (self.linear(m, z), self.linear(m ^ by, z))
            for z in range(self.planes)
            for m in range(self.members)
        ]
        with jax.named_scope(f"member_{by}"):
            return lax.ppermute(value, AXES, pairs)


def from_behind(value, axis, by):
    length = lax.axis_size(axis)
    return lax.ppermute(value, axis, [(i, (i + by) % length) for i in range(length)])


def pick_pages(slots, pages):
    count = slots.shape[0]
    last = pages.shape[0] - 1

    def kernel(slots_ref, pages_ref, out_ref, sems):
        copies = []
        for i in range(count):
            page = jnp.clip(slots_ref[i], 0, last)
            copies.append(pltpu.make_async_copy(pages_ref.at[page], out_ref.at[i], sems.at[i]))
            copies[-1].start()
        for copy in copies:
            copy.wait()

    return pl.pallas_call(
        kernel,
        out_shape=jax.ShapeDtypeStruct((count,) + pages.shape[1:], pages.dtype),
        in_specs=[SMEM, HBM],
        out_specs=VMEM,
        scratch_shapes=[pltpu.SemaphoreType.DMA((count,))],
        compiler_params=pltpu.CompilerParams(vmem_limit_bytes=4 * MEBI),
        cost_estimate=pl.CostEstimate(flops=0, bytes_accessed=MEBI, transcendentals=0),
        name="pick_pages",
    )(slots, in_hbm(pages))


def head_blocks(query):
    rows = query.shape[0]
    head = lax.broadcasted_iota(jnp.int32, (rows, HEAD_DIMENSION), 0) % HEADS
    nothing = jnp.zeros_like(query)
    low = head < QUERY_GROUP_SIZE
    return jnp.concatenate([jnp.where(low, query, nothing), jnp.where(low, nothing, query)], axis=1)


def own_head(both):
    rows = both.shape[0]
    head = lax.broadcasted_iota(jnp.int32, (rows, HEAD_DIMENSION), 0) % HEADS
    return jnp.where(
        head < QUERY_GROUP_SIZE, both[:, :HEAD_DIMENSION], both[:, HEAD_DIMENSION:]
    )


def tokens_of_pages(table, lengths_ref, first, page_len):
    count_of_rows, width = table.shape
    page = lax.broadcasted_iota(jnp.int32, (count_of_rows, 128), 1) + first
    row = lax.broadcasted_iota(jnp.int32, (count_of_rows, 128), 0)
    lengths = jnp.zeros((count_of_rows, 128), jnp.int32)
    for r in range(count_of_rows):
        lengths = jnp.where(row == r, lengths_ref[r], lengths)
    held = jnp.zeros((count_of_rows, 128), jnp.float32)
    for p in range(width):
        filled = jnp.clip(lengths - p * page_len, 0, page_len).astype(jnp.float32)
        held = held + jnp.where(table[:, p : p + 1] == page, filled, 0.0)
    return held


def token_bias(held, first_page, tokens, page_len):
    page = lax.broadcasted_iota(jnp.int32, (128, tokens), 0)
    token = lax.broadcasted_iota(jnp.int32, (128, tokens), 1)
    widen = (page == token // page_len + first_page).astype(jnp.bfloat16)
    limit = jnp.dot(held.astype(jnp.bfloat16), widen, preferred_element_type=jnp.float32)
    inside = (token[: held.shape[0]] % page_len).astype(jnp.float32)
    return jnp.where(inside < limit, 0.0, masked_score)


def masked_scores(blocks, keys, bias, scaling):
    scores = lax.dot_general(
        blocks, keys, (((1,), (1,)), ((), ())), preferred_element_type=jnp.float32
    )
    requests, tokens = bias.shape
    return (
        (scores * scaling).reshape(requests, HEADS, tokens) + bias[:, None, :]
    ).reshape(requests * HEADS, tokens)


def narrowed(value, join):
    result = value[:, :128]
    for start in range(128, value.shape[1], 128):
        result = join(result, value[:, start : start + 128])
    return result


def own_attention(queries, new_kv, pages, table, lengths):
    page_count, page_len, kv_width = pages.shape
    requests = new_kv.shape[0]
    rows = requests * HEADS
    half = kv_width // 2
    chunk_pages = 128 * (page_count // 128) // 4
    chunk = chunk_pages * page_len
    chunks = page_count // chunk_pages
    scaling = 1.0 / math.sqrt(HEAD_DIMENSION)

    def kernel(
        queries_hbm,
        new_hbm,
        pages_hbm,
        table_hbm,
        lengths_hbm,
        out_ref,
        top_ref,
        sum_ref,
        query_ref,
        s_ref,
        fresh_ref,
        heads_ref,
        flat_ref,
        pages_ref,
        table_ref,
        lengths_ref,
        sems,
    ):
        page_copies = [
            pltpu.make_async_copy(
                pages_hbm.at[pl.ds(c * chunk_pages, chunk_pages)],
                pages_ref.at[pl.ds(c * chunk_pages, chunk_pages)],
                sems.at[4 + c],
            )
            for c in range(chunks)
        ]
        copies = [
            pltpu.make_async_copy(queries_hbm, flat_ref, sems.at[0]),
            pltpu.make_async_copy(table_hbm, table_ref, sems.at[1]),
            pltpu.make_async_copy(lengths_hbm, lengths_ref, sems.at[2]),
            pltpu.make_async_copy(new_hbm, fresh_ref.at[pl.ds(0, requests)], sems.at[3]),
        ]
        fresh_ref[requests:] = jnp.zeros_like(fresh_ref[requests:])
        for copy in copies + page_copies:
            copy.start()
        for copy in copies:
            copy.wait()
        for h in range(HEADS):
            heads_ref[pl.ds(h, requests, stride=HEADS), :] = flat_ref[
                :, h * 128 : (h + 1) * 128
            ].astype(jnp.float32)
        query = heads_ref[...].astype(jnp.bfloat16)
        query_ref[...] = query
        blocks = head_blocks(query)
        held = tokens_of_pages(table_ref[...], lengths_ref, 0, page_len)
        lane = lax.broadcasted_iota(jnp.int32, (requests, 128), 1)
        own = lax.broadcasted_iota(jnp.int32, (requests, 128), 0)
        fresh_bias = jnp.where(lane == own, 0.0, masked_score)
        fresh = masked_scores(blocks, fresh_ref[:, :half], fresh_bias, scaling)
        s_ref[:, chunks * chunk :] = fresh
        top = fresh
        for c in range(chunks):
            page_copies[c].wait()
            keys = pages_ref[c * chunk_pages : (c + 1) * chunk_pages, :, :half].reshape(chunk, half)
            bias = token_bias(held, c * chunk_pages, chunk, page_len)
            scores = masked_scores(blocks, keys, bias, scaling)
            s_ref[:, c * chunk : (c + 1) * chunk] = scores
            top = jnp.maximum(top, narrowed(scores, jnp.maximum))
        top = jnp.max(top, axis=1, keepdims=True)
        weights = jnp.exp(s_ref[:, chunks * chunk :] - top)
        total = weights
        summed = jnp.dot(
            weights.astype(jnp.bfloat16), fresh_ref[:, half:], preferred_element_type=jnp.float32
        )
        for c in range(chunks):
            values = pages_ref[c * chunk_pages : (c + 1) * chunk_pages, :, half:].reshape(chunk, half)
            weights = jnp.exp(s_ref[:, c * chunk : (c + 1) * chunk] - top)
            total = total + narrowed(weights, jnp.add)
            summed = summed + jnp.dot(
                weights.astype(jnp.bfloat16), values, preferred_element_type=jnp.float32
            )
        out_ref[...] = own_head(summed)
        top_ref[...] = jnp.broadcast_to(top, top_ref.shape)
        sum_ref[...] = jnp.broadcast_to(jnp.sum(total, axis=1, keepdims=True), sum_ref.shape)

    shape = jax.ShapeDtypeStruct((rows, 128), jnp.float32)
    return pl.pallas_call(
        kernel,
        out_shape=(shape, shape, shape, jax.ShapeDtypeStruct((rows, 128), jnp.bfloat16)),
        in_specs=[HBM] * 5,
        out_specs=(VMEM,) * 4,
        scratch_shapes=[
            pltpu.VMEM((rows, chunks * chunk + 128), jnp.float32),
            pltpu.VMEM((128, kv_width), jnp.bfloat16),
            pltpu.VMEM((rows, 128), jnp.float32),
            pltpu.VMEM(queries.shape, jnp.bfloat16),
            pltpu.VMEM(pages.shape, jnp.bfloat16),
            pltpu.VMEM(table.shape, jnp.int32),
            pltpu.SMEM(lengths.shape, jnp.int32),
            pltpu.SemaphoreType.DMA((4 + chunks,)),
        ],
        compiler_params=pltpu.CompilerParams(vmem_limit_bytes=24 * MEBI),
        cost_estimate=pl.CostEstimate(
            flops=4 * rows * half * chunks * chunk,
            bytes_accessed=16 * MEBI,
            transcendentals=rows * chunks * chunk,
        ),
        name="own_attention",
    )(*[in_hbm(value) for value in (queries, new_kv, pages, table, lengths)])


def routing_columns(ids, gates):
    top_count = ids.shape[0]
    high = gates.astype(jnp.bfloat16)
    rest = gates - high.astype(jnp.float32)
    middle = rest.astype(jnp.bfloat16)
    low = (rest - middle.astype(jnp.float32)).astype(jnp.bfloat16)
    source = lax.broadcasted_iota(jnp.int32, (top_count, 128), 0)
    lane = lax.broadcasted_iota(jnp.int32, (top_count, 128), 1)
    columns = 0.0
    for i, part in enumerate((ids.astype(jnp.float32).astype(jnp.bfloat16), high, middle, low)):
        place = (lane == source + i * top_count).astype(jnp.bfloat16)
        columns = columns + lax.dot_general(
            part, place, (((0,), (0,)), ((), ())), preferred_element_type=jnp.float32
        )
    return columns.astype(jnp.bfloat16)


def stacked(parts):
    if len(parts) == 1:
        return parts[0]
    return jnp.concatenate(parts, axis=0)


def packed(parts, work=0):
    if len(parts) == 1 and not work:
        return parts[0]
    rows = sum(part.shape[0] for part in parts)
    columns = parts[0].shape[1]

    def kernel(*refs):
        out_ref, offset = refs[-1], 0
        for ref in refs[:-1]:
            out_ref[offset : offset + ref.shape[0]] = ref[...]
            offset += ref.shape[0]

    return pl.pallas_call(
        kernel,
        out_shape=jax.ShapeDtypeStruct((rows, columns), parts[0].dtype),
        in_specs=[VMEM] * len(parts),
        out_specs=VMEM,
        compiler_params=pltpu.CompilerParams(vmem_limit_bytes=12 * MEBI),
        cost_estimate=pl.CostEstimate(flops=work, bytes_accessed=0, transcendentals=0),
        name="packed",
    )(*parts)


def after(value, *others):
    return lax.optimization_barrier((value, *others))[0]


def run_experts(own, other, weights, expert, top_count, slots, keep):
    rows, model_dim = own.shape
    rows, model_dim = 2 * rows, model_dim - 128
    gate_up, down_proj = weights
    double, hidden_dim = gate_up.shape[-1], down_proj.shape[-2]
    width = 256
    up_steps = hidden_dim // width
    out_width = 1024 if rows <= 512 else 512
    out_steps = model_dim // out_width
    strip = 256

    def kernel(expert_ref, own_ref, other_ref, *refs):
        copies = {}
        if keep:
            up_hbm, down_hbm, out_ref, over_ref, up_ref, down_ref, tokens_ref, hidden_ref, sems = refs
            for c in range(up_steps):
                for half in range(2):
                    columns = pl.ds(half * hidden_dim + c * width, width)
                    copies["up", c, half] = pltpu.make_async_copy(
                        up_hbm.at[0, :, columns], up_ref.at[:, columns], sems.at[2 * c + half]
                    )
            for c in range(out_steps):
                columns = pl.ds(c * out_width, out_width)
                copies["down", c] = pltpu.make_async_copy(
                    down_hbm.at[0, :, columns], down_ref.at[:, columns], sems.at[2 * up_steps + c]
                )
            for copy in copies.values():
                copy.start()
        else:
            up_ref, down_ref, out_ref, over_ref, tokens_ref, hidden_ref = refs

        def arrive(*name):
            if keep:
                copies[name].wait()

        token_refs = [own_ref, other_ref]
        routing = stacked([ref[:, model_dim:] for ref in token_refs]).astype(jnp.float32)
        wanted = expert_ref[0].astype(jnp.float32)
        match = jnp.zeros((rows, 1), jnp.float32)
        gates = [jnp.zeros((rows, 1), jnp.float32)] * 3
        for k in range(top_count):
            hit = routing[:, k : k + 1] == wanted
            match = jnp.where(hit, 1.0, match)
            gates = [
                jnp.where(hit, routing[:, i * top_count + k : i * top_count + k + 1], gate)
                for i, gate in enumerate(gates, 1)
            ]
        lane = lax.broadcasted_iota(jnp.int32, (rows, slots), 1)
        match = jnp.broadcast_to(match, (rows, slots))
        earlier = (
            lax.broadcasted_iota(jnp.int32, (strip, strip), 0)
            > lax.broadcasted_iota(jnp.int32, (strip, strip), 1)
        ).astype(jnp.bfloat16)
        ranks, before = [], jnp.zeros((1, slots), jnp.float32)
        for start in range(0, rows, strip):
            piece = match[start : start + strip]
            ranks.append(
                before
                + jnp.dot(earlier, piece.astype(jnp.bfloat16), preferred_element_type=jnp.float32)
            )
            before = before + jnp.sum(piece, axis=0, keepdims=True)
        rank = stacked(ranks)
        choice = jnp.where(rank == lane.astype(jnp.float32), match, 0.0)
        pick = choice.T.astype(jnp.bfloat16)
        place = choice.astype(jnp.bfloat16)
        gate_columns = jnp.where(
            lane == 0, gates[0], jnp.where(lane == 1, gates[1], jnp.where(lane == 2, gates[2], 0.0))
        ).astype(jnp.bfloat16)
        gate = jnp.sum(
            jnp.dot(pick, gate_columns, preferred_element_type=jnp.float32), axis=1, keepdims=True
        )
        for start in range(0, model_dim, out_width):
            columns = slice(start, start + out_width)
            tokens = stacked([ref[:, columns] for ref in token_refs])
            tokens_ref[:, columns] = jnp.dot(
                pick, tokens, preferred_element_type=jnp.float32
            ).astype(jnp.bfloat16)

        for c in range(up_steps):
            arrive("up", c, 0)
            arrive("up", c, 1)
            start = c * width
            tokens = tokens_ref[...]
            gated = jnp.dot(
                tokens, up_ref[:, start : start + width], preferred_element_type=jnp.float32
            )
            up = jnp.dot(
                tokens,
                up_ref[:, hidden_dim + start : hidden_dim + start + width],
                preferred_element_type=jnp.float32,
            )
            hidden_ref[:, start : start + width] = (gated / (1.0 + jnp.exp(-gated)) * up).astype(
                jnp.bfloat16
            )

        for c in range(out_steps):
            arrive("down", c)
            columns = slice(c * out_width, (c + 1) * out_width)
            result = jnp.dot(
                hidden_ref[...], down_ref[:, columns], preferred_element_type=jnp.float32
            )
            result = (result * gate).astype(jnp.bfloat16)
            sums = jnp.dot(place, result, preferred_element_type=jnp.float32).astype(jnp.bfloat16)
            out_ref[:, columns] = sums[: rows // 2]
            over_ref[:, columns] = sums[rows // 2 :]

    shape = jax.ShapeDtypeStruct((rows // 2, model_dim), jnp.bfloat16)
    kept, scratch = (), []
    if keep:
        kept = (
            pltpu.VMEM((model_dim, double), jnp.bfloat16),
            pltpu.VMEM((hidden_dim, model_dim), jnp.bfloat16),
        )
        scratch = [pltpu.SemaphoreType.DMA((2 * up_steps + out_steps,))]
        weights = [in_hbm(gate_up), in_hbm(down_proj)]
    else:
        weights = [pltpu.with_memory_space_constraint(value, pltpu.VMEM) for value in weights]
    results = pl.pallas_call(
        kernel,
        out_shape=(shape, shape) + kept,
        in_specs=[SMEM, VMEM, VMEM] + [HBM if keep else VMEM] * 2,
        out_specs=(VMEM,) * (2 + len(kept)),
        scratch_shapes=[
            pltpu.VMEM((slots, model_dim), jnp.bfloat16),
            pltpu.VMEM((slots, hidden_dim), jnp.bfloat16),
        ]
        + scratch,
        compiler_params=pltpu.CompilerParams(vmem_limit_bytes=EXPERT_LIMIT),
        cost_estimate=pl.CostEstimate(
            flops=6 * slots * model_dim * hidden_dim,
            bytes_accessed=20 * MEBI,
            transcendentals=slots * hidden_dim,
        ),
        name="run_experts",
    )(expert, own, other, *weights)
    return results[0], results[1], results[2:]


def add_up(parts, cuts, name):
    rows = sum(cuts)
    model_dim = parts[0][0].shape[1]
    flat = [piece for part in parts for piece in part]
    places = []
    for part in parts:
        start = 0
        for piece in part:
            places.append((start, start + piece.shape[0]))
            start += piece.shape[0]

    def kernel(*refs):
        in_refs, out_refs = refs[: len(flat)], refs[len(flat) :]
        step = 1024
        for start in range(0, model_dim, step):
            columns = slice(start, start + step)
            offset = 0
            for out_ref, cut in zip(out_refs, cuts):
                total = 0.0
                for ref, (low, high) in zip(in_refs, places):
                    if low <= offset and offset + cut <= high:
                        rows_of = slice(offset - low, offset - low + cut)
                        total = total + ref[rows_of, columns].astype(jnp.float32)
                out_ref[:, columns] = total.astype(jnp.bfloat16)
                offset += cut

    return pl.pallas_call(
        kernel,
        out_shape=tuple(jax.ShapeDtypeStruct((cut, model_dim), jnp.bfloat16) for cut in cuts),
        in_specs=[VMEM] * len(flat),
        out_specs=(VMEM,) * len(cuts),
        compiler_params=pltpu.CompilerParams(vmem_limit_bytes=12 * MEBI),
        cost_estimate=pl.CostEstimate(
            flops=0, bytes_accessed=0, transcendentals=0
        ),
        name=name,
    )(*flat)


def finish_attention(
    query, fetched, table, lengths, partial, residual, gain, ids, gates, pages_own
):
    count, page_len, kv_width = fetched.shape
    half = kv_width // 2
    tokens = count * page_len
    requests, model_dim = residual.shape
    rows = query.shape[0]
    scaling = 1.0 / math.sqrt(HEAD_DIMENSION)

    def kernel(q_ref, fetched_ref, table_ref, lengths_ref, sum_ref, top_ref, total_ref, residual_ref, gain_ref, ids_ref, gates_ref, attended_ref, merged_ref, normed_ref, heads_ref):
        blocks = head_blocks(q_ref[...])
        held = tokens_of_pages(table_ref[...], lengths_ref, pages_own, page_len)
        bias = token_bias(held, 0, tokens, page_len)
        keys = fetched_ref[:, :, :half].reshape(tokens, half)
        values = fetched_ref[:, :, half:].reshape(tokens, half)
        scores = masked_scores(blocks, keys, bias, scaling)
        before = top_ref[...]
        shed_top = jnp.max(narrowed(scores, jnp.maximum), axis=1, keepdims=True)
        top = jnp.maximum(before, shed_top)
        kept = jnp.exp(before - top)
        weights = jnp.exp(scores - jnp.concatenate([top] * (tokens // 128), axis=1))
        added = jnp.sum(narrowed(weights, jnp.add), axis=1, keepdims=True)
        total = total_ref[...] * kept + added
        summed = own_head(
            jnp.dot(weights.astype(jnp.bfloat16), values, preferred_element_type=jnp.float32)
        )
        heads_ref[...] = (sum_ref[...] * kept + summed) / total
        square = jnp.zeros((requests, 128), jnp.float32)
        for h in range(HEADS):
            columns = slice(h * 128, (h + 1) * 128)
            attended = heads_ref[pl.ds(h, requests, stride=HEADS), :].astype(jnp.bfloat16)
            attended_ref[:, columns] = attended
            merged = (
                residual_ref[:, columns].astype(jnp.float32) + attended.astype(jnp.float32)
            ).astype(jnp.bfloat16)
            merged_ref[:, columns] = merged
            wide = merged.astype(jnp.float32)
            square = square + wide * wide
        mean = jnp.sum(square, axis=1, keepdims=True) * (1.0 / model_dim)
        inverse = lax.rsqrt(mean + epsilon)
        normed_ref[:, model_dim:] = routing_columns(ids_ref[...], gates_ref[...])
        normed_ref[:, :model_dim] = (
            merged_ref[...].astype(jnp.float32) * inverse * gain_ref[...]
        ).astype(jnp.bfloat16)

    shape = jax.ShapeDtypeStruct((requests, model_dim), jnp.bfloat16)
    return pl.pallas_call(
        kernel,
        out_shape=(shape, shape, jax.ShapeDtypeStruct((requests, model_dim + 128), jnp.bfloat16)),
        in_specs=[VMEM] * 3 + [SMEM] + [VMEM] * 7,
        out_specs=(VMEM,) * 3,
        scratch_shapes=[pltpu.VMEM((rows, 128), jnp.float32)],
        compiler_params=pltpu.CompilerParams(vmem_limit_bytes=16 * MEBI),
        cost_estimate=pl.CostEstimate(
            flops=4 * rows * half * tokens, bytes_accessed=4 * MEBI, transcendentals=rows * tokens
        ),
        name="finish_attention",
    )(query, fetched, table, lengths, *partial, residual, gain, ids, gates)


def local(
    queries,
    new_kv,
    kv_pages,
    page_table,
    lengths,
    shed_slots,
    residual,
    norm_gain,
    expert_ids,
    gate_weights,
    w_gate_up,
    w_down,
):
    count_of_rows, model_dim = queries.shape
    top_count = expert_ids.shape[1]
    layout = Layout(lax.axis_size("pool"), lax.axis_size("dev"))
    capacity = 2 * count_of_rows * top_count // (layout.pool * layout.dev)
    planes = layout.planes

    requested = from_behind(shed_slots, "pool", 1)
    picked = pick_pages(requested, kv_pages)
    fetched = from_behind(picked, "pool", 1)
    queries, expert_ids, picked = lax.optimization_barrier((queries, expert_ids, picked))

    expert = (lax.axis_index("pool") * layout.dev + lax.axis_index("dev")).reshape(1)
    *partial, query = own_attention(queries, new_kv, kv_pages, page_table, lengths)
    attended, merged, normed = finish_attention(
        query,
        fetched,
        page_table,
        lengths,
        partial,
        residual,
        norm_gain.reshape(1, model_dim),
        expert_ids.T,
        gate_weights.T,
        kv_pages.shape[0],
    )

    first = max(1, planes // 4)
    groups = [range(0, first), range(first, 2 * first), range(2 * first, planes)]
    chips = range(0, layout.members, 2)
    blocks = [layout.shifted(normed, s) for s in range(planes)]
    arrived = []
    for g, group in enumerate(groups):
        rows = packed([blocks[s] for s in group])
        sent = []
        for c, chip in enumerate(chips):
            ready = rows
            if g == 1:
                ready = after(rows, arrived[0][c])
            sent.append(layout.swapped(ready, chip))
        arrived.append(sent)
    arrived[0][0] = after(arrived[0][0], arrived[2][0])

    def to_experts(members, tie):
        pieces = [arrived[g][c] for c in range(len(chips)) for g in members]
        if tie is not None:
            pieces[0] = after(pieces[0], tie)
        own = packed(pieces)
        slots = layout.members * sum(len(groups[g]) for g in members) * capacity
        return own, layout.swapped(own, 1), slots

    def add_cores(mine, over):
        back = layout.swapped(over, 1)
        cuts = [count_of_rows] * (mine.shape[0] // count_of_rows)
        return add_up([[mine], [back]], cuts, "add_cores")

    def to_owners(sums, i):
        pieces = len(sums) // len(chips)
        return [layout.swapped(sums[c * pieces + i], chip) for c, chip in enumerate(chips)]

    def total_of(parts):
        return add_up([[part] for part in parts], [count_of_rows], "add_chips")[0]

    near = [s for g in (0, 1) for s in groups[g]]
    own, other, slots = to_experts((0, 1), None)
    mine, over, kept = run_experts(own, other, (w_gate_up, w_down), expert, top_count, slots, True)
    far_own, far_other, slots = to_experts((2,), over)
    near_sums = list(add_cores(mine, over))
    far_other = after(far_other, near_sums[0])
    mine, over, _ = run_experts(far_own, far_other, kept, expert, top_count, slots, False)
    early = [to_owners(near_sums, i) for i in range(1, len(near))]
    over = after(over, *[part for parts in early for part in parts[1:]])
    far_sums = add_cores(mine, over)
    totals = {s: total_of(to_owners(far_sums, i)) for i, s in enumerate(groups[2])}
    totals.update({s: total_of(parts) for s, parts in zip(near[1:], early)})
    pieces = len(near_sums) // len(chips)
    for c in range(len(chips)):
        near_sums[c * pieces] = after(near_sums[c * pieces], totals[groups[2][-1]])
    totals[near[0]] = total_of(to_owners(near_sums, 0))
    others = [layout.shifted(total, s) for s, total in totals.items()]
    total = merged.astype(jnp.float32) + sum(part.astype(jnp.float32) for part in others)
    layer_out = total.astype(jnp.bfloat16)
    return (attended, layer_out)


def solution(mesh):
    return jax.shard_map(
        local,
        mesh=mesh,
        in_specs=(
            P(("pool", "dev"), None),
            P(("pool", "dev"), None),
            P(("pool", "dev"), None, None),
            P(("pool", "dev"), None),
            P(("pool", "dev")),
            P(("pool", "dev")),
            P(("pool", "dev"), None),
            P(),
            P(("pool", "dev"), None),
            P(("pool", "dev"), None),
            P(("pool", "dev"), None, None),
            P(("pool", "dev"), None, None),
        ),
        out_specs=(P(("pool", "dev"), None), P(("pool", "dev"), None)),
        check_vma=False,
    )
```

```python
import math

import jax
import jax.numpy as jnp
from jax import lax
from jax.experimental import pallas as pl
from jax.experimental.pallas import tpu as pltpu
from jax.sharding import PartitionSpec as P

HEAD_DIMENSION = 128
KEY_VALUE_HEADS = 2
QUERY_GROUP_SIZE = 16
HEADS = KEY_VALUE_HEADS * QUERY_GROUP_SIZE

masked_score = -1e30
epsilon = 1e-06
AXES = ("pool", "dev")
VMEM = pl.BlockSpec(memory_space=pltpu.VMEM)
SMEM = pl.BlockSpec(memory_space=pltpu.SMEM)
HBM = pl.BlockSpec(memory_space=pltpu.HBM)
MEBI = 1 << 20
EXPERT_LIMIT = 16 * MEBI


def in_hbm(value):
    return pltpu.with_memory_space_constraint(value, pltpu.HBM)


class Layout:
    def __init__(self, pool, dev):
        self.pool, self.dev = pool, dev
        self.inner = math.gcd(dev, 4)
        self.planes = dev // self.inner
        self.members = pool * self.inner
        self.groups = [
            [self.linear(member, plane) for member in range(self.members)]
            for plane in range(self.planes)
        ]

    def linear(self, member, plane):
        return member // self.inner * self.dev + plane * self.inner + member % self.inner

    def shifted(self, value, by):
        if by == 0:
            return value
        pairs = [
            (self.linear(m, z), self.linear(m, z ^ by))
            for z in range(self.planes)
            for m in range(self.members)
        ]
        with jax.named_scope(f"plane_{by}"):
            return lax.ppermute(value, AXES, pairs)

    def swapped(self, value, by):
        if by == 0:
            return value
        pairs = [
            (self.linear(m, z), self.linear(m ^ by, z))
            for z in range(self.planes)
            for m in range(self.members)
        ]
        with jax.named_scope(f"member_{by}"):
            return lax.ppermute(value, AXES, pairs)


def from_behind(value, axis, by):
    length = lax.axis_size(axis)
    return lax.ppermute(value, axis, [(i, (i + by) % length) for i in range(length)])


def pick_pages(slots, pages):
    count = slots.shape[0]
    last = pages.shape[0] - 1

    def kernel(slots_ref, pages_ref, out_ref, sems):
        copies = []
        for i in range(count):
            page = jnp.clip(slots_ref[i], 0, last)
            copies.append(pltpu.make_async_copy(pages_ref.at[page], out_ref.at[i], sems.at[i]))
            copies[-1].start()
        for copy in copies:
            copy.wait()

    return pl.pallas_call(
        kernel,
        out_shape=jax.ShapeDtypeStruct((count,) + pages.shape[1:], pages.dtype),
        in_specs=[SMEM, HBM],
        out_specs=VMEM,
        scratch_shapes=[pltpu.SemaphoreType.DMA((count,))],
        compiler_params=pltpu.CompilerParams(vmem_limit_bytes=4 * MEBI),
        cost_estimate=pl.CostEstimate(flops=0, bytes_accessed=MEBI, transcendentals=0),
        name="pick_pages",
    )(slots, in_hbm(pages))


def head_blocks(query):
    rows = query.shape[0]
    head = lax.broadcasted_iota(jnp.int32, (rows, HEAD_DIMENSION), 0) % HEADS
    nothing = jnp.zeros_like(query)
    low = head < QUERY_GROUP_SIZE
    return jnp.concatenate([jnp.where(low, query, nothing), jnp.where(low, nothing, query)], axis=1)


def own_head(both):
    rows = both.shape[0]
    head = lax.broadcasted_iota(jnp.int32, (rows, HEAD_DIMENSION), 0) % HEADS
    return jnp.where(
        head < QUERY_GROUP_SIZE, both[:, :HEAD_DIMENSION], both[:, HEAD_DIMENSION:]
    )


def tokens_of_pages(table, lengths_ref, first, page_len):
    count_of_rows, width = table.shape
    page = lax.broadcasted_iota(jnp.int32, (count_of_rows, 128), 1) + first
    row = lax.broadcasted_iota(jnp.int32, (count_of_rows, 128), 0)
    lengths = jnp.zeros((count_of_rows, 128), jnp.int32)
    for r in range(count_of_rows):
        lengths = jnp.where(row == r, lengths_ref[r], lengths)
    held = jnp.zeros((count_of_rows, 128), jnp.float32)
    for p in range(width):
        filled = jnp.clip(lengths - p * page_len, 0, page_len).astype(jnp.float32)
        held = held + jnp.where(table[:, p : p + 1] == page, filled, 0.0)
    return held


def token_bias(held, first_page, tokens, page_len):
    page = lax.broadcasted_iota(jnp.int32, (128, tokens), 0)
    token = lax.broadcasted_iota(jnp.int32, (128, tokens), 1)
    widen = (page == token // page_len + first_page).astype(jnp.bfloat16)
    limit = jnp.dot(held.astype(jnp.bfloat16), widen, preferred_element_type=jnp.float32)
    inside = (token[: held.shape[0]] % page_len).astype(jnp.float32)
    return jnp.where(inside < limit, 0.0, masked_score)


def masked_scores(blocks, keys, bias, scaling):
    scores = lax.dot_general(
        blocks, keys, (((1,), (1,)), ((), ())), preferred_element_type=jnp.float32
    )
    requests, tokens = bias.shape
    return (
        (scores * scaling).reshape(requests, HEADS, tokens) + bias[:, None, :]
    ).reshape(requests * HEADS, tokens)


def narrowed(value, join):
    result = value[:, :128]
    for start in range(128, value.shape[1], 128):
        result = join(result, value[:, start : start + 128])
    return result


def own_attention(queries, new_kv, pages, table, lengths):
    page_count, page_len, kv_width = pages.shape
    requests = new_kv.shape[0]
    rows = requests * HEADS
    half = kv_width // 2
    chunk_pages = 128 * (page_count // 128) // 4
    chunk = chunk_pages * page_len
    chunks = page_count // chunk_pages
    scaling = 1.0 / math.sqrt(HEAD_DIMENSION)

    def kernel(
        queries_hbm,
        new_hbm,
        pages_hbm,
        table_hbm,
        lengths_hbm,
        out_ref,
        top_ref,
        sum_ref,
        query_ref,
        s_ref,
        fresh_ref,
        heads_ref,
        flat_ref,
        pages_ref,
        table_ref,
        lengths_ref,
        sems,
    ):
        page_copies = [
            pltpu.make_async_copy(
                pages_hbm.at[pl.ds(c * chunk_pages, chunk_pages)],
                pages_ref.at[pl.ds(c * chunk_pages, chunk_pages)],
                sems.at[4 + c],
            )
            for c in range(chunks)
        ]
        copies = [
            pltpu.make_async_copy(queries_hbm, flat_ref, sems.at[0]),
            pltpu.make_async_copy(table_hbm, table_ref, sems.at[1]),
            pltpu.make_async_copy(lengths_hbm, lengths_ref, sems.at[2]),
            pltpu.make_async_copy(new_hbm, fresh_ref.at[pl.ds(0, requests)], sems.at[3]),
        ]
        fresh_ref[requests:] = jnp.zeros_like(fresh_ref[requests:])
        for copy in copies + page_copies:
            copy.start()
        for copy in copies:
            copy.wait()
        for h in range(HEADS):
            heads_ref[pl.ds(h, requests, stride=HEADS), :] = flat_ref[
                :, h * 128 : (h + 1) * 128
            ].astype(jnp.float32)
        query = heads_ref[...].astype(jnp.bfloat16)
        query_ref[...] = query
        blocks = head_blocks(query)
        held = tokens_of_pages(table_ref[...], lengths_ref, 0, page_len)
        lane = lax.broadcasted_iota(jnp.int32, (requests, 128), 1)
        own = lax.broadcasted_iota(jnp.int32, (requests, 128), 0)
        fresh_bias = jnp.where(lane == own, 0.0, masked_score)
        fresh = masked_scores(blocks, fresh_ref[:, :half], fresh_bias, scaling)
        s_ref[:, chunks * chunk :] = fresh
        top = fresh
        for c in range(chunks):
            page_copies[c].wait()
            keys = pages_ref[c * chunk_pages : (c + 1) * chunk_pages, :, :half].reshape(chunk, half)
            bias = token_bias(held, c * chunk_pages, chunk, page_len)
            scores = masked_scores(blocks, keys, bias, scaling)
            s_ref[:, c * chunk : (c + 1) * chunk] = scores
            top = jnp.maximum(top, narrowed(scores, jnp.maximum))
        top = jnp.max(top, axis=1, keepdims=True)
        weights = jnp.exp(s_ref[:, chunks * chunk :] - top)
        total = weights
        summed = jnp.dot(
            weights.astype(jnp.bfloat16), fresh_ref[:, half:], preferred_element_type=jnp.float32
        )
        for c in range(chunks):
            values = pages_ref[c * chunk_pages : (c + 1) * chunk_pages, :, half:].reshape(chunk, half)
            weights = jnp.exp(s_ref[:, c * chunk : (c + 1) * chunk] - top)
            total = total + narrowed(weights, jnp.add)
            summed = summed + jnp.dot(
                weights.astype(jnp.bfloat16), values, preferred_element_type=jnp.float32
            )
        out_ref[...] = own_head(summed)
        top_ref[...] = jnp.broadcast_to(top, top_ref.shape)
        sum_ref[...] = jnp.broadcast_to(jnp.sum(total, axis=1, keepdims=True), sum_ref.shape)

    shape = jax.ShapeDtypeStruct((rows, 128), jnp.float32)
    return pl.pallas_call(
        kernel,
        out_shape=(shape, shape, shape, jax.ShapeDtypeStruct((rows, 128), jnp.bfloat16)),
        in_specs=[HBM] * 5,
        out_specs=(VMEM,) * 4,
        scratch_shapes=[
            pltpu.VMEM((rows, chunks * chunk + 128), jnp.float32),
            pltpu.VMEM((128, kv_width), jnp.bfloat16),
            pltpu.VMEM((rows, 128), jnp.float32),
            pltpu.VMEM(queries.shape, jnp.bfloat16),
            pltpu.VMEM(pages.shape, jnp.bfloat16),
            pltpu.VMEM(table.shape, jnp.int32),
            pltpu.SMEM(lengths.shape, jnp.int32),
            pltpu.SemaphoreType.DMA((4 + chunks,)),
        ],
        compiler_params=pltpu.CompilerParams(vmem_limit_bytes=24 * MEBI),
        cost_estimate=pl.CostEstimate(
            flops=4 * rows * half * chunks * chunk,
            bytes_accessed=16 * MEBI,
            transcendentals=rows * chunks * chunk,
        ),
        name="own_attention",
    )(*[in_hbm(value) for value in (queries, new_kv, pages, table, lengths)])


def routing_columns(ids, gates):
    top_count = ids.shape[0]
    high = gates.astype(jnp.bfloat16)
    rest = gates - high.astype(jnp.float32)
    middle = rest.astype(jnp.bfloat16)
    low = (rest - middle.astype(jnp.float32)).astype(jnp.bfloat16)
    source = lax.broadcasted_iota(jnp.int32, (top_count, 128), 0)
    lane = lax.broadcasted_iota(jnp.int32, (top_count, 128), 1)
    columns = 0.0
    for i, part in enumerate((ids.astype(jnp.float32).astype(jnp.bfloat16), high, middle, low)):
        place = (lane == source + i * top_count).astype(jnp.bfloat16)
        columns = columns + lax.dot_general(
            part, place, (((0,), (0,)), ((), ())), preferred_element_type=jnp.float32
        )
    return columns.astype(jnp.bfloat16)


def stacked(parts):
    if len(parts) == 1:
        return parts[0]
    return jnp.concatenate(parts, axis=0)


def packed(parts, work=0):
    if len(parts) == 1 and not work:
        return parts[0]
    rows = sum(part.shape[0] for part in parts)
    columns = parts[0].shape[1]

    def kernel(*refs):
        out_ref, offset = refs[-1], 0
        for ref in refs[:-1]:
            out_ref[offset : offset + ref.shape[0]] = ref[...]
            offset += ref.shape[0]

    return pl.pallas_call(
        kernel,
        out_shape=jax.ShapeDtypeStruct((rows, columns), parts[0].dtype),
        in_specs=[VMEM] * len(parts),
        out_specs=VMEM,
        compiler_params=pltpu.CompilerParams(vmem_limit_bytes=12 * MEBI),
        cost_estimate=pl.CostEstimate(flops=work, bytes_accessed=0, transcendentals=0),
        name="packed",
    )(*parts)


def after(value, *others):
    return lax.optimization_barrier((value, *others))[0]


def run_experts(own, other, weights, expert, top_count, slots, keep):
    rows, model_dim = own.shape
    rows, model_dim = 2 * rows, model_dim - 128
    gate_up, down_proj = weights
    double, hidden_dim = gate_up.shape[-1], down_proj.shape[-2]
    width = 256
    up_steps = hidden_dim // width
    out_width = 1024 if rows <= 512 else 512
    out_steps = model_dim // out_width
    strip = 256

    def kernel(expert_ref, own_ref, other_ref, *refs):
        copies = {}
        if keep:
            up_hbm, down_hbm, out_ref, over_ref, up_ref, down_ref, tokens_ref, hidden_ref, sems = refs
            for c in range(up_steps):
                for half in range(2):
                    columns = pl.ds(half * hidden_dim + c * width, width)
                    copies["up", c, half] = pltpu.make_async_copy(
                        up_hbm.at[0, :, columns], up_ref.at[:, columns], sems.at[2 * c + half]
                    )
            for c in range(out_steps):
                columns = pl.ds(c * out_width, out_width)
                copies["down", c] = pltpu.make_async_copy(
                    down_hbm.at[0, :, columns], down_ref.at[:, columns], sems.at[2 * up_steps + c]
                )
            for copy in copies.values():
                copy.start()
        else:
            up_ref, down_ref, out_ref, over_ref, tokens_ref, hidden_ref = refs

        def arrive(*name):
            if keep:
                copies[name].wait()

        token_refs = [own_ref, other_ref]
        routing = stacked([ref[:, model_dim:] for ref in token_refs]).astype(jnp.float32)
        wanted = expert_ref[0].astype(jnp.float32)
        match = jnp.zeros((rows, 1), jnp.float32)
        gates = [jnp.zeros((rows, 1), jnp.float32)] * 3
        for k in range(top_count):
            hit = routing[:, k : k + 1] == wanted
            match = jnp.where(hit, 1.0, match)
            gates = [
                jnp.where(hit, routing[:, i * top_count + k : i * top_count + k + 1], gate)
                for i, gate in enumerate(gates, 1)
            ]
        lane = lax.broadcasted_iota(jnp.int32, (rows, slots), 1)
        match = jnp.broadcast_to(match, (rows, slots))
        earlier = (
            lax.broadcasted_iota(jnp.int32, (strip, strip), 0)
            > lax.broadcasted_iota(jnp.int32, (strip, strip), 1)
        ).astype(jnp.bfloat16)
        ranks, before = [], jnp.zeros((1, slots), jnp.float32)
        for start in range(0, rows, strip):
            piece = match[start : start + strip]
            ranks.append(
                before
                + jnp.dot(earlier, piece.astype(jnp.bfloat16), preferred_element_type=jnp.float32)
            )
            before = before + jnp.sum(piece, axis=0, keepdims=True)
        rank = stacked(ranks)
        choice = jnp.where(rank == lane.astype(jnp.float32), match, 0.0)
        pick = choice.T.astype(jnp.bfloat16)
        place = choice.astype(jnp.bfloat16)
        gate_columns = jnp.where(
            lane == 0, gates[0], jnp.where(lane == 1, gates[1], jnp.where(lane == 2, gates[2], 0.0))
        ).astype(jnp.bfloat16)
        gate = jnp.sum(
            jnp.dot(pick, gate_columns, preferred_element_type=jnp.float32), axis=1, keepdims=True
        )
        for start in range(0, model_dim, out_width):
            columns = slice(start, start + out_width)
            tokens = stacked([ref[:, columns] for ref in token_refs])
            tokens_ref[:, columns] = jnp.dot(
                pick, tokens, preferred_element_type=jnp.float32
            ).astype(jnp.bfloat16)

        for c in range(up_steps):
            arrive("up", c, 0)
            arrive("up", c, 1)
            start = c * width
            tokens = tokens_ref[...]
            gated = jnp.dot(
                tokens, up_ref[:, start : start + width], preferred_element_type=jnp.float32
            )
            up = jnp.dot(
                tokens,
                up_ref[:, hidden_dim + start : hidden_dim + start + width],
                preferred_element_type=jnp.float32,
            )
            hidden_ref[:, start : start + width] = (gated / (1.0 + jnp.exp(-gated)) * up).astype(
                jnp.bfloat16
            )

        for c in range(out_steps):
            arrive("down", c)
            columns = slice(c * out_width, (c + 1) * out_width)
            result = jnp.dot(
                hidden_ref[...], down_ref[:, columns], preferred_element_type=jnp.float32
            )
            result = (result * gate).astype(jnp.bfloat16)
            sums = jnp.dot(place, result, preferred_element_type=jnp.float32).astype(jnp.bfloat16)
            out_ref[:, columns] = sums[: rows // 2]
            over_ref[:, columns] = sums[rows // 2 :]

    shape = jax.ShapeDtypeStruct((rows // 2, model_dim), jnp.bfloat16)
    kept, scratch = (), []
    if keep:
        kept = (
            pltpu.VMEM((model_dim, double), jnp.bfloat16),
            pltpu.VMEM((hidden_dim, model_dim), jnp.bfloat16),
        )
        scratch = [pltpu.SemaphoreType.DMA((2 * up_steps + out_steps,))]
        weights = [in_hbm(gate_up), in_hbm(down_proj)]
    else:
        weights = [pltpu.with_memory_space_constraint(value, pltpu.VMEM) for value in weights]
    results = pl.pallas_call(
        kernel,
        out_shape=(shape, shape) + kept,
        in_specs=[SMEM, VMEM, VMEM] + [HBM if keep else VMEM] * 2,
        out_specs=(VMEM,) * (2 + len(kept)),
        scratch_shapes=[
            pltpu.VMEM((slots, model_dim), jnp.bfloat16),
            pltpu.VMEM((slots, hidden_dim), jnp.bfloat16),
        ]
        + scratch,
        compiler_params=pltpu.CompilerParams(vmem_limit_bytes=EXPERT_LIMIT),
        cost_estimate=pl.CostEstimate(
            flops=6 * slots * model_dim * hidden_dim,
            bytes_accessed=20 * MEBI,
            transcendentals=slots * hidden_dim,
        ),
        name="run_experts",
    )(expert, own, other, *weights)
    return results[0], results[1], results[2:]


def add_up(parts, cuts, name, work=0):
    rows = sum(cuts)
    model_dim = parts[0][0].shape[1]
    flat = [piece for part in parts for piece in part]
    places = []
    for part in parts:
        start = 0
        for piece in part:
            places.append((start, start + piece.shape[0]))
            start += piece.shape[0]

    def kernel(*refs):
        in_refs, out_refs = refs[: len(flat)], refs[len(flat) :]
        step = 1024
        for start in range(0, model_dim, step):
            columns = slice(start, start + step)
            offset = 0
            for out_ref, cut in zip(out_refs, cuts):
                total = 0.0
                for ref, (low, high) in zip(in_refs, places):
                    if low <= offset and offset + cut <= high:
                        rows_of = slice(offset - low, offset - low + cut)
                        total = total + ref[rows_of, columns].astype(jnp.float32)
                out_ref[:, columns] = total.astype(jnp.bfloat16)
                offset += cut

    return pl.pallas_call(
        kernel,
        out_shape=tuple(jax.ShapeDtypeStruct((cut, model_dim), jnp.bfloat16) for cut in cuts),
        in_specs=[VMEM] * len(flat),
        out_specs=(VMEM,) * len(cuts),
        compiler_params=pltpu.CompilerParams(vmem_limit_bytes=12 * MEBI),
        cost_estimate=pl.CostEstimate(
            flops=work, bytes_accessed=0, transcendentals=0
        ),
        name=name,
    )(*flat)


def finish_attention(
    query, fetched, table, lengths, partial, residual, gain, ids, gates, pages_own
):
    count, page_len, kv_width = fetched.shape
    half = kv_width // 2
    tokens = count * page_len
    requests, model_dim = residual.shape
    rows = query.shape[0]
    scaling = 1.0 / math.sqrt(HEAD_DIMENSION)

    def kernel(q_ref, fetched_ref, table_ref, lengths_ref, sum_ref, top_ref, total_ref, residual_ref, gain_ref, ids_ref, gates_ref, attended_ref, merged_ref, normed_ref, heads_ref):
        blocks = head_blocks(q_ref[...])
        held = tokens_of_pages(table_ref[...], lengths_ref, pages_own, page_len)
        bias = token_bias(held, 0, tokens, page_len)
        keys = fetched_ref[:, :, :half].reshape(tokens, half)
        values = fetched_ref[:, :, half:].reshape(tokens, half)
        scores = masked_scores(blocks, keys, bias, scaling)
        before = top_ref[...]
        shed_top = jnp.max(narrowed(scores, jnp.maximum), axis=1, keepdims=True)
        top = jnp.maximum(before, shed_top)
        kept = jnp.exp(before - top)
        weights = jnp.exp(scores - jnp.concatenate([top] * (tokens // 128), axis=1))
        added = jnp.sum(narrowed(weights, jnp.add), axis=1, keepdims=True)
        total = total_ref[...] * kept + added
        summed = own_head(
            jnp.dot(weights.astype(jnp.bfloat16), values, preferred_element_type=jnp.float32)
        )
        heads_ref[...] = (sum_ref[...] * kept + summed) / total
        square = jnp.zeros((requests, 128), jnp.float32)
        for h in range(HEADS):
            columns = slice(h * 128, (h + 1) * 128)
            attended = heads_ref[pl.ds(h, requests, stride=HEADS), :].astype(jnp.bfloat16)
            attended_ref[:, columns] = attended
            merged = (
                residual_ref[:, columns].astype(jnp.float32) + attended.astype(jnp.float32)
            ).astype(jnp.bfloat16)
            merged_ref[:, columns] = merged
            wide = merged.astype(jnp.float32)
            square = square + wide * wide
        mean = jnp.sum(square, axis=1, keepdims=True) * (1.0 / model_dim)
        inverse = lax.rsqrt(mean + epsilon)
        normed_ref[:, model_dim:] = routing_columns(ids_ref[...], gates_ref[...])
        normed_ref[:, :model_dim] = (
            merged_ref[...].astype(jnp.float32) * inverse * gain_ref[...]
        ).astype(jnp.bfloat16)

    shape = jax.ShapeDtypeStruct((requests, model_dim), jnp.bfloat16)
    return pl.pallas_call(
        kernel,
        out_shape=(shape, shape, jax.ShapeDtypeStruct((requests, model_dim + 128), jnp.bfloat16)),
        in_specs=[VMEM] * 3 + [SMEM] + [VMEM] * 7,
        out_specs=(VMEM,) * 3,
        scratch_shapes=[pltpu.VMEM((rows, 128), jnp.float32)],
        compiler_params=pltpu.CompilerParams(vmem_limit_bytes=16 * MEBI),
        cost_estimate=pl.CostEstimate(
            flops=4 * rows * half * tokens, bytes_accessed=4 * MEBI, transcendentals=rows * tokens
        ),
        name="finish_attention",
    )(query, fetched, table, lengths, *partial, residual, gain, ids, gates)


def local(
    queries,
    new_kv,
    kv_pages,
    page_table,
    lengths,
    shed_slots,
    residual,
    norm_gain,
    expert_ids,
    gate_weights,
    w_gate_up,
    w_down,
):
    count_of_rows, model_dim = queries.shape
    top_count = expert_ids.shape[1]
    layout = Layout(lax.axis_size("pool"), lax.axis_size("dev"))
    capacity = 2 * count_of_rows * top_count // (layout.pool * layout.dev)
    planes = layout.planes

    requested = from_behind(shed_slots, "pool", 1)
    picked = pick_pages(requested, kv_pages)
    fetched = from_behind(picked, "pool", 1)
    queries, expert_ids, picked = lax.optimization_barrier((queries, expert_ids, picked))

    expert = (lax.axis_index("pool") * layout.dev + lax.axis_index("dev")).reshape(1)
    *partial, query = own_attention(queries, new_kv, kv_pages, page_table, lengths)
    attended, merged, normed = finish_attention(
        query,
        fetched,
        page_table,
        lengths,
        partial,
        residual,
        norm_gain.reshape(1, model_dim),
        expert_ids.T,
        gate_weights.T,
        kv_pages.shape[0],
    )

    first = max(1, planes // 4)
    order = sorted(range(planes), key=lambda s: (s & 1, s))
    groups = [order[:first], order[first : 2 * first], order[2 * first :]]
    chips = range(0, layout.members, 2)
    blocks = [layout.shifted(normed, s) for s in range(planes)]
    arrived = []
    for g, group in enumerate(groups):
        rows = packed([blocks[s] for s in group])
        sent = []
        for c, chip in enumerate(chips):
            ready = rows
            if g == 1:
                ready = after(rows, arrived[0][c])
            sent.append(layout.swapped(ready, chip))
        arrived.append(sent)
    arrived[0][0] = after(arrived[0][0], arrived[2][0])

    def to_experts(members, tie):
        pieces = [arrived[g][c] for c in range(len(chips)) for g in members]
        if tie is not None:
            pieces[0] = after(pieces[0], tie)
        own = packed(pieces)
        slots = layout.members * sum(len(groups[g]) for g in members) * capacity
        return own, layout.swapped(own, 1), slots

    def add_cores(mine, over):
        cuts = [count_of_rows] * (mine.shape[0] // count_of_rows)
        return list(add_up([[mine], [over]], cuts, "add_cores"))

    def to_owners(sums, i):
        pieces = len(sums) // len(chips)
        return [layout.swapped(sums[c * pieces + i], chip) for c, chip in enumerate(chips)]

    def total_of(parts):
        return add_up([[part] for part in parts], [count_of_rows], "add_chips")[0]

    near = [s for g in (0, 1) for s in groups[g]]
    own, other, slots = to_experts((0, 1), None)
    mine, over, kept = run_experts(own, other, (w_gate_up, w_down), expert, top_count, slots, True)
    near_mine, near_back = mine, layout.swapped(over, 1)
    far_own, far_other, slots = to_experts((2,), over)
    far_other = after(far_other, near_back)
    mine, over, _ = run_experts(far_own, far_other, kept, expert, top_count, slots, False)
    near_sums = add_up(
        [[near_mine], [near_back]], [count_of_rows * len(near)] * len(chips), "add_cores"
    )
    far_sums = add_cores(mine, layout.swapped(over, 1))
    parts = to_owners(near_sums, 0)
    totals = add_up([[part] for part in parts], [count_of_rows] * len(near), "add_chips")
    others = [layout.shifted(total, by) for total, by in zip(totals, near)]
    for i, by in list(enumerate(groups[2]))[::-1]:
        others.append(layout.shifted(total_of(to_owners(far_sums, i)), by))
    count = len(near) + 1
    merged = add_up(
        [[merged]] + [[part] for part in others[:count]], [count_of_rows], "add_first", 10**10
    )[0]
    others = others[count:]
    total = merged.astype(jnp.float32) + sum(part.astype(jnp.float32) for part in others)
    layer_out = total.astype(jnp.bfloat16)
    return (attended, layer_out)


def solution(mesh):
    return jax.shard_map(
        local,
        mesh=mesh,
        in_specs=(
            P(("pool", "dev"), None),
            P(("pool", "dev"), None),
            P(("pool", "dev"), None, None),
            P(("pool", "dev"), None),
            P(("pool", "dev")),
            P(("pool", "dev")),
            P(("pool", "dev"), None),
            P(),
            P(("pool", "dev"), None),
            P(("pool", "dev"), None),
            P(("pool", "dev"), None, None),
            P(("pool", "dev"), None, None),
        ),
        out_specs=(P(("pool", "dev"), None), P(("pool", "dev"), None)),
        check_vma=False,
    )
```

```python
import math

import jax
import jax.numpy as jnp
from jax import lax
from jax.experimental import pallas as pl
from jax.experimental.pallas import tpu as pltpu
from jax.sharding import PartitionSpec as P

HEAD_DIMENSION = 128
KEY_VALUE_HEADS = 2
QUERY_GROUP_SIZE = 16
HEADS = KEY_VALUE_HEADS * QUERY_GROUP_SIZE

masked_score = -1e30
epsilon = 1e-06
AXES = ("pool", "dev")
VMEM = pl.BlockSpec(memory_space=pltpu.VMEM)
SMEM = pl.BlockSpec(memory_space=pltpu.SMEM)
HBM = pl.BlockSpec(memory_space=pltpu.HBM)
MEBI = 1 << 20
EXPERT_LIMIT = 16 * MEBI


def in_hbm(value):
    return pltpu.with_memory_space_constraint(value, pltpu.HBM)


class Layout:
    def __init__(self, pool, dev):
        self.pool, self.dev = pool, dev
        self.inner = math.gcd(dev, 4)
        self.planes = dev // self.inner
        self.members = pool * self.inner
        self.groups = [
            [self.linear(member, plane) for member in range(self.members)]
            for plane in range(self.planes)
        ]

    def linear(self, member, plane):
        return member // self.inner * self.dev + plane * self.inner + member % self.inner

    def shifted(self, value, by):
        if by == 0:
            return value
        pairs = [
            (self.linear(m, z), self.linear(m, z ^ by))
            for z in range(self.planes)
            for m in range(self.members)
        ]
        with jax.named_scope(f"plane_{by}"):
            return lax.ppermute(value, AXES, pairs)

    def swapped(self, value, by):
        if by == 0:
            return value
        pairs = [
            (self.linear(m, z), self.linear(m ^ by, z))
            for z in range(self.planes)
            for m in range(self.members)
        ]
        with jax.named_scope(f"member_{by}"):
            return lax.ppermute(value, AXES, pairs)


def from_behind(value, axis, by):
    length = lax.axis_size(axis)
    return lax.ppermute(value, axis, [(i, (i + by) % length) for i in range(length)])


def pick_pages(slots, pages):
    count = slots.shape[0]
    last = pages.shape[0] - 1

    def kernel(slots_ref, pages_ref, out_ref, sems):
        copies = []
        for i in range(count):
            page = jnp.clip(slots_ref[i], 0, last)
            copies.append(pltpu.make_async_copy(pages_ref.at[page], out_ref.at[i], sems.at[i]))
            copies[-1].start()
        for copy in copies:
            copy.wait()

    return pl.pallas_call(
        kernel,
        out_shape=jax.ShapeDtypeStruct((count,) + pages.shape[1:], pages.dtype),
        in_specs=[SMEM, HBM],
        out_specs=VMEM,
        scratch_shapes=[pltpu.SemaphoreType.DMA((count,))],
        compiler_params=pltpu.CompilerParams(vmem_limit_bytes=4 * MEBI),
        cost_estimate=pl.CostEstimate(flops=0, bytes_accessed=MEBI, transcendentals=0),
        name="pick_pages",
    )(slots, in_hbm(pages))


def head_blocks(query):
    rows = query.shape[0]
    head = lax.broadcasted_iota(jnp.int32, (rows, HEAD_DIMENSION), 0) % HEADS
    nothing = jnp.zeros_like(query)
    low = head < QUERY_GROUP_SIZE
    return jnp.concatenate([jnp.where(low, query, nothing), jnp.where(low, nothing, query)], axis=1)


def own_head(both):
    rows = both.shape[0]
    head = lax.broadcasted_iota(jnp.int32, (rows, HEAD_DIMENSION), 0) % HEADS
    return jnp.where(
        head < QUERY_GROUP_SIZE, both[:, :HEAD_DIMENSION], both[:, HEAD_DIMENSION:]
    )


def tokens_of_pages(table, lengths_ref, first, page_len):
    count_of_rows, width = table.shape
    page = lax.broadcasted_iota(jnp.int32, (count_of_rows, 128), 1) + first
    row = lax.broadcasted_iota(jnp.int32, (count_of_rows, 128), 0)
    lengths = jnp.zeros((count_of_rows, 128), jnp.int32)
    for r in range(count_of_rows):
        lengths = jnp.where(row == r, lengths_ref[r], lengths)
    held = jnp.zeros((count_of_rows, 128), jnp.float32)
    for p in range(width):
        filled = jnp.clip(lengths - p * page_len, 0, page_len).astype(jnp.float32)
        held = held + jnp.where(table[:, p : p + 1] == page, filled, 0.0)
    return held


def token_bias(held, first_page, tokens, page_len):
    page = lax.broadcasted_iota(jnp.int32, (128, tokens), 0)
    token = lax.broadcasted_iota(jnp.int32, (128, tokens), 1)
    widen = (page == token // page_len + first_page).astype(jnp.bfloat16)
    limit = jnp.dot(held.astype(jnp.bfloat16), widen, preferred_element_type=jnp.float32)
    inside = (token[: held.shape[0]] % page_len).astype(jnp.float32)
    return jnp.where(inside < limit, 0.0, masked_score)


def masked_scores(blocks, keys, bias, scaling):
    scores = lax.dot_general(
        blocks, keys, (((1,), (1,)), ((), ())), preferred_element_type=jnp.float32
    )
    requests, tokens = bias.shape
    return (
        (scores * scaling).reshape(requests, HEADS, tokens) + bias[:, None, :]
    ).reshape(requests * HEADS, tokens)


def narrowed(value, join):
    result = value[:, :128]
    for start in range(128, value.shape[1], 128):
        result = join(result, value[:, start : start + 128])
    return result


def own_attention(queries, new_kv, pages, table, lengths):
    page_count, page_len, kv_width = pages.shape
    requests = new_kv.shape[0]
    rows = requests * HEADS
    half = kv_width // 2
    chunk_pages = 128 * (page_count // 128) // 4
    chunk = chunk_pages * page_len
    chunks = page_count // chunk_pages
    scaling = 1.0 / math.sqrt(HEAD_DIMENSION)

    def kernel(
        queries_hbm,
        new_hbm,
        pages_hbm,
        table_hbm,
        lengths_hbm,
        out_ref,
        top_ref,
        sum_ref,
        query_ref,
        s_ref,
        fresh_ref,
        heads_ref,
        flat_ref,
        pages_ref,
        table_ref,
        lengths_ref,
        sems,
    ):
        page_copies = [
            pltpu.make_async_copy(
                pages_hbm.at[pl.ds(c * chunk_pages, chunk_pages)],
                pages_ref.at[pl.ds(c * chunk_pages, chunk_pages)],
                sems.at[4 + c],
            )
            for c in range(chunks)
        ]
        copies = [
            pltpu.make_async_copy(queries_hbm, flat_ref, sems.at[0]),
            pltpu.make_async_copy(table_hbm, table_ref, sems.at[1]),
            pltpu.make_async_copy(lengths_hbm, lengths_ref, sems.at[2]),
            pltpu.make_async_copy(new_hbm, fresh_ref.at[pl.ds(0, requests)], sems.at[3]),
        ]
        fresh_ref[requests:] = jnp.zeros_like(fresh_ref[requests:])
        for copy in copies + page_copies:
            copy.start()
        for copy in copies:
            copy.wait()
        for h in range(HEADS):
            heads_ref[pl.ds(h, requests, stride=HEADS), :] = flat_ref[
                :, h * 128 : (h + 1) * 128
            ].astype(jnp.float32)
        query = heads_ref[...].astype(jnp.bfloat16)
        query_ref[...] = query
        blocks = head_blocks(query)
        held = tokens_of_pages(table_ref[...], lengths_ref, 0, page_len)
        lane = lax.broadcasted_iota(jnp.int32, (requests, 128), 1)
        own = lax.broadcasted_iota(jnp.int32, (requests, 128), 0)
        fresh_bias = jnp.where(lane == own, 0.0, masked_score)
        fresh = masked_scores(blocks, fresh_ref[:, :half], fresh_bias, scaling)
        s_ref[:, chunks * chunk :] = fresh
        top = fresh
        for c in range(chunks):
            page_copies[c].wait()
            keys = pages_ref[c * chunk_pages : (c + 1) * chunk_pages, :, :half].reshape(chunk, half)
            bias = token_bias(held, c * chunk_pages, chunk, page_len)
            scores = masked_scores(blocks, keys, bias, scaling)
            s_ref[:, c * chunk : (c + 1) * chunk] = scores
            top = jnp.maximum(top, narrowed(scores, jnp.maximum))
        top = jnp.max(top, axis=1, keepdims=True)
        weights = jnp.exp(s_ref[:, chunks * chunk :] - top)
        total = weights
        summed = jnp.dot(
            weights.astype(jnp.bfloat16), fresh_ref[:, half:], preferred_element_type=jnp.float32
        )
        for c in range(chunks):
            values = pages_ref[c * chunk_pages : (c + 1) * chunk_pages, :, half:].reshape(chunk, half)
            weights = jnp.exp(s_ref[:, c * chunk : (c + 1) * chunk] - top)
            total = total + narrowed(weights, jnp.add)
            summed = summed + jnp.dot(
                weights.astype(jnp.bfloat16), values, preferred_element_type=jnp.float32
            )
        out_ref[...] = own_head(summed)
        top_ref[...] = jnp.broadcast_to(top, top_ref.shape)
        sum_ref[...] = jnp.broadcast_to(jnp.sum(total, axis=1, keepdims=True), sum_ref.shape)

    shape = jax.ShapeDtypeStruct((rows, 128), jnp.float32)
    return pl.pallas_call(
        kernel,
        out_shape=(shape, shape, shape, jax.ShapeDtypeStruct((rows, 128), jnp.bfloat16)),
        in_specs=[HBM] * 5,
        out_specs=(VMEM,) * 4,
        scratch_shapes=[
            pltpu.VMEM((rows, chunks * chunk + 128), jnp.float32),
            pltpu.VMEM((128, kv_width), jnp.bfloat16),
            pltpu.VMEM((rows, 128), jnp.float32),
            pltpu.VMEM(queries.shape, jnp.bfloat16),
            pltpu.VMEM(pages.shape, jnp.bfloat16),
            pltpu.VMEM(table.shape, jnp.int32),
            pltpu.SMEM(lengths.shape, jnp.int32),
            pltpu.SemaphoreType.DMA((4 + chunks,)),
        ],
        compiler_params=pltpu.CompilerParams(vmem_limit_bytes=24 * MEBI),
        cost_estimate=pl.CostEstimate(
            flops=4 * rows * half * chunks * chunk,
            bytes_accessed=16 * MEBI,
            transcendentals=rows * chunks * chunk,
        ),
        name="own_attention",
    )(*[in_hbm(value) for value in (queries, new_kv, pages, table, lengths)])


def routing_columns(ids, gates):
    top_count = ids.shape[0]
    high = gates.astype(jnp.bfloat16)
    rest = gates - high.astype(jnp.float32)
    middle = rest.astype(jnp.bfloat16)
    low = (rest - middle.astype(jnp.float32)).astype(jnp.bfloat16)
    source = lax.broadcasted_iota(jnp.int32, (top_count, 128), 0)
    lane = lax.broadcasted_iota(jnp.int32, (top_count, 128), 1)
    columns = 0.0
    for i, part in enumerate((ids.astype(jnp.float32).astype(jnp.bfloat16), high, middle, low)):
        place = (lane == source + i * top_count).astype(jnp.bfloat16)
        columns = columns + lax.dot_general(
            part, place, (((0,), (0,)), ((), ())), preferred_element_type=jnp.float32
        )
    return columns.astype(jnp.bfloat16)


def stacked(parts):
    if len(parts) == 1:
        return parts[0]
    return jnp.concatenate(parts, axis=0)


def packed(parts, work=0):
    if len(parts) == 1 and not work:
        return parts[0]
    rows = sum(part.shape[0] for part in parts)
    columns = parts[0].shape[1]

    def kernel(*refs):
        out_ref, offset = refs[-1], 0
        for ref in refs[:-1]:
            out_ref[offset : offset + ref.shape[0]] = ref[...]
            offset += ref.shape[0]

    return pl.pallas_call(
        kernel,
        out_shape=jax.ShapeDtypeStruct((rows, columns), parts[0].dtype),
        in_specs=[VMEM] * len(parts),
        out_specs=VMEM,
        compiler_params=pltpu.CompilerParams(vmem_limit_bytes=12 * MEBI),
        cost_estimate=pl.CostEstimate(flops=work, bytes_accessed=0, transcendentals=0),
        name="packed",
    )(*parts)


def after(value, *others):
    return lax.optimization_barrier((value, *others))[0]


def run_experts(own, other, weights, expert, top_count, slots, keep):
    rows, model_dim = own.shape
    rows, model_dim = 2 * rows, model_dim - 128
    gate_up, down_proj = weights
    double, hidden_dim = gate_up.shape[-1], down_proj.shape[-2]
    width = 256
    up_steps = hidden_dim // width
    out_width = 1024 if rows <= 512 else 512
    out_steps = model_dim // out_width
    strip = 256

    def kernel(expert_ref, own_ref, other_ref, *refs):
        copies = {}
        if keep:
            up_hbm, down_hbm, out_ref, over_ref, up_ref, down_ref, tokens_ref, hidden_ref, sems = refs
            for c in range(up_steps):
                for half in range(2):
                    columns = pl.ds(half * hidden_dim + c * width, width)
                    copies["up", c, half] = pltpu.make_async_copy(
                        up_hbm.at[0, :, columns], up_ref.at[:, columns], sems.at[2 * c + half]
                    )
            for c in range(out_steps):
                columns = pl.ds(c * out_width, out_width)
                copies["down", c] = pltpu.make_async_copy(
                    down_hbm.at[0, :, columns], down_ref.at[:, columns], sems.at[2 * up_steps + c]
                )
            for copy in copies.values():
                copy.start()
        else:
            up_ref, down_ref, out_ref, over_ref, tokens_ref, hidden_ref = refs

        def arrive(*name):
            if keep:
                copies[name].wait()

        token_refs = [own_ref, other_ref]
        routing = stacked([ref[:, model_dim:] for ref in token_refs]).astype(jnp.float32)
        wanted = expert_ref[0].astype(jnp.float32)
        match = jnp.zeros((rows, 1), jnp.float32)
        gates = [jnp.zeros((rows, 1), jnp.float32)] * 3
        for k in range(top_count):
            hit = routing[:, k : k + 1] == wanted
            match = jnp.where(hit, 1.0, match)
            gates = [
                jnp.where(hit, routing[:, i * top_count + k : i * top_count + k + 1], gate)
                for i, gate in enumerate(gates, 1)
            ]
        lane = lax.broadcasted_iota(jnp.int32, (rows, slots), 1)
        match = jnp.broadcast_to(match, (rows, slots))
        earlier = (
            lax.broadcasted_iota(jnp.int32, (strip, strip), 0)
            > lax.broadcasted_iota(jnp.int32, (strip, strip), 1)
        ).astype(jnp.bfloat16)
        ranks, before = [], jnp.zeros((1, slots), jnp.float32)
        for start in range(0, rows, strip):
            piece = match[start : start + strip]
            ranks.append(
                before
                + jnp.dot(earlier, piece.astype(jnp.bfloat16), preferred_element_type=jnp.float32)
            )
            before = before + jnp.sum(piece, axis=0, keepdims=True)
        rank = stacked(ranks)
        choice = jnp.where(rank == lane.astype(jnp.float32), match, 0.0)
        pick = choice.T.astype(jnp.bfloat16)
        place = choice.astype(jnp.bfloat16)
        gate_columns = jnp.where(
            lane == 0, gates[0], jnp.where(lane == 1, gates[1], jnp.where(lane == 2, gates[2], 0.0))
        ).astype(jnp.bfloat16)
        gate = jnp.sum(
            jnp.dot(pick, gate_columns, preferred_element_type=jnp.float32), axis=1, keepdims=True
        )
        for start in range(0, model_dim, out_width):
            columns = slice(start, start + out_width)
            tokens = stacked([ref[:, columns] for ref in token_refs])
            tokens_ref[:, columns] = jnp.dot(
                pick, tokens, preferred_element_type=jnp.float32
            ).astype(jnp.bfloat16)

        for c in range(up_steps):
            arrive("up", c, 0)
            arrive("up", c, 1)
            start = c * width
            tokens = tokens_ref[...]
            gated = jnp.dot(
                tokens, up_ref[:, start : start + width], preferred_element_type=jnp.float32
            )
            up = jnp.dot(
                tokens,
                up_ref[:, hidden_dim + start : hidden_dim + start + width],
                preferred_element_type=jnp.float32,
            )
            hidden_ref[:, start : start + width] = (gated / (1.0 + jnp.exp(-gated)) * up).astype(
                jnp.bfloat16
            )

        for c in range(out_steps):
            arrive("down", c)
            columns = slice(c * out_width, (c + 1) * out_width)
            result = jnp.dot(
                hidden_ref[...], down_ref[:, columns], preferred_element_type=jnp.float32
            )
            result = (result * gate).astype(jnp.bfloat16)
            sums = jnp.dot(place, result, preferred_element_type=jnp.float32).astype(jnp.bfloat16)
            out_ref[:, columns] = sums[: rows // 2]
            over_ref[:, columns] = sums[rows // 2 :]

    shape = jax.ShapeDtypeStruct((rows // 2, model_dim), jnp.bfloat16)
    kept, scratch = (), []
    if keep:
        kept = (
            pltpu.VMEM((model_dim, double), jnp.bfloat16),
            pltpu.VMEM((hidden_dim, model_dim), jnp.bfloat16),
        )
        scratch = [pltpu.SemaphoreType.DMA((2 * up_steps + out_steps,))]
        weights = [in_hbm(gate_up), in_hbm(down_proj)]
    else:
        weights = [pltpu.with_memory_space_constraint(value, pltpu.VMEM) for value in weights]
    results = pl.pallas_call(
        kernel,
        out_shape=(shape, shape) + kept,
        in_specs=[SMEM, VMEM, VMEM] + [HBM if keep else VMEM] * 2,
        out_specs=(VMEM,) * (2 + len(kept)),
        scratch_shapes=[
            pltpu.VMEM((slots, model_dim), jnp.bfloat16),
            pltpu.VMEM((slots, hidden_dim), jnp.bfloat16),
        ]
        + scratch,
        compiler_params=pltpu.CompilerParams(vmem_limit_bytes=EXPERT_LIMIT),
        cost_estimate=pl.CostEstimate(
            flops=6 * slots * model_dim * hidden_dim,
            bytes_accessed=20 * MEBI,
            transcendentals=slots * hidden_dim,
        ),
        name="run_experts",
    )(expert, own, other, *weights)
    return results[0], results[1], results[2:]


def add_up(parts, cuts, name, work=0):
    rows = sum(cuts)
    model_dim = parts[0][0].shape[1]
    flat = [piece for part in parts for piece in part]
    places = []
    for part in parts:
        start = 0
        for piece in part:
            places.append((start, start + piece.shape[0]))
            start += piece.shape[0]

    def kernel(*refs):
        in_refs, out_refs = refs[: len(flat)], refs[len(flat) :]
        step = 1024
        for start in range(0, model_dim, step):
            columns = slice(start, start + step)
            offset = 0
            for out_ref, cut in zip(out_refs, cuts):
                total = 0.0
                for ref, (low, high) in zip(in_refs, places):
                    if low <= offset and offset + cut <= high:
                        rows_of = slice(offset - low, offset - low + cut)
                        total = total + ref[rows_of, columns].astype(jnp.float32)
                out_ref[:, columns] = total.astype(jnp.bfloat16)
                offset += cut

    return pl.pallas_call(
        kernel,
        out_shape=tuple(jax.ShapeDtypeStruct((cut, model_dim), jnp.bfloat16) for cut in cuts),
        in_specs=[VMEM] * len(flat),
        out_specs=(VMEM,) * len(cuts),
        compiler_params=pltpu.CompilerParams(vmem_limit_bytes=12 * MEBI),
        cost_estimate=pl.CostEstimate(
            flops=work, bytes_accessed=0, transcendentals=0
        ),
        name=name,
    )(*flat)


def finish_attention(
    query, fetched, table, lengths, partial, residual, gain, ids, gates, pages_own
):
    count, page_len, kv_width = fetched.shape
    half = kv_width // 2
    tokens = count * page_len
    requests, model_dim = residual.shape
    rows = query.shape[0]
    scaling = 1.0 / math.sqrt(HEAD_DIMENSION)

    def kernel(q_ref, fetched_ref, table_ref, lengths_ref, sum_ref, top_ref, total_ref, residual_ref, gain_ref, ids_ref, gates_ref, attended_ref, merged_ref, normed_ref, heads_ref):
        blocks = head_blocks(q_ref[...])
        held = tokens_of_pages(table_ref[...], lengths_ref, pages_own, page_len)
        bias = token_bias(held, 0, tokens, page_len)
        keys = fetched_ref[:, :, :half].reshape(tokens, half)
        values = fetched_ref[:, :, half:].reshape(tokens, half)
        scores = masked_scores(blocks, keys, bias, scaling)
        before = top_ref[...]
        shed_top = jnp.max(narrowed(scores, jnp.maximum), axis=1, keepdims=True)
        top = jnp.maximum(before, shed_top)
        kept = jnp.exp(before - top)
        weights = jnp.exp(scores - jnp.concatenate([top] * (tokens // 128), axis=1))
        added = jnp.sum(narrowed(weights, jnp.add), axis=1, keepdims=True)
        total = total_ref[...] * kept + added
        summed = own_head(
            jnp.dot(weights.astype(jnp.bfloat16), values, preferred_element_type=jnp.float32)
        )
        heads_ref[...] = (sum_ref[...] * kept + summed) / total
        square = jnp.zeros((requests, 128), jnp.float32)
        for h in range(HEADS):
            columns = slice(h * 128, (h + 1) * 128)
            attended = heads_ref[pl.ds(h, requests, stride=HEADS), :].astype(jnp.bfloat16)
            attended_ref[:, columns] = attended
            merged = (
                residual_ref[:, columns].astype(jnp.float32) + attended.astype(jnp.float32)
            ).astype(jnp.bfloat16)
            merged_ref[:, columns] = merged
            wide = merged.astype(jnp.float32)
            square = square + wide * wide
        mean = jnp.sum(square, axis=1, keepdims=True) * (1.0 / model_dim)
        inverse = lax.rsqrt(mean + epsilon)
        normed_ref[:, model_dim:] = routing_columns(ids_ref[...], gates_ref[...])
        normed_ref[:, :model_dim] = (
            merged_ref[...].astype(jnp.float32) * inverse * gain_ref[...]
        ).astype(jnp.bfloat16)

    shape = jax.ShapeDtypeStruct((requests, model_dim), jnp.bfloat16)
    return pl.pallas_call(
        kernel,
        out_shape=(shape, shape, jax.ShapeDtypeStruct((requests, model_dim + 128), jnp.bfloat16)),
        in_specs=[VMEM] * 3 + [SMEM] + [VMEM] * 7,
        out_specs=(VMEM,) * 3,
        scratch_shapes=[pltpu.VMEM((rows, 128), jnp.float32)],
        compiler_params=pltpu.CompilerParams(vmem_limit_bytes=16 * MEBI),
        cost_estimate=pl.CostEstimate(
            flops=4 * rows * half * tokens, bytes_accessed=4 * MEBI, transcendentals=rows * tokens
        ),
        name="finish_attention",
    )(query, fetched, table, lengths, *partial, residual, gain, ids, gates)


def local(
    queries,
    new_kv,
    kv_pages,
    page_table,
    lengths,
    shed_slots,
    residual,
    norm_gain,
    expert_ids,
    gate_weights,
    w_gate_up,
    w_down,
):
    count_of_rows, model_dim = queries.shape
    top_count = expert_ids.shape[1]
    layout = Layout(lax.axis_size("pool"), lax.axis_size("dev"))
    capacity = 2 * count_of_rows * top_count // (layout.pool * layout.dev)
    planes = layout.planes

    requested = from_behind(shed_slots, "pool", 1)
    picked = pick_pages(requested, kv_pages)
    fetched = from_behind(picked, "pool", 1)
    queries, expert_ids, picked = lax.optimization_barrier((queries, expert_ids, picked))

    expert = (lax.axis_index("pool") * layout.dev + lax.axis_index("dev")).reshape(1)
    *partial, query = own_attention(queries, new_kv, kv_pages, page_table, lengths)
    attended, merged, normed = finish_attention(
        query,
        fetched,
        page_table,
        lengths,
        partial,
        residual,
        norm_gain.reshape(1, model_dim),
        expert_ids.T,
        gate_weights.T,
        kv_pages.shape[0],
    )

    near = list(range(1, planes // 2 + 1))
    far = [0, *range(planes // 2 + 1, planes)]
    chips = range(0, layout.members, 2)
    blocks = [normed]
    for s in range(1, planes):
        blocks.append(layout.shifted(blocks[s ^ 1], 1) if s & 1 else layout.shifted(normed, s))
    arrived = []
    for s, block in enumerate(blocks):
        ready = [block] * len(chips)
        if 0 < s <= len(near):
            ready = [after(block, part) for part in arrived[0]]
        arrived.append([layout.swapped(rows, chip) for rows, chip in zip(ready, chips)])

    def to_experts(some, tie):
        pieces = [arrived[s][c] for c in range(len(chips)) for s in some]
        if tie is not None:
            pieces[0] = after(pieces[0], tie)
        own = packed(pieces)
        return own, layout.swapped(own, 1), layout.members * len(some) * capacity

    def add_cores(mine, over):
        cuts = [count_of_rows] * (mine.shape[0] // count_of_rows)
        return list(add_up([[mine], [over]], cuts, "add_cores"))

    def to_owners(sums, i):
        pieces = len(sums) // len(chips)
        return [layout.swapped(sums[c * pieces + i], chip) for c, chip in enumerate(chips)]

    def total_of(parts):
        return add_up([[part] for part in parts], [count_of_rows], "add_chips")[0]

    own, other, slots = to_experts(near, blocks[far[-1]])
    mine, over, kept = run_experts(own, other, (w_gate_up, w_down), expert, top_count, slots, True)
    near_mine, near_back = mine, layout.swapped(over, 1)
    own, other, slots = to_experts(far, over)
    other = after(other, near_back)
    mine, over, _ = run_experts(own, other, kept, expert, top_count, slots, False)
    near_sums = add_up(
        [[near_mine], [near_back]], [count_of_rows * len(near)] * len(chips), "add_cores"
    )
    far_sums = add_cores(mine, layout.swapped(over, 1))
    parts = to_owners(near_sums, 0)
    totals = add_up([[part] for part in parts], [count_of_rows] * len(near), "add_chips")
    others = [layout.shifted(total, by) for total, by in zip(totals, near)]
    for i, by in list(enumerate(far))[:0:-1]:
        others.append(layout.shifted(total_of(to_owners(far_sums, i)), by))
    merged = add_up(
        [[merged]] + [[part] for part in others], [count_of_rows], "add_first", 10**10
    )[0]
    others = [total_of(to_owners(far_sums, 0))]
    total = merged.astype(jnp.float32) + sum(part.astype(jnp.float32) for part in others)
    layer_out = total.astype(jnp.bfloat16)
    return (attended, layer_out)


def solution(mesh):
    return jax.shard_map(
        local,
        mesh=mesh,
        in_specs=(
            P(("pool", "dev"), None),
            P(("pool", "dev"), None),
            P(("pool", "dev"), None, None),
            P(("pool", "dev"), None),
            P(("pool", "dev")),
            P(("pool", "dev")),
            P(("pool", "dev"), None),
            P(),
            P(("pool", "dev"), None),
            P(("pool", "dev"), None),
            P(("pool", "dev"), None, None),
            P(("pool", "dev"), None, None),
        ),
        out_specs=(P(("pool", "dev"), None), P(("pool", "dev"), None)),
        check_vma=False,
    )
```

```python
import math

import jax
import jax.numpy as jnp
from jax import lax
from jax.experimental import pallas as pl
from jax.experimental.pallas import tpu as pltpu
from jax.sharding import PartitionSpec as P

HEAD_DIMENSION = 128
KEY_VALUE_HEADS = 2
QUERY_GROUP_SIZE = 16
HEADS = KEY_VALUE_HEADS * QUERY_GROUP_SIZE

masked_score = -1e30
epsilon = 1e-06
AXES = ("pool", "dev")
VMEM = pl.BlockSpec(memory_space=pltpu.VMEM)
SMEM = pl.BlockSpec(memory_space=pltpu.SMEM)
HBM = pl.BlockSpec(memory_space=pltpu.HBM)
MEBI = 1 << 20
DOWN_PARTS = 4
UP_WIDTH = 256
EXPERT_LIMIT = 16 * MEBI


def in_hbm(value):
    return pltpu.with_memory_space_constraint(value, pltpu.HBM)


class Layout:
    def __init__(self, pool, dev):
        self.pool, self.dev = pool, dev
        self.inner = math.gcd(dev, 4)
        self.planes = dev // self.inner
        self.members = pool * self.inner
        self.groups = [
            [self.linear(member, plane) for member in range(self.members)]
            for plane in range(self.planes)
        ]

    def linear(self, member, plane):
        return member // self.inner * self.dev + plane * self.inner + member % self.inner

    def shifted(self, value, by):
        if by == 0:
            return value
        pairs = [
            (self.linear(m, z), self.linear(m, z ^ by))
            for z in range(self.planes)
            for m in range(self.members)
        ]
        with jax.named_scope(f"plane_{by}"):
            return lax.ppermute(value, AXES, pairs)

    def swapped(self, value, by):
        if by == 0:
            return value
        pairs = [
            (self.linear(m, z), self.linear(m ^ by, z))
            for z in range(self.planes)
            for m in range(self.members)
        ]
        with jax.named_scope(f"member_{by}"):
            return lax.ppermute(value, AXES, pairs)


def from_behind(value, axis, by):
    length = lax.axis_size(axis)
    return lax.ppermute(value, axis, [(i, (i + by) % length) for i in range(length)])


def pick_pages(slots, pages):
    count = slots.shape[0]
    last = pages.shape[0] - 1

    def kernel(slots_ref, pages_ref, out_ref, sems):
        copies = []
        for i in range(count):
            page = jnp.clip(slots_ref[i], 0, last)
            copies.append(pltpu.make_async_copy(pages_ref.at[page], out_ref.at[i], sems.at[i]))
            copies[-1].start()
        for copy in copies:
            copy.wait()

    return pl.pallas_call(
        kernel,
        out_shape=jax.ShapeDtypeStruct((count,) + pages.shape[1:], pages.dtype),
        in_specs=[SMEM, HBM],
        out_specs=VMEM,
        scratch_shapes=[pltpu.SemaphoreType.DMA((count,))],
        compiler_params=pltpu.CompilerParams(vmem_limit_bytes=4 * MEBI),
        cost_estimate=pl.CostEstimate(flops=0, bytes_accessed=MEBI, transcendentals=0),
        name="pick_pages",
    )(slots, in_hbm(pages))


def head_blocks(query):
    rows = query.shape[0]
    head = lax.broadcasted_iota(jnp.int32, (rows, HEAD_DIMENSION), 0) % HEADS
    nothing = jnp.zeros_like(query)
    low = head < QUERY_GROUP_SIZE
    return jnp.concatenate([jnp.where(low, query, nothing), jnp.where(low, nothing, query)], axis=1)


def own_head(both):
    rows = both.shape[0]
    head = lax.broadcasted_iota(jnp.int32, (rows, HEAD_DIMENSION), 0) % HEADS
    return jnp.where(
        head < QUERY_GROUP_SIZE, both[:, :HEAD_DIMENSION], both[:, HEAD_DIMENSION:]
    )


def tokens_of_pages(table, lengths_ref, first, page_len):
    count_of_rows, width = table.shape
    page = lax.broadcasted_iota(jnp.int32, (count_of_rows, 128), 1) + first
    row = lax.broadcasted_iota(jnp.int32, (count_of_rows, 128), 0)
    lengths = jnp.zeros((count_of_rows, 128), jnp.int32)
    for r in range(count_of_rows):
        lengths = jnp.where(row == r, lengths_ref[r], lengths)
    held = jnp.zeros((count_of_rows, 128), jnp.float32)
    for p in range(width):
        filled = jnp.clip(lengths - p * page_len, 0, page_len).astype(jnp.float32)
        held = held + jnp.where(table[:, p : p + 1] == page, filled, 0.0)
    return held


def token_bias(held, first_page, tokens, page_len):
    page = lax.broadcasted_iota(jnp.int32, (128, tokens), 0)
    token = lax.broadcasted_iota(jnp.int32, (128, tokens), 1)
    widen = (page == token // page_len + first_page).astype(jnp.bfloat16)
    limit = jnp.dot(held.astype(jnp.bfloat16), widen, preferred_element_type=jnp.float32)
    inside = (token[: held.shape[0]] % page_len).astype(jnp.float32)
    return jnp.where(inside < limit, 0.0, masked_score)


def masked_scores(blocks, keys, bias, scaling):
    scores = lax.dot_general(
        blocks, keys, (((1,), (1,)), ((), ())), preferred_element_type=jnp.float32
    )
    requests, tokens = bias.shape
    return (
        (scores * scaling).reshape(requests, HEADS, tokens) + bias[:, None, :]
    ).reshape(requests * HEADS, tokens)


def narrowed(value, join):
    result = value[:, :128]
    for start in range(128, value.shape[1], 128):
        result = join(result, value[:, start : start + 128])
    return result


def own_attention(queries, new_kv, pages, table, lengths, down_proj):
    page_count, page_len, kv_width = pages.shape
    requests = new_kv.shape[0]
    rows = requests * HEADS
    half = kv_width // 2
    chunk_pages = 128 * (page_count // 128) // 4
    chunk = chunk_pages * page_len
    chunks = page_count // chunk_pages
    scaling = 1.0 / math.sqrt(HEAD_DIMENSION)

    def kernel(
        queries_hbm,
        new_hbm,
        pages_hbm,
        table_hbm,
        lengths_hbm,
        down_hbm,
        out_ref,
        top_ref,
        sum_ref,
        query_ref,
        down_ref,
        s_ref,
        fresh_ref,
        heads_ref,
        flat_ref,
        pages_ref,
        table_ref,
        lengths_ref,
        sems,
    ):
        page_copies = [
            pltpu.make_async_copy(
                pages_hbm.at[pl.ds(c * chunk_pages, chunk_pages)],
                pages_ref.at[pl.ds(c * chunk_pages, chunk_pages)],
                sems.at[4 + c],
            )
            for c in range(chunks)
        ]
        copies = [
            pltpu.make_async_copy(queries_hbm, flat_ref, sems.at[0]),
            pltpu.make_async_copy(table_hbm, table_ref, sems.at[1]),
            pltpu.make_async_copy(lengths_hbm, lengths_ref, sems.at[2]),
            pltpu.make_async_copy(new_hbm, fresh_ref.at[pl.ds(0, requests)], sems.at[3]),
        ]
        down_rows = down_ref.shape[0] // DOWN_PARTS
        down_copies = [
            pltpu.make_async_copy(
                down_hbm.at[0, pl.ds(c * down_rows, down_rows)],
                down_ref.at[pl.ds(c * down_rows, down_rows)],
                sems.at[4 + chunks + c],
            )
            for c in range(DOWN_PARTS)
        ]
        fresh_ref[requests:] = jnp.zeros_like(fresh_ref[requests:])
        for copy in copies + page_copies:
            copy.start()
        for copy in copies:
            copy.wait()
        for h in range(HEADS):
            heads_ref[pl.ds(h, requests, stride=HEADS), :] = flat_ref[
                :, h * 128 : (h + 1) * 128
            ].astype(jnp.float32)
        query = heads_ref[...].astype(jnp.bfloat16)
        query_ref[...] = query
        blocks = head_blocks(query)
        held = tokens_of_pages(table_ref[...], lengths_ref, 0, page_len)
        lane = lax.broadcasted_iota(jnp.int32, (requests, 128), 1)
        own = lax.broadcasted_iota(jnp.int32, (requests, 128), 0)
        fresh_bias = jnp.where(lane == own, 0.0, masked_score)
        fresh = masked_scores(blocks, fresh_ref[:, :half], fresh_bias, scaling)
        s_ref[:, chunks * chunk :] = fresh
        top = fresh
        for c in range(chunks):
            page_copies[c].wait()
            if c == chunks - 1:
                for copy in down_copies:
                    copy.start()
            keys = pages_ref[c * chunk_pages : (c + 1) * chunk_pages, :, :half].reshape(chunk, half)
            bias = token_bias(held, c * chunk_pages, chunk, page_len)
            scores = masked_scores(blocks, keys, bias, scaling)
            s_ref[:, c * chunk : (c + 1) * chunk] = scores
            top = jnp.maximum(top, narrowed(scores, jnp.maximum))
        top = jnp.max(top, axis=1, keepdims=True)
        weights = jnp.exp(s_ref[:, chunks * chunk :] - top)
        total = weights
        summed = jnp.dot(
            weights.astype(jnp.bfloat16), fresh_ref[:, half:], preferred_element_type=jnp.float32
        )
        for c in range(chunks):
            values = pages_ref[c * chunk_pages : (c + 1) * chunk_pages, :, half:].reshape(chunk, half)
            weights = jnp.exp(s_ref[:, c * chunk : (c + 1) * chunk] - top)
            total = total + narrowed(weights, jnp.add)
            summed = summed + jnp.dot(
                weights.astype(jnp.bfloat16), values, preferred_element_type=jnp.float32
            )
        out_ref[...] = own_head(summed)
        top_ref[...] = jnp.broadcast_to(top, top_ref.shape)
        sum_ref[...] = jnp.broadcast_to(jnp.sum(total, axis=1, keepdims=True), sum_ref.shape)
        for copy in down_copies:
            copy.wait()

    shape = jax.ShapeDtypeStruct((rows, 128), jnp.float32)
    return pl.pallas_call(
        kernel,
        out_shape=(
            shape,
            shape,
            shape,
            jax.ShapeDtypeStruct((rows, 128), jnp.bfloat16),
            pltpu.VMEM(down_proj.shape[1:], jnp.bfloat16),
        ),
        in_specs=[HBM] * 6,
        out_specs=(VMEM,) * 5,
        scratch_shapes=[
            pltpu.VMEM((rows, chunks * chunk + 128), jnp.float32),
            pltpu.VMEM((128, kv_width), jnp.bfloat16),
            pltpu.VMEM((rows, 128), jnp.float32),
            pltpu.VMEM(queries.shape, jnp.bfloat16),
            pltpu.VMEM(pages.shape, jnp.bfloat16),
            pltpu.VMEM(table.shape, jnp.int32),
            pltpu.SMEM(lengths.shape, jnp.int32),
            pltpu.SemaphoreType.DMA((4 + chunks + DOWN_PARTS,)),
        ],
        compiler_params=pltpu.CompilerParams(vmem_limit_bytes=24 * MEBI),
        cost_estimate=pl.CostEstimate(
            flops=4 * rows * half * chunks * chunk,
            bytes_accessed=16 * MEBI,
            transcendentals=rows * chunks * chunk,
        ),
        name="own_attention",
    )(*[in_hbm(value) for value in (queries, new_kv, pages, table, lengths, down_proj)])


def routing_columns(ids, gates):
    top_count = ids.shape[0]
    high = gates.astype(jnp.bfloat16)
    rest = gates - high.astype(jnp.float32)
    middle = rest.astype(jnp.bfloat16)
    low = (rest - middle.astype(jnp.float32)).astype(jnp.bfloat16)
    source = lax.broadcasted_iota(jnp.int32, (top_count, 128), 0)
    lane = lax.broadcasted_iota(jnp.int32, (top_count, 128), 1)
    columns = 0.0
    for i, part in enumerate((ids.astype(jnp.float32).astype(jnp.bfloat16), high, middle, low)):
        place = (lane == source + i * top_count).astype(jnp.bfloat16)
        columns = columns + lax.dot_general(
            part, place, (((0,), (0,)), ((), ())), preferred_element_type=jnp.float32
        )
    return columns.astype(jnp.bfloat16)


def stacked(parts):
    if len(parts) == 1:
        return parts[0]
    return jnp.concatenate(parts, axis=0)


def packed(parts, work=0):
    if len(parts) == 1 and not work:
        return parts[0]
    rows = sum(part.shape[0] for part in parts)
    columns = parts[0].shape[1]

    def kernel(*refs):
        out_ref, offset = refs[-1], 0
        for ref in refs[:-1]:
            out_ref[offset : offset + ref.shape[0]] = ref[...]
            offset += ref.shape[0]

    return pl.pallas_call(
        kernel,
        out_shape=jax.ShapeDtypeStruct((rows, columns), parts[0].dtype),
        in_specs=[VMEM] * len(parts),
        out_specs=VMEM,
        compiler_params=pltpu.CompilerParams(vmem_limit_bytes=12 * MEBI),
        cost_estimate=pl.CostEstimate(flops=work, bytes_accessed=0, transcendentals=0),
        name="packed",
    )(*parts)


def after(value, *others):
    return lax.optimization_barrier((value, *others))[0]


def run_experts(own, other, weights, expert, top_count, slots, keep):
    rows, model_dim = own.shape
    rows, model_dim = 2 * rows, model_dim - 128
    up_first, up_rest, down_proj = weights
    hidden_dim = down_proj.shape[0]
    width = UP_WIDTH
    up_steps = hidden_dim // width
    out_width = 1024 if rows <= 512 else 512
    out_steps = model_dim // out_width
    strip = 256

    def kernel(expert_ref, own_ref, other_ref, first_ref, rest_in, down_ref, out_ref, over_ref, *refs):
        if keep:
            rest_ref, tokens_ref, hidden_ref, sems = refs
            copies = up_parts(rest_in, rest_ref, range(1, up_steps), sems)
            for copy in copies:
                copy.start()
        else:
            rest_ref, copies = rest_in, []
            tokens_ref, hidden_ref = refs

        token_refs = [own_ref, other_ref]
        routing = stacked([ref[:, model_dim:] for ref in token_refs]).astype(jnp.float32)
        wanted = expert_ref[0].astype(jnp.float32)
        match = jnp.zeros((rows, 1), jnp.float32)
        gates = [jnp.zeros((rows, 1), jnp.float32)] * 3
        for k in range(top_count):
            hit = routing[:, k : k + 1] == wanted
            match = jnp.where(hit, 1.0, match)
            gates = [
                jnp.where(hit, routing[:, i * top_count + k : i * top_count + k + 1], gate)
                for i, gate in enumerate(gates, 1)
            ]
        lane = lax.broadcasted_iota(jnp.int32, (rows, slots), 1)
        match = jnp.broadcast_to(match, (rows, slots))
        earlier = (
            lax.broadcasted_iota(jnp.int32, (strip, strip), 0)
            > lax.broadcasted_iota(jnp.int32, (strip, strip), 1)
        ).astype(jnp.bfloat16)
        ranks, before = [], jnp.zeros((1, slots), jnp.float32)
        for start in range(0, rows, strip):
            piece = match[start : start + strip]
            ranks.append(
                before
                + jnp.dot(earlier, piece.astype(jnp.bfloat16), preferred_element_type=jnp.float32)
            )
            before = before + jnp.sum(piece, axis=0, keepdims=True)
        rank = stacked(ranks)
        choice = jnp.where(rank == lane.astype(jnp.float32), match, 0.0)
        pick = choice.T.astype(jnp.bfloat16)
        place = choice.astype(jnp.bfloat16)
        gate_columns = jnp.where(
            lane == 0, gates[0], jnp.where(lane == 1, gates[1], jnp.where(lane == 2, gates[2], 0.0))
        ).astype(jnp.bfloat16)
        gate = jnp.sum(
            jnp.dot(pick, gate_columns, preferred_element_type=jnp.float32), axis=1, keepdims=True
        )
        for start in range(0, model_dim, out_width):
            columns = slice(start, start + out_width)
            tokens = stacked([ref[:, columns] for ref in token_refs])
            tokens_ref[:, columns] = jnp.dot(
                pick, tokens, preferred_element_type=jnp.float32
            ).astype(jnp.bfloat16)

        for c in range(up_steps):
            for copy in copies[2 * c - 2 : 2 * c] if c else []:
                copy.wait()
            start = c * width
            up_ref, place_of = (rest_ref, 2 * start - 2 * width) if c else (first_ref, 0)
            tokens = tokens_ref[...]
            gated = jnp.dot(
                tokens, up_ref[:, place_of : place_of + width], preferred_element_type=jnp.float32
            )
            up = jnp.dot(
                tokens,
                up_ref[:, place_of + width : place_of + 2 * width],
                preferred_element_type=jnp.float32,
            )
            hidden_ref[:, start : start + width] = (gated / (1.0 + jnp.exp(-gated)) * up).astype(
                jnp.bfloat16
            )

        for c in range(out_steps):
            columns = slice(c * out_width, (c + 1) * out_width)
            result = jnp.dot(
                hidden_ref[...], down_ref[:, columns], preferred_element_type=jnp.float32
            )
            result = (result * gate).astype(jnp.bfloat16)
            sums = jnp.dot(place, result, preferred_element_type=jnp.float32).astype(jnp.bfloat16)
            out_ref[:, columns] = sums[: rows // 2]
            over_ref[:, columns] = sums[rows // 2 :]

    shape = jax.ShapeDtypeStruct((rows // 2, model_dim), jnp.bfloat16)
    kept, scratch = (), []
    if keep:
        kept = (pltpu.VMEM((model_dim, 2 * (hidden_dim - width)), jnp.bfloat16),)
        scratch = [pltpu.SemaphoreType.DMA((2 * (up_steps - 1),))]
        up_rest = in_hbm(up_rest)
    results = pl.pallas_call(
        kernel,
        out_shape=(shape, shape) + kept,
        in_specs=[SMEM, VMEM, VMEM, VMEM, HBM if keep else VMEM, VMEM],
        out_specs=(VMEM,) * (2 + len(kept)),
        scratch_shapes=[
            pltpu.VMEM((slots, model_dim), jnp.bfloat16),
            pltpu.VMEM((slots, hidden_dim), jnp.bfloat16),
        ]
        + scratch,
        compiler_params=pltpu.CompilerParams(vmem_limit_bytes=EXPERT_LIMIT),
        cost_estimate=pl.CostEstimate(
            flops=6 * slots * model_dim * hidden_dim,
            bytes_accessed=20 * MEBI,
            transcendentals=slots * hidden_dim,
        ),
        name="run_experts",
    )(expert, own, other, up_first, up_rest, down_proj)
    return results[0], results[1], results[2:]


def add_up(parts, cuts, name, work=0):
    rows = sum(cuts)
    model_dim = parts[0][0].shape[1]
    flat = [piece for part in parts for piece in part]
    places = []
    for part in parts:
        start = 0
        for piece in part:
            places.append((start, start + piece.shape[0]))
            start += piece.shape[0]

    def kernel(*refs):
        in_refs, out_refs = refs[: len(flat)], refs[len(flat) :]
        step = 1024
        for start in range(0, model_dim, step):
            columns = slice(start, start + step)
            offset = 0
            for out_ref, cut in zip(out_refs, cuts):
                total = 0.0
                for ref, (low, high) in zip(in_refs, places):
                    if low <= offset and offset + cut <= high:
                        rows_of = slice(offset - low, offset - low + cut)
                        total = total + ref[rows_of, columns].astype(jnp.float32)
                out_ref[:, columns] = total.astype(jnp.bfloat16)
                offset += cut

    return pl.pallas_call(
        kernel,
        out_shape=tuple(jax.ShapeDtypeStruct((cut, model_dim), jnp.bfloat16) for cut in cuts),
        in_specs=[VMEM] * len(flat),
        out_specs=(VMEM,) * len(cuts),
        compiler_params=pltpu.CompilerParams(vmem_limit_bytes=12 * MEBI),
        cost_estimate=pl.CostEstimate(
            flops=work, bytes_accessed=0, transcendentals=0
        ),
        name=name,
    )(*flat)


def up_parts(up_hbm, up_ref, steps, sems):
    hidden_dim = up_hbm.shape[2] // 2
    return [
        pltpu.make_async_copy(
            up_hbm.at[0, :, pl.ds(half * hidden_dim + c * UP_WIDTH, UP_WIDTH)],
            up_ref.at[:, pl.ds((2 * i + half) * UP_WIDTH, UP_WIDTH)],
            sems.at[2 * i + half],
        )
        for i, c in enumerate(steps)
        for half in range(2)
    ]


def finish_attention(
    query, fetched, table, lengths, partial, residual, gain, ids, gates, gate_up, pages_own
):
    count, page_len, kv_width = fetched.shape
    half = kv_width // 2
    tokens = count * page_len
    requests, model_dim = residual.shape
    rows = query.shape[0]
    scaling = 1.0 / math.sqrt(HEAD_DIMENSION)

    def kernel(q_ref, fetched_ref, table_ref, lengths_ref, sum_ref, top_ref, total_ref, residual_ref, gain_ref, ids_ref, gates_ref, up_hbm, attended_ref, merged_ref, normed_ref, up_ref, heads_ref, sems):
        up_copies = up_parts(up_hbm, up_ref, [0], sems)
        for copy in up_copies:
            copy.start()
        blocks = head_blocks(q_ref[...])
        held = tokens_of_pages(table_ref[...], lengths_ref, pages_own, page_len)
        bias = token_bias(held, 0, tokens, page_len)
        keys = fetched_ref[:, :, :half].reshape(tokens, half)
        values = fetched_ref[:, :, half:].reshape(tokens, half)
        scores = masked_scores(blocks, keys, bias, scaling)
        before = top_ref[...]
        shed_top = jnp.max(narrowed(scores, jnp.maximum), axis=1, keepdims=True)
        top = jnp.maximum(before, shed_top)
        kept = jnp.exp(before - top)
        weights = jnp.exp(scores - jnp.concatenate([top] * (tokens // 128), axis=1))
        added = jnp.sum(narrowed(weights, jnp.add), axis=1, keepdims=True)
        total = total_ref[...] * kept + added
        summed = own_head(
            jnp.dot(weights.astype(jnp.bfloat16), values, preferred_element_type=jnp.float32)
        )
        heads_ref[...] = (sum_ref[...] * kept + summed) / total
        square = jnp.zeros((requests, 128), jnp.float32)
        for h in range(HEADS):
            columns = slice(h * 128, (h + 1) * 128)
            attended = heads_ref[pl.ds(h, requests, stride=HEADS), :].astype(jnp.bfloat16)
            attended_ref[:, columns] = attended
            merged = (
                residual_ref[:, columns].astype(jnp.float32) + attended.astype(jnp.float32)
            ).astype(jnp.bfloat16)
            merged_ref[:, columns] = merged
            wide = merged.astype(jnp.float32)
            square = square + wide * wide
        mean = jnp.sum(square, axis=1, keepdims=True) * (1.0 / model_dim)
        inverse = lax.rsqrt(mean + epsilon)
        normed_ref[:, model_dim:] = routing_columns(ids_ref[...], gates_ref[...])
        normed_ref[:, :model_dim] = (
            merged_ref[...].astype(jnp.float32) * inverse * gain_ref[...]
        ).astype(jnp.bfloat16)
        for copy in up_copies:
            copy.wait()

    shape = jax.ShapeDtypeStruct((requests, model_dim), jnp.bfloat16)
    return pl.pallas_call(
        kernel,
        out_shape=(
            shape,
            shape,
            jax.ShapeDtypeStruct((requests, model_dim + 128), jnp.bfloat16),
            pltpu.VMEM((model_dim, 2 * UP_WIDTH), jnp.bfloat16),
        ),
        in_specs=[VMEM] * 3 + [SMEM] + [VMEM] * 7 + [HBM],
        out_specs=(VMEM,) * 4,
        scratch_shapes=[pltpu.VMEM((rows, 128), jnp.float32), pltpu.SemaphoreType.DMA((2,))],
        compiler_params=pltpu.CompilerParams(vmem_limit_bytes=16 * MEBI),
        cost_estimate=pl.CostEstimate(
            flops=4 * rows * half * tokens, bytes_accessed=4 * MEBI, transcendentals=rows * tokens
        ),
        name="finish_attention",
    )(query, fetched, table, lengths, *partial, residual, gain, ids, gates, in_hbm(gate_up))


def local(
    queries,
    new_kv,
    kv_pages,
    page_table,
    lengths,
    shed_slots,
    residual,
    norm_gain,
    expert_ids,
    gate_weights,
    w_gate_up,
    w_down,
):
    count_of_rows, model_dim = queries.shape
    top_count = expert_ids.shape[1]
    layout = Layout(lax.axis_size("pool"), lax.axis_size("dev"))
    capacity = 2 * count_of_rows * top_count // (layout.pool * layout.dev)
    planes = layout.planes

    requested = from_behind(shed_slots, "pool", 1)
    picked = pick_pages(requested, kv_pages)
    fetched = from_behind(picked, "pool", 1)
    queries, expert_ids, picked = lax.optimization_barrier((queries, expert_ids, picked))

    expert = (lax.axis_index("pool") * layout.dev + lax.axis_index("dev")).reshape(1)
    *partial, query, down_near = own_attention(
        queries, new_kv, kv_pages, page_table, lengths, w_down
    )
    attended, merged, normed, up_first = finish_attention(
        query,
        fetched,
        page_table,
        lengths,
        partial,
        residual,
        norm_gain.reshape(1, model_dim),
        expert_ids.T,
        gate_weights.T,
        w_gate_up,
        kv_pages.shape[0],
    )

    near = list(range(1, planes // 2 + 1))
    far = [0, *range(planes // 2 + 1, planes)]
    chips = range(0, layout.members, 2)
    blocks = [normed]
    for s in range(1, planes):
        blocks.append(layout.shifted(blocks[s ^ 1], 1) if s & 1 else layout.shifted(normed, s))
    arrived = []
    for s, block in enumerate(blocks):
        ready = [block] * len(chips)
        if 0 < s <= len(near):
            ready = [after(block, part) for part in arrived[0]]
        arrived.append([layout.swapped(rows, chip) for rows, chip in zip(ready, chips)])

    def to_experts(some, tie):
        pieces = [arrived[s][c] for c in range(len(chips)) for s in some]
        if tie is not None:
            pieces[0] = after(pieces[0], tie)
        own = packed(pieces)
        return own, layout.swapped(own, 1), layout.members * len(some) * capacity

    def add_cores(mine, over):
        cuts = [count_of_rows] * (mine.shape[0] // count_of_rows)
        return list(add_up([[mine], [over]], cuts, "add_cores"))

    def to_owners(sums, i):
        pieces = len(sums) // len(chips)
        return [layout.swapped(sums[c * pieces + i], chip) for c, chip in enumerate(chips)]

    def total_of(parts):
        return add_up([[part] for part in parts], [count_of_rows], "add_chips")[0]

    own, other, slots = to_experts(near, blocks[far[-1]])
    mine, over, (up_rest,) = run_experts(
        own, other, (up_first, w_gate_up, down_near), expert, top_count, slots, True
    )
    near_mine, near_back = mine, layout.swapped(over, 1)
    own, other, slots = to_experts(far, over)
    mine, over, _ = run_experts(
        own, other, (up_first, up_rest, down_near), expert, top_count, slots, False
    )
    near_sums = add_up(
        [[near_mine], [near_back]], [count_of_rows * len(near)] * len(chips), "add_cores"
    )
    far_sums = add_cores(mine, layout.swapped(over, 1))
    parts = to_owners(near_sums, 0)
    totals = add_up([[part] for part in parts], [count_of_rows] * len(near), "add_chips")
    others = [layout.shifted(total, by) for total, by in list(zip(totals, near))[::-1]]
    for i, by in list(enumerate(far))[:0:-1]:
        others.append(layout.shifted(total_of(to_owners(far_sums, i)), by))
    merged = add_up(
        [[merged]] + [[part] for part in others], [count_of_rows], "add_first", 10**10
    )[0]
    others = [total_of(to_owners(far_sums, 0))]
    total = merged.astype(jnp.float32) + sum(part.astype(jnp.float32) for part in others)
    layer_out = total.astype(jnp.bfloat16)
    return (attended, layer_out)


def solution(mesh):
    return jax.shard_map(
        local,
        mesh=mesh,
        in_specs=(
            P(("pool", "dev"), None),
            P(("pool", "dev"), None),
            P(("pool", "dev"), None, None),
            P(("pool", "dev"), None),
            P(("pool", "dev")),
            P(("pool", "dev")),
            P(("pool", "dev"), None),
            P(),
            P(("pool", "dev"), None),
            P(("pool", "dev"), None),
            P(("pool", "dev"), None, None),
            P(("pool", "dev"), None, None),
        ),
        out_specs=(P(("pool", "dev"), None), P(("pool", "dev"), None)),
        check_vma=False,
    )
```

```python
import math

import jax
import jax.numpy as jnp
from jax import lax
from jax.experimental import pallas as pl
from jax.experimental.pallas import tpu as pltpu
from jax.sharding import PartitionSpec as P

HEAD_DIMENSION = 128
KEY_VALUE_HEADS = 2
QUERY_GROUP_SIZE = 16
HEADS = KEY_VALUE_HEADS * QUERY_GROUP_SIZE

masked_score = -1e30
epsilon = 1e-06
AXES = ("pool", "dev")
VMEM = pl.BlockSpec(memory_space=pltpu.VMEM)
SMEM = pl.BlockSpec(memory_space=pltpu.SMEM)
HBM = pl.BlockSpec(memory_space=pltpu.HBM)
MEBI = 1 << 20
EXPERT_LIMIT = 16 * MEBI


def in_hbm(value):
    return pltpu.with_memory_space_constraint(value, pltpu.HBM)


class Layout:
    def __init__(self, pool, dev):
        self.pool, self.dev = pool, dev
        self.inner = math.gcd(dev, 4)
        self.planes = dev // self.inner
        self.members = pool * self.inner
        self.groups = [
            [self.linear(member, plane) for member in range(self.members)]
            for plane in range(self.planes)
        ]

    def linear(self, member, plane):
        return member // self.inner * self.dev + plane * self.inner + member % self.inner

    def shifted(self, value, by):
        if by == 0:
            return value
        pairs = [
            (self.linear(m, z), self.linear(m, z ^ by))
            for z in range(self.planes)
            for m in range(self.members)
        ]
        with jax.named_scope(f"plane_{by}"):
            return lax.ppermute(value, AXES, pairs)

    def swapped(self, value, by):
        if by == 0:
            return value
        pairs = [
            (self.linear(m, z), self.linear(m ^ by, z))
            for z in range(self.planes)
            for m in range(self.members)
        ]
        with jax.named_scope(f"member_{by}"):
            return lax.ppermute(value, AXES, pairs)


def from_behind(value, axis, by):
    length = lax.axis_size(axis)
    return lax.ppermute(value, axis, [(i, (i + by) % length) for i in range(length)])


def pick_pages(slots, pages):
    count = slots.shape[0]
    last = pages.shape[0] - 1

    def kernel(slots_ref, pages_ref, out_ref, sems):
        copies = []
        for i in range(count):
            page = jnp.clip(slots_ref[i], 0, last)
            copies.append(pltpu.make_async_copy(pages_ref.at[page], out_ref.at[i], sems.at[i]))
            copies[-1].start()
        for copy in copies:
            copy.wait()

    return pl.pallas_call(
        kernel,
        out_shape=jax.ShapeDtypeStruct((count,) + pages.shape[1:], pages.dtype),
        in_specs=[SMEM, HBM],
        out_specs=VMEM,
        scratch_shapes=[pltpu.SemaphoreType.DMA((count,))],
        compiler_params=pltpu.CompilerParams(vmem_limit_bytes=4 * MEBI),
        cost_estimate=pl.CostEstimate(flops=0, bytes_accessed=MEBI, transcendentals=0),
        name="pick_pages",
    )(slots, in_hbm(pages))


def head_blocks(query):
    rows = query.shape[0]
    head = lax.broadcasted_iota(jnp.int32, (rows, HEAD_DIMENSION), 0) % HEADS
    nothing = jnp.zeros_like(query)
    low = head < QUERY_GROUP_SIZE
    return jnp.concatenate([jnp.where(low, query, nothing), jnp.where(low, nothing, query)], axis=1)


def own_head(both):
    rows = both.shape[0]
    head = lax.broadcasted_iota(jnp.int32, (rows, HEAD_DIMENSION), 0) % HEADS
    return jnp.where(
        head < QUERY_GROUP_SIZE, both[:, :HEAD_DIMENSION], both[:, HEAD_DIMENSION:]
    )


def tokens_of_pages(table, lengths_ref, first, page_len):
    count_of_rows, width = table.shape
    page = lax.broadcasted_iota(jnp.int32, (count_of_rows, 128), 1) + first
    row = lax.broadcasted_iota(jnp.int32, (count_of_rows, 128), 0)
    lengths = jnp.zeros((count_of_rows, 128), jnp.int32)
    for r in range(count_of_rows):
        lengths = jnp.where(row == r, lengths_ref[r], lengths)
    held = jnp.zeros((count_of_rows, 128), jnp.float32)
    for p in range(width):
        filled = jnp.clip(lengths - p * page_len, 0, page_len).astype(jnp.float32)
        held = held + jnp.where(table[:, p : p + 1] == page, filled, 0.0)
    return held


def token_bias(held, first_page, tokens, page_len):
    page = lax.broadcasted_iota(jnp.int32, (128, tokens), 0)
    token = lax.broadcasted_iota(jnp.int32, (128, tokens), 1)
    widen = (page == token // page_len + first_page).astype(jnp.bfloat16)
    limit = jnp.dot(held.astype(jnp.bfloat16), widen, preferred_element_type=jnp.float32)
    inside = (token[: held.shape[0]] % page_len).astype(jnp.float32)
    return jnp.where(inside < limit, 0.0, masked_score)


def masked_scores(blocks, keys, bias, scaling):
    scores = lax.dot_general(
        blocks, keys, (((1,), (1,)), ((), ())), preferred_element_type=jnp.float32
    )
    requests, tokens = bias.shape
    return (
        (scores * scaling).reshape(requests, HEADS, tokens) + bias[:, None, :]
    ).reshape(requests * HEADS, tokens)


def narrowed(value, join):
    result = value[:, :128]
    for start in range(128, value.shape[1], 128):
        result = join(result, value[:, start : start + 128])
    return result


def own_attention(queries, new_kv, pages, table, lengths):
    page_count, page_len, kv_width = pages.shape
    requests = new_kv.shape[0]
    rows = requests * HEADS
    half = kv_width // 2
    chunk_pages = 128 * (page_count // 128) // 4
    chunk = chunk_pages * page_len
    chunks = page_count // chunk_pages
    scaling = 1.0 / math.sqrt(HEAD_DIMENSION)

    def kernel(
        queries_hbm,
        new_hbm,
        pages_hbm,
        table_hbm,
        lengths_hbm,
        out_ref,
        top_ref,
        sum_ref,
        query_ref,
        s_ref,
        fresh_ref,
        heads_ref,
        flat_ref,
        pages_ref,
        table_ref,
        lengths_ref,
        sems,
    ):
        page_copies = [
            pltpu.make_async_copy(
                pages_hbm.at[pl.ds(c * chunk_pages, chunk_pages)],
                pages_ref.at[pl.ds(c * chunk_pages, chunk_pages)],
                sems.at[4 + c],
            )
            for c in range(chunks)
        ]
        copies = [
            pltpu.make_async_copy(queries_hbm, flat_ref, sems.at[0]),
            pltpu.make_async_copy(table_hbm, table_ref, sems.at[1]),
            pltpu.make_async_copy(lengths_hbm, lengths_ref, sems.at[2]),
            pltpu.make_async_copy(new_hbm, fresh_ref.at[pl.ds(0, requests)], sems.at[3]),
        ]
        fresh_ref[requests:] = jnp.zeros_like(fresh_ref[requests:])
        for copy in copies + page_copies:
            copy.start()
        for copy in copies:
            copy.wait()
        for h in range(HEADS):
            heads_ref[pl.ds(h, requests, stride=HEADS), :] = flat_ref[
                :, h * 128 : (h + 1) * 128
            ].astype(jnp.float32)
        query = heads_ref[...].astype(jnp.bfloat16)
        query_ref[...] = query
        blocks = head_blocks(query)
        held = tokens_of_pages(table_ref[...], lengths_ref, 0, page_len)
        lane = lax.broadcasted_iota(jnp.int32, (requests, 128), 1)
        own = lax.broadcasted_iota(jnp.int32, (requests, 128), 0)
        fresh_bias = jnp.where(lane == own, 0.0, masked_score)
        fresh = masked_scores(blocks, fresh_ref[:, :half], fresh_bias, scaling)
        s_ref[:, chunks * chunk :] = fresh
        top = fresh
        for c in range(chunks):
            page_copies[c].wait()
            keys = pages_ref[c * chunk_pages : (c + 1) * chunk_pages, :, :half].reshape(chunk, half)
            bias = token_bias(held, c * chunk_pages, chunk, page_len)
            scores = masked_scores(blocks, keys, bias, scaling)
            s_ref[:, c * chunk : (c + 1) * chunk] = scores
            top = jnp.maximum(top, narrowed(scores, jnp.maximum))
        top = jnp.max(top, axis=1, keepdims=True)
        weights = jnp.exp(s_ref[:, chunks * chunk :] - top)
        total = weights
        summed = jnp.dot(
            weights.astype(jnp.bfloat16), fresh_ref[:, half:], preferred_element_type=jnp.float32
        )
        for c in range(chunks):
            values = pages_ref[c * chunk_pages : (c + 1) * chunk_pages, :, half:].reshape(chunk, half)
            weights = jnp.exp(s_ref[:, c * chunk : (c + 1) * chunk] - top)
            total = total + narrowed(weights, jnp.add)
            summed = summed + jnp.dot(
                weights.astype(jnp.bfloat16), values, preferred_element_type=jnp.float32
            )
        out_ref[...] = own_head(summed)
        top_ref[...] = jnp.broadcast_to(top, top_ref.shape)
        sum_ref[...] = jnp.broadcast_to(jnp.sum(total, axis=1, keepdims=True), sum_ref.shape)

    shape = jax.ShapeDtypeStruct((rows, 128), jnp.float32)
    return pl.pallas_call(
        kernel,
        out_shape=(shape, shape, shape, jax.ShapeDtypeStruct((rows, 128), jnp.bfloat16)),
        in_specs=[HBM] * 5,
        out_specs=(VMEM,) * 4,
        scratch_shapes=[
            pltpu.VMEM((rows, chunks * chunk + 128), jnp.float32),
            pltpu.VMEM((128, kv_width), jnp.bfloat16),
            pltpu.VMEM((rows, 128), jnp.float32),
            pltpu.VMEM(queries.shape, jnp.bfloat16),
            pltpu.VMEM(pages.shape, jnp.bfloat16),
            pltpu.VMEM(table.shape, jnp.int32),
            pltpu.SMEM(lengths.shape, jnp.int32),
            pltpu.SemaphoreType.DMA((4 + chunks,)),
        ],
        compiler_params=pltpu.CompilerParams(vmem_limit_bytes=24 * MEBI),
        cost_estimate=pl.CostEstimate(
            flops=4 * rows * half * chunks * chunk,
            bytes_accessed=16 * MEBI,
            transcendentals=rows * chunks * chunk,
        ),
        name="own_attention",
    )(*[in_hbm(value) for value in (queries, new_kv, pages, table, lengths)])


def routing_columns(ids, gates):
    top_count = ids.shape[0]
    high = gates.astype(jnp.bfloat16)
    rest = gates - high.astype(jnp.float32)
    middle = rest.astype(jnp.bfloat16)
    low = (rest - middle.astype(jnp.float32)).astype(jnp.bfloat16)
    source = lax.broadcasted_iota(jnp.int32, (top_count, 128), 0)
    lane = lax.broadcasted_iota(jnp.int32, (top_count, 128), 1)
    columns = 0.0
    for i, part in enumerate((ids.astype(jnp.float32).astype(jnp.bfloat16), high, middle, low)):
        place = (lane == source + i * top_count).astype(jnp.bfloat16)
        columns = columns + lax.dot_general(
            part, place, (((0,), (0,)), ((), ())), preferred_element_type=jnp.float32
        )
    return columns.astype(jnp.bfloat16)


def stacked(parts):
    if len(parts) == 1:
        return parts[0]
    return jnp.concatenate(parts, axis=0)


def packed(parts, work=0):
    if len(parts) == 1 and not work:
        return parts[0]
    rows = sum(part.shape[0] for part in parts)
    columns = parts[0].shape[1]

    def kernel(*refs):
        out_ref, offset = refs[-1], 0
        for ref in refs[:-1]:
            out_ref[offset : offset + ref.shape[0]] = ref[...]
            offset += ref.shape[0]

    return pl.pallas_call(
        kernel,
        out_shape=jax.ShapeDtypeStruct((rows, columns), parts[0].dtype),
        in_specs=[VMEM] * len(parts),
        out_specs=VMEM,
        compiler_params=pltpu.CompilerParams(vmem_limit_bytes=12 * MEBI),
        cost_estimate=pl.CostEstimate(flops=work, bytes_accessed=0, transcendentals=0),
        name="packed",
    )(*parts)


def after(value, *others):
    return lax.optimization_barrier((value, *others))[0]


def run_experts(own, other, weights, expert, top_count, slots, keep):
    rows, model_dim = own.shape
    rows, model_dim = 2 * rows, model_dim - 128
    gate_up, down_proj = weights
    double, hidden_dim = gate_up.shape[-1], down_proj.shape[-2]
    width = 256
    up_steps = hidden_dim // width
    out_width = 1024 if rows <= 512 else 512
    out_steps = model_dim // out_width
    strip = 256

    def kernel(expert_ref, own_ref, other_ref, *refs):
        copies = {}
        if keep:
            up_hbm, down_hbm, out_ref, over_ref, up_ref, down_ref, tokens_ref, hidden_ref, sems = refs
            for c in range(up_steps):
                for half in range(2):
                    columns = pl.ds(half * hidden_dim + c * width, width)
                    copies["up", c, half] = pltpu.make_async_copy(
                        up_hbm.at[0, :, columns], up_ref.at[:, columns], sems.at[2 * c + half]
                    )
            for c in range(out_steps):
                columns = pl.ds(c * out_width, out_width)
                copies["down", c] = pltpu.make_async_copy(
                    down_hbm.at[0, :, columns], down_ref.at[:, columns], sems.at[2 * up_steps + c]
                )
            for copy in copies.values():
                copy.start()
        else:
            up_ref, down_ref, out_ref, over_ref, tokens_ref, hidden_ref = refs

        def arrive(*name):
            if keep:
                copies[name].wait()

        token_refs = [own_ref, other_ref]
        routing = stacked([ref[:, model_dim:] for ref in token_refs]).astype(jnp.float32)
        wanted = expert_ref[0].astype(jnp.float32)
        match = jnp.zeros((rows, 1), jnp.float32)
        gates = [jnp.zeros((rows, 1), jnp.float32)] * 3
        for k in range(top_count):
            hit = routing[:, k : k + 1] == wanted
            match = jnp.where(hit, 1.0, match)
            gates = [
                jnp.where(hit, routing[:, i * top_count + k : i * top_count + k + 1], gate)
                for i, gate in enumerate(gates, 1)
            ]
        lane = lax.broadcasted_iota(jnp.int32, (rows, slots), 1)
        match = jnp.broadcast_to(match, (rows, slots))
        earlier = (
            lax.broadcasted_iota(jnp.int32, (strip, strip), 0)
            > lax.broadcasted_iota(jnp.int32, (strip, strip), 1)
        ).astype(jnp.bfloat16)
        ranks, before = [], jnp.zeros((1, slots), jnp.float32)
        for start in range(0, rows, strip):
            piece = match[start : start + strip]
            ranks.append(
                before
                + jnp.dot(earlier, piece.astype(jnp.bfloat16), preferred_element_type=jnp.float32)
            )
            before = before + jnp.sum(piece, axis=0, keepdims=True)
        rank = stacked(ranks)
        choice = jnp.where(rank == lane.astype(jnp.float32), match, 0.0)
        pick = choice.T.astype(jnp.bfloat16)
        place = choice.astype(jnp.bfloat16)
        gate_columns = jnp.where(
            lane == 0, gates[0], jnp.where(lane == 1, gates[1], jnp.where(lane == 2, gates[2], 0.0))
        ).astype(jnp.bfloat16)
        gate = jnp.sum(
            jnp.dot(pick, gate_columns, preferred_element_type=jnp.float32), axis=1, keepdims=True
        )
        for start in range(0, model_dim, out_width):
            columns = slice(start, start + out_width)
            tokens = stacked([ref[:, columns] for ref in token_refs])
            tokens_ref[:, columns] = jnp.dot(
                pick, tokens, preferred_element_type=jnp.float32
            ).astype(jnp.bfloat16)

        for c in range(up_steps):
            arrive("up", c, 0)
            arrive("up", c, 1)
            start = c * width
            tokens = tokens_ref[...]
            gated = jnp.dot(
                tokens, up_ref[:, start : start + width], preferred_element_type=jnp.float32
            )
            up = jnp.dot(
                tokens,
                up_ref[:, hidden_dim + start : hidden_dim + start + width],
                preferred_element_type=jnp.float32,
            )
            hidden_ref[:, start : start + width] = (gated / (1.0 + jnp.exp(-gated)) * up).astype(
                jnp.bfloat16
            )

        for c in range(out_steps):
            arrive("down", c)
            columns = slice(c * out_width, (c + 1) * out_width)
            result = jnp.dot(
                hidden_ref[...], down_ref[:, columns], preferred_element_type=jnp.float32
            )
            result = (result * gate).astype(jnp.bfloat16)
            sums = jnp.dot(place, result, preferred_element_type=jnp.float32).astype(jnp.bfloat16)
            out_ref[:, columns] = sums[: rows // 2]
            over_ref[:, columns] = sums[rows // 2 :]

    shape = jax.ShapeDtypeStruct((rows // 2, model_dim), jnp.bfloat16)
    kept, scratch = (), []
    if keep:
        kept = (
            pltpu.VMEM((model_dim, double), jnp.bfloat16),
            pltpu.VMEM((hidden_dim, model_dim), jnp.bfloat16),
        )
        scratch = [pltpu.SemaphoreType.DMA((2 * up_steps + out_steps,))]
        weights = [in_hbm(gate_up), in_hbm(down_proj)]
    else:
        weights = [pltpu.with_memory_space_constraint(value, pltpu.VMEM) for value in weights]
    results = pl.pallas_call(
        kernel,
        out_shape=(shape, shape) + kept,
        in_specs=[SMEM, VMEM, VMEM] + [HBM if keep else VMEM] * 2,
        out_specs=(VMEM,) * (2 + len(kept)),
        scratch_shapes=[
            pltpu.VMEM((slots, model_dim), jnp.bfloat16),
            pltpu.VMEM((slots, hidden_dim), jnp.bfloat16),
        ]
        + scratch,
        compiler_params=pltpu.CompilerParams(vmem_limit_bytes=EXPERT_LIMIT),
        cost_estimate=pl.CostEstimate(
            flops=6 * slots * model_dim * hidden_dim,
            bytes_accessed=20 * MEBI,
            transcendentals=slots * hidden_dim,
        ),
        name="run_experts",
    )(expert, own, other, *weights)
    return results[0], results[1], results[2:]


def add_up(parts, cuts, name, work=0):
    rows = sum(cuts)
    model_dim = parts[0][0].shape[1]
    flat = [piece for part in parts for piece in part]
    places = []
    for part in parts:
        start = 0
        for piece in part:
            places.append((start, start + piece.shape[0]))
            start += piece.shape[0]

    def kernel(*refs):
        in_refs, out_refs = refs[: len(flat)], refs[len(flat) :]
        step = 1024
        for start in range(0, model_dim, step):
            columns = slice(start, start + step)
            offset = 0
            for out_ref, cut in zip(out_refs, cuts):
                total = 0.0
                for ref, (low, high) in zip(in_refs, places):
                    if low <= offset and offset + cut <= high:
                        rows_of = slice(offset - low, offset - low + cut)
                        total = total + ref[rows_of, columns].astype(jnp.float32)
                out_ref[:, columns] = total.astype(jnp.bfloat16)
                offset += cut

    return pl.pallas_call(
        kernel,
        out_shape=tuple(jax.ShapeDtypeStruct((cut, model_dim), jnp.bfloat16) for cut in cuts),
        in_specs=[VMEM] * len(flat),
        out_specs=(VMEM,) * len(cuts),
        compiler_params=pltpu.CompilerParams(vmem_limit_bytes=12 * MEBI),
        cost_estimate=pl.CostEstimate(
            flops=work, bytes_accessed=0, transcendentals=0
        ),
        name=name,
    )(*flat)


def finish_attention(
    query, fetched, table, lengths, partial, residual, gain, ids, gates, pages_own
):
    count, page_len, kv_width = fetched.shape
    half = kv_width // 2
    tokens = count * page_len
    requests, model_dim = residual.shape
    rows = query.shape[0]
    scaling = 1.0 / math.sqrt(HEAD_DIMENSION)

    def kernel(q_ref, fetched_ref, table_ref, lengths_ref, sum_ref, top_ref, total_ref, residual_ref, gain_ref, ids_ref, gates_ref, attended_ref, merged_ref, normed_ref, heads_ref):
        blocks = head_blocks(q_ref[...])
        held = tokens_of_pages(table_ref[...], lengths_ref, pages_own, page_len)
        bias = token_bias(held, 0, tokens, page_len)
        keys = fetched_ref[:, :, :half].reshape(tokens, half)
        values = fetched_ref[:, :, half:].reshape(tokens, half)
        scores = masked_scores(blocks, keys, bias, scaling)
        before = top_ref[...]
        shed_top = jnp.max(narrowed(scores, jnp.maximum), axis=1, keepdims=True)
        top = jnp.maximum(before, shed_top)
        kept = jnp.exp(before - top)
        weights = jnp.exp(scores - jnp.concatenate([top] * (tokens // 128), axis=1))
        added = jnp.sum(narrowed(weights, jnp.add), axis=1, keepdims=True)
        total = total_ref[...] * kept + added
        summed = own_head(
            jnp.dot(weights.astype(jnp.bfloat16), values, preferred_element_type=jnp.float32)
        )
        heads_ref[...] = (sum_ref[...] * kept + summed) / total
        square = jnp.zeros((requests, 128), jnp.float32)
        for h in range(HEADS):
            columns = slice(h * 128, (h + 1) * 128)
            attended = heads_ref[pl.ds(h, requests, stride=HEADS), :].astype(jnp.bfloat16)
            attended_ref[:, columns] = attended
            merged = (
                residual_ref[:, columns].astype(jnp.float32) + attended.astype(jnp.float32)
            ).astype(jnp.bfloat16)
            merged_ref[:, columns] = merged
            wide = merged.astype(jnp.float32)
            square = square + wide * wide
        mean = jnp.sum(square, axis=1, keepdims=True) * (1.0 / model_dim)
        inverse = lax.rsqrt(mean + epsilon)
        normed_ref[:, model_dim:] = routing_columns(ids_ref[...], gates_ref[...])
        normed_ref[:, :model_dim] = (
            merged_ref[...].astype(jnp.float32) * inverse * gain_ref[...]
        ).astype(jnp.bfloat16)

    shape = jax.ShapeDtypeStruct((requests, model_dim), jnp.bfloat16)
    return pl.pallas_call(
        kernel,
        out_shape=(shape, shape, jax.ShapeDtypeStruct((requests, model_dim + 128), jnp.bfloat16)),
        in_specs=[VMEM] * 3 + [SMEM] + [VMEM] * 7,
        out_specs=(VMEM,) * 3,
        scratch_shapes=[pltpu.VMEM((rows, 128), jnp.float32)],
        compiler_params=pltpu.CompilerParams(vmem_limit_bytes=16 * MEBI),
        cost_estimate=pl.CostEstimate(
            flops=4 * rows * half * tokens, bytes_accessed=4 * MEBI, transcendentals=rows * tokens
        ),
        name="finish_attention",
    )(query, fetched, table, lengths, *partial, residual, gain, ids, gates)


def local(
    queries,
    new_kv,
    kv_pages,
    page_table,
    lengths,
    shed_slots,
    residual,
    norm_gain,
    expert_ids,
    gate_weights,
    w_gate_up,
    w_down,
):
    count_of_rows, model_dim = queries.shape
    top_count = expert_ids.shape[1]
    layout = Layout(lax.axis_size("pool"), lax.axis_size("dev"))
    capacity = 2 * count_of_rows * top_count // (layout.pool * layout.dev)
    planes = layout.planes

    requested = from_behind(shed_slots, "pool", 1)
    picked = pick_pages(requested, kv_pages)
    fetched = from_behind(picked, "pool", 1)
    queries, expert_ids, picked = lax.optimization_barrier((queries, expert_ids, picked))

    expert = (lax.axis_index("pool") * layout.dev + lax.axis_index("dev")).reshape(1)
    *partial, query = own_attention(queries, new_kv, kv_pages, page_table, lengths)
    attended, merged, normed = finish_attention(
        query,
        fetched,
        page_table,
        lengths,
        partial,
        residual,
        norm_gain.reshape(1, model_dim),
        expert_ids.T,
        gate_weights.T,
        kv_pages.shape[0],
    )

    near = list(range(1, planes // 2 + 1))
    far = [0, *range(planes // 2 + 1, planes)]
    chips = range(0, layout.members, 2)
    blocks = [normed]
    for s in range(1, planes):
        blocks.append(layout.shifted(blocks[s ^ 1], 1) if s & 1 else layout.shifted(normed, s))
    arrived = []
    for s, block in enumerate(blocks):
        ready = [block] * len(chips)
        if 0 < s <= len(near):
            ready = [after(block, part) for part in arrived[0]]
        arrived.append([layout.swapped(rows, chip) for rows, chip in zip(ready, chips)])

    def to_experts(some, tie):
        pieces = [arrived[s][c] for c in range(len(chips)) for s in some]
        if tie is not None:
            pieces[0] = after(pieces[0], tie)
        own = packed(pieces)
        return own, layout.swapped(own, 1), layout.members * len(some) * capacity

    def add_cores(mine, over):
        cuts = [count_of_rows] * (mine.shape[0] // count_of_rows)
        return list(add_up([[mine], [over]], cuts, "add_cores"))

    def to_owners(sums, i):
        pieces = len(sums) // len(chips)
        return [layout.swapped(sums[c * pieces + i], chip) for c, chip in enumerate(chips)]

    def total_of(parts):
        return add_up([[part] for part in parts], [count_of_rows], "add_chips")[0]

    own, other, slots = to_experts(near, blocks[far[-1]])
    mine, over, kept = run_experts(own, other, (w_gate_up, w_down), expert, top_count, slots, True)
    near_mine, near_back = mine, layout.swapped(over, 1)
    own, other, slots = to_experts(far, over)
    near_sums = add_up(
        [[near_mine], [near_back]], [count_of_rows * len(near)] * len(chips), "add_cores"
    )
    other = after(other, near_sums[0])
    mine, over, _ = run_experts(own, other, kept, expert, top_count, slots, False)
    parts = to_owners(near_sums, 0)
    over = after(over, parts[1], parts[2])
    far_sums = add_cores(mine, layout.swapped(over, 1))
    totals = add_up([[part] for part in parts], [count_of_rows] * len(near), "add_chips")
    others = [layout.shifted(total, by) for total, by in list(zip(totals, near))[::-1]]
    for i, by in list(enumerate(far))[:0:-1]:
        others.append(layout.shifted(total_of(to_owners(far_sums, i)), by))
    merged = add_up(
        [[merged]] + [[part] for part in others], [count_of_rows], "add_first", 10**10
    )[0]
    others = [total_of(to_owners(far_sums, 0))]
    total = merged.astype(jnp.float32) + sum(part.astype(jnp.float32) for part in others)
    layer_out = total.astype(jnp.bfloat16)
    return (attended, layer_out)


def solution(mesh):
    return jax.shard_map(
        local,
        mesh=mesh,
        in_specs=(
            P(("pool", "dev"), None),
            P(("pool", "dev"), None),
            P(("pool", "dev"), None, None),
            P(("pool", "dev"), None),
            P(("pool", "dev")),
            P(("pool", "dev")),
            P(("pool", "dev"), None),
            P(),
            P(("pool", "dev"), None),
            P(("pool", "dev"), None),
            P(("pool", "dev"), None, None),
            P(("pool", "dev"), None, None),
        ),
        out_specs=(P(("pool", "dev"), None), P(("pool", "dev"), None)),
        check_vma=False,
    )
```

```python
import math

import jax
import jax.numpy as jnp
from jax import lax
from jax.experimental import pallas as pl
from jax.experimental.pallas import tpu as pltpu
from jax.sharding import PartitionSpec as P

HEAD_DIMENSION = 128
KEY_VALUE_HEADS = 2
QUERY_GROUP_SIZE = 16
HEADS = KEY_VALUE_HEADS * QUERY_GROUP_SIZE

masked_score = -1e30
epsilon = 1e-06
AXES = ("pool", "dev")
VMEM = pl.BlockSpec(memory_space=pltpu.VMEM)
SMEM = pl.BlockSpec(memory_space=pltpu.SMEM)
HBM = pl.BlockSpec(memory_space=pltpu.HBM)
MEBI = 1 << 20
EXPERT_LIMIT = 16 * MEBI


def in_hbm(value):
    return pltpu.with_memory_space_constraint(value, pltpu.HBM)


class Layout:
    def __init__(self, pool, dev):
        self.pool, self.dev = pool, dev
        self.inner = math.gcd(dev, 4)
        self.planes = dev // self.inner
        self.members = pool * self.inner
        self.groups = [
            [self.linear(member, plane) for member in range(self.members)]
            for plane in range(self.planes)
        ]

    def linear(self, member, plane):
        return member // self.inner * self.dev + plane * self.inner + member % self.inner

    def shifted(self, value, by):
        if by == 0:
            return value
        pairs = [
            (self.linear(m, z), self.linear(m, z ^ by))
            for z in range(self.planes)
            for m in range(self.members)
        ]
        with jax.named_scope(f"plane_{by}"):
            return lax.ppermute(value, AXES, pairs)

    def swapped(self, value, by):
        if by == 0:
            return value
        pairs = [
            (self.linear(m, z), self.linear(m ^ by, z))
            for z in range(self.planes)
            for m in range(self.members)
        ]
        with jax.named_scope(f"member_{by}"):
            return lax.ppermute(value, AXES, pairs)


def from_behind(value, axis, by):
    length = lax.axis_size(axis)
    return lax.ppermute(value, axis, [(i, (i + by) % length) for i in range(length)])


def in_fast_memory(value, parts, name):
    rows = value.shape[0] // parts

    def kernel(in_ref, out_ref, sign_ref, sems):
        copies = [
            pltpu.make_async_copy(
                in_ref.at[pl.ds(c * rows, rows)], out_ref.at[pl.ds(c * rows, rows)], sems.at[c]
            )
            for c in range(parts)
        ]
        for copy in copies:
            copy.start()
        sign_ref[...] = jnp.zeros_like(sign_ref)
        for copy in copies:
            copy.wait()

    size = math.prod(value.shape) * 2
    return pl.pallas_call(
        kernel,
        out_shape=(
            pltpu.VMEM(value.shape, value.dtype),
            jax.ShapeDtypeStruct((8, 128), jnp.float32),
        ),
        in_specs=[HBM],
        out_specs=(VMEM, VMEM),
        scratch_shapes=[pltpu.SemaphoreType.DMA((parts,))],
        compiler_params=pltpu.CompilerParams(vmem_limit_bytes=2 * MEBI),
        cost_estimate=pl.CostEstimate(flops=0, bytes_accessed=2 * size, transcendentals=0),
        name=name,
    )(in_hbm(value))


def pick_pages(slots, pages):
    count = slots.shape[0]
    last = pages.shape[0] - 1

    def kernel(slots_ref, pages_ref, out_ref):
        for i in range(count):
            out_ref[i] = pages_ref[jnp.clip(slots_ref[i], 0, last)]

    return pl.pallas_call(
        kernel,
        out_shape=jax.ShapeDtypeStruct((count,) + pages.shape[1:], pages.dtype),
        in_specs=[SMEM, VMEM],
        out_specs=VMEM,
        compiler_params=pltpu.CompilerParams(vmem_limit_bytes=8 * MEBI),
        cost_estimate=pl.CostEstimate(flops=0, bytes_accessed=MEBI, transcendentals=0),
        name="pick_pages",
    )(slots, pages)


def head_blocks(query):
    rows = query.shape[0]
    head = lax.broadcasted_iota(jnp.int32, (rows, HEAD_DIMENSION), 0) % HEADS
    nothing = jnp.zeros_like(query)
    low = head < QUERY_GROUP_SIZE
    return jnp.concatenate([jnp.where(low, query, nothing), jnp.where(low, nothing, query)], axis=1)


def own_head(both):
    rows = both.shape[0]
    head = lax.broadcasted_iota(jnp.int32, (rows, HEAD_DIMENSION), 0) % HEADS
    return jnp.where(
        head < QUERY_GROUP_SIZE, both[:, :HEAD_DIMENSION], both[:, HEAD_DIMENSION:]
    )


def tokens_of_pages(table, lengths_ref, first, page_len):
    count_of_rows, width = table.shape
    page = lax.broadcasted_iota(jnp.int32, (count_of_rows, 128), 1) + first
    row = lax.broadcasted_iota(jnp.int32, (count_of_rows, 128), 0)
    lengths = jnp.zeros((count_of_rows, 128), jnp.int32)
    for r in range(count_of_rows):
        lengths = jnp.where(row == r, lengths_ref[r], lengths)
    held = jnp.zeros((count_of_rows, 128), jnp.float32)
    for p in range(width):
        filled = jnp.clip(lengths - p * page_len, 0, page_len).astype(jnp.float32)
        held = held + jnp.where(table[:, p : p + 1] == page, filled, 0.0)
    return held


def token_bias(held, first_page, tokens, page_len):
    page = lax.broadcasted_iota(jnp.int32, (128, tokens), 0)
    token = lax.broadcasted_iota(jnp.int32, (128, tokens), 1)
    widen = (page == token // page_len + first_page).astype(jnp.bfloat16)
    limit = jnp.dot(held.astype(jnp.bfloat16), widen, preferred_element_type=jnp.float32)
    inside = (token[: held.shape[0]] % page_len).astype(jnp.float32)
    return jnp.where(inside < limit, 0.0, masked_score)


def masked_scores(blocks, keys, bias, scaling):
    scores = lax.dot_general(
        blocks, keys, (((1,), (1,)), ((), ())), preferred_element_type=jnp.float32
    )
    requests, tokens = bias.shape
    return (
        (scores * scaling).reshape(requests, HEADS, tokens) + bias[:, None, :]
    ).reshape(requests * HEADS, tokens)


def narrowed(value, join):
    result = value[:, :128]
    for start in range(128, value.shape[1], 128):
        result = join(result, value[:, start : start + 128])
    return result


def own_attention(queries, new_kv, pages, table, lengths):
    page_count, page_len, kv_width = pages.shape
    requests = new_kv.shape[0]
    rows = requests * HEADS
    half = kv_width // 2
    chunk_pages = 128 * (page_count // 128) // 4
    chunk = chunk_pages * page_len
    chunks = page_count // chunk_pages
    scaling = 1.0 / math.sqrt(HEAD_DIMENSION)

    def kernel(
        queries_hbm,
        new_hbm,
        pages_ref,
        table_hbm,
        lengths_hbm,
        out_ref,
        top_ref,
        sum_ref,
        query_ref,
        s_ref,
        fresh_ref,
        heads_ref,
        flat_ref,
        table_ref,
        lengths_ref,
        sems,
    ):
        copies = [
            pltpu.make_async_copy(queries_hbm, flat_ref, sems.at[0]),
            pltpu.make_async_copy(table_hbm, table_ref, sems.at[1]),
            pltpu.make_async_copy(lengths_hbm, lengths_ref, sems.at[2]),
            pltpu.make_async_copy(new_hbm, fresh_ref.at[pl.ds(0, requests)], sems.at[3]),
        ]
        fresh_ref[requests:] = jnp.zeros_like(fresh_ref[requests:])
        for copy in copies:
            copy.start()
        for copy in copies:
            copy.wait()
        for h in range(HEADS):
            heads_ref[pl.ds(h, requests, stride=HEADS), :] = flat_ref[
                :, h * 128 : (h + 1) * 128
            ].astype(jnp.float32)
        query = heads_ref[...].astype(jnp.bfloat16)
        query_ref[...] = query
        blocks = head_blocks(query)
        held = tokens_of_pages(table_ref[...], lengths_ref, 0, page_len)
        lane = lax.broadcasted_iota(jnp.int32, (requests, 128), 1)
        own = lax.broadcasted_iota(jnp.int32, (requests, 128), 0)
        fresh_bias = jnp.where(lane == own, 0.0, masked_score)
        fresh = masked_scores(blocks, fresh_ref[:, :half], fresh_bias, scaling)
        s_ref[:, chunks * chunk :] = fresh
        top = fresh
        for c in range(chunks):
            keys = pages_ref[c * chunk_pages : (c + 1) * chunk_pages, :, :half].reshape(chunk, half)
            bias = token_bias(held, c * chunk_pages, chunk, page_len)
            scores = masked_scores(blocks, keys, bias, scaling)
            s_ref[:, c * chunk : (c + 1) * chunk] = scores
            top = jnp.maximum(top, narrowed(scores, jnp.maximum))
        top = jnp.max(top, axis=1, keepdims=True)
        weights = jnp.exp(s_ref[:, chunks * chunk :] - top)
        total = weights
        summed = jnp.dot(
            weights.astype(jnp.bfloat16), fresh_ref[:, half:], preferred_element_type=jnp.float32
        )
        for c in range(chunks):
            values = pages_ref[c * chunk_pages : (c + 1) * chunk_pages, :, half:].reshape(chunk, half)
            weights = jnp.exp(s_ref[:, c * chunk : (c + 1) * chunk] - top)
            total = total + narrowed(weights, jnp.add)
            summed = summed + jnp.dot(
                weights.astype(jnp.bfloat16), values, preferred_element_type=jnp.float32
            )
        out_ref[...] = own_head(summed)
        top_ref[...] = jnp.broadcast_to(top, top_ref.shape)
        sum_ref[...] = jnp.broadcast_to(jnp.sum(total, axis=1, keepdims=True), sum_ref.shape)

    shape = jax.ShapeDtypeStruct((rows, 128), jnp.float32)
    return pl.pallas_call(
        kernel,
        out_shape=(shape, shape, shape, jax.ShapeDtypeStruct((rows, 128), jnp.bfloat16)),
        in_specs=[HBM, HBM, VMEM, HBM, HBM],
        out_specs=(VMEM,) * 4,
        scratch_shapes=[
            pltpu.VMEM((rows, chunks * chunk + 128), jnp.float32),
            pltpu.VMEM((128, kv_width), jnp.bfloat16),
            pltpu.VMEM((rows, 128), jnp.float32),
            pltpu.VMEM(queries.shape, jnp.bfloat16),
            pltpu.VMEM(table.shape, jnp.int32),
            pltpu.SMEM(lengths.shape, jnp.int32),
            pltpu.SemaphoreType.DMA((4,)),
        ],
        compiler_params=pltpu.CompilerParams(vmem_limit_bytes=24 * MEBI),
        cost_estimate=pl.CostEstimate(
            flops=4 * rows * half * chunks * chunk,
            bytes_accessed=16 * MEBI,
            transcendentals=rows * chunks * chunk,
        ),
        name="own_attention",
    )(in_hbm(queries), in_hbm(new_kv), pages, in_hbm(table), in_hbm(lengths))


def routing_columns(ids, gates):
    top_count = ids.shape[0]
    high = gates.astype(jnp.bfloat16)
    rest = gates - high.astype(jnp.float32)
    middle = rest.astype(jnp.bfloat16)
    low = (rest - middle.astype(jnp.float32)).astype(jnp.bfloat16)
    source = lax.broadcasted_iota(jnp.int32, (top_count, 128), 0)
    lane = lax.broadcasted_iota(jnp.int32, (top_count, 128), 1)
    columns = 0.0
    for i, part in enumerate((ids.astype(jnp.float32).astype(jnp.bfloat16), high, middle, low)):
        place = (lane == source + i * top_count).astype(jnp.bfloat16)
        columns = columns + lax.dot_general(
            part, place, (((0,), (0,)), ((), ())), preferred_element_type=jnp.float32
        )
    return columns.astype(jnp.bfloat16)


def stacked(parts):
    if len(parts) == 1:
        return parts[0]
    return jnp.concatenate(parts, axis=0)


def packed(parts, *signs):
    rows = sum(part.shape[0] for part in parts)
    columns = parts[0].shape[1]

    def kernel(*refs):
        out_ref, offset = refs[-1], 0
        for ref in refs[: len(parts)]:
            out_ref[offset : offset + ref.shape[0]] = ref[...]
            offset += ref.shape[0]

    return pl.pallas_call(
        kernel,
        out_shape=jax.ShapeDtypeStruct((rows, columns), parts[0].dtype),
        in_specs=[VMEM] * (len(parts) + len(signs)),
        out_specs=VMEM,
        compiler_params=pltpu.CompilerParams(vmem_limit_bytes=12 * MEBI),
        cost_estimate=pl.CostEstimate(flops=0, bytes_accessed=0, transcendentals=0),
        name="packed",
    )(*parts, *signs)


def after(value, *others):
    return lax.optimization_barrier((value, *others))[0]


def run_experts(own, other, weights, expert, top_count, slots, keep):
    rows, model_dim = own.shape
    rows, model_dim = 2 * rows, model_dim - 128
    gate_up, down_proj = weights
    double, hidden_dim = gate_up.shape[-1], down_proj.shape[-2]
    width = 256
    up_steps = hidden_dim // width
    out_width = 1024 if rows <= 512 else 512
    out_steps = model_dim // out_width
    strip = 256

    def kernel(expert_ref, own_ref, other_ref, *refs):
        copies = {}
        if keep:
            up_hbm, down_ref, out_ref, over_ref, up_ref, tokens_ref, hidden_ref, sems = refs
            for c in range(up_steps):
                for half in range(2):
                    columns = pl.ds(half * hidden_dim + c * width, width)
                    copies["up", c, half] = pltpu.make_async_copy(
                        up_hbm.at[0, :, columns], up_ref.at[:, columns], sems.at[2 * c + half]
                    )
            for copy in copies.values():
                copy.start()
        else:
            up_ref, down_ref, out_ref, over_ref, tokens_ref, hidden_ref = refs

        def arrive(*name):
            if keep:
                copies[name].wait()

        token_refs = [own_ref, other_ref]
        routing = stacked([ref[:, model_dim:] for ref in token_refs]).astype(jnp.float32)
        wanted = expert_ref[0].astype(jnp.float32)
        match = jnp.zeros((rows, 1), jnp.float32)
        gates = [jnp.zeros((rows, 1), jnp.float32)] * 3
        for k in range(top_count):
            hit = routing[:, k : k + 1] == wanted
            match = jnp.where(hit, 1.0, match)
            gates = [
                jnp.where(hit, routing[:, i * top_count + k : i * top_count + k + 1], gate)
                for i, gate in enumerate(gates, 1)
            ]
        lane = lax.broadcasted_iota(jnp.int32, (rows, slots), 1)
        match = jnp.broadcast_to(match, (rows, slots))
        earlier = (
            lax.broadcasted_iota(jnp.int32, (strip, strip), 0)
            > lax.broadcasted_iota(jnp.int32, (strip, strip), 1)
        ).astype(jnp.bfloat16)
        ranks, before = [], jnp.zeros((1, slots), jnp.float32)
        for start in range(0, rows, strip):
            piece = match[start : start + strip]
            ranks.append(
                before
                + jnp.dot(earlier, piece.astype(jnp.bfloat16), preferred_element_type=jnp.float32)
            )
            before = before + jnp.sum(piece, axis=0, keepdims=True)
        rank = stacked(ranks)
        choice = jnp.where(rank == lane.astype(jnp.float32), match, 0.0)
        pick = choice.T.astype(jnp.bfloat16)
        place = choice.astype(jnp.bfloat16)
        gate_columns = jnp.where(
            lane == 0, gates[0], jnp.where(lane == 1, gates[1], jnp.where(lane == 2, gates[2], 0.0))
        ).astype(jnp.bfloat16)
        gate = jnp.sum(
            jnp.dot(pick, gate_columns, preferred_element_type=jnp.float32), axis=1, keepdims=True
        )
        for start in range(0, model_dim, out_width):
            columns = slice(start, start + out_width)
            tokens = stacked([ref[:, columns] for ref in token_refs])
            tokens_ref[:, columns] = jnp.dot(
                pick, tokens, preferred_element_type=jnp.float32
            ).astype(jnp.bfloat16)

        for c in range(up_steps):
            arrive("up", c, 0)
            arrive("up", c, 1)
            start = c * width
            tokens = tokens_ref[...]
            gated = jnp.dot(
                tokens, up_ref[:, start : start + width], preferred_element_type=jnp.float32
            )
            up = jnp.dot(
                tokens,
                up_ref[:, hidden_dim + start : hidden_dim + start + width],
                preferred_element_type=jnp.float32,
            )
            hidden_ref[:, start : start + width] = (gated / (1.0 + jnp.exp(-gated)) * up).astype(
                jnp.bfloat16
            )

        for c in range(out_steps):
            columns = slice(c * out_width, (c + 1) * out_width)
            result = jnp.dot(
                hidden_ref[...], down_ref[:, columns], preferred_element_type=jnp.float32
            )
            result = (result * gate).astype(jnp.bfloat16)
            sums = jnp.dot(place, result, preferred_element_type=jnp.float32).astype(jnp.bfloat16)
            out_ref[:, columns] = sums[: rows // 2]
            over_ref[:, columns] = sums[rows // 2 :]

    shape = jax.ShapeDtypeStruct((rows // 2, model_dim), jnp.bfloat16)
    kept, scratch = (), []
    if keep:
        kept = (pltpu.VMEM((model_dim, double), jnp.bfloat16),)
        scratch = [pltpu.SemaphoreType.DMA((2 * up_steps,))]
        gate_up = in_hbm(gate_up)
    results = pl.pallas_call(
        kernel,
        out_shape=(shape, shape) + kept,
        in_specs=[SMEM, VMEM, VMEM, HBM if keep else VMEM, VMEM],
        out_specs=(VMEM,) * (2 + len(kept)),
        scratch_shapes=[
            pltpu.VMEM((slots, model_dim), jnp.bfloat16),
            pltpu.VMEM((slots, hidden_dim), jnp.bfloat16),
        ]
        + scratch,
        compiler_params=pltpu.CompilerParams(vmem_limit_bytes=EXPERT_LIMIT),
        cost_estimate=pl.CostEstimate(
            flops=6 * slots * model_dim * hidden_dim,
            bytes_accessed=20 * MEBI,
            transcendentals=slots * hidden_dim,
        ),
        name="run_experts",
    )(expert, own, other, gate_up, down_proj)
    return results[0], results[1], results[2:]


def add_up(parts, cuts, name, work=0):
    rows = sum(cuts)
    model_dim = parts[0][0].shape[1]
    flat = [piece for part in parts for piece in part]
    places = []
    for part in parts:
        start = 0
        for piece in part:
            places.append((start, start + piece.shape[0]))
            start += piece.shape[0]

    def kernel(*refs):
        in_refs, out_refs = refs[: len(flat)], refs[len(flat) :]
        step = 1024
        for start in range(0, model_dim, step):
            columns = slice(start, start + step)
            offset = 0
            for out_ref, cut in zip(out_refs, cuts):
                total = 0.0
                for ref, (low, high) in zip(in_refs, places):
                    if low <= offset and offset + cut <= high:
                        rows_of = slice(offset - low, offset - low + cut)
                        total = total + ref[rows_of, columns].astype(jnp.float32)
                out_ref[:, columns] = total.astype(jnp.bfloat16)
                offset += cut

    return pl.pallas_call(
        kernel,
        out_shape=tuple(jax.ShapeDtypeStruct((cut, model_dim), jnp.bfloat16) for cut in cuts),
        in_specs=[VMEM] * len(flat),
        out_specs=(VMEM,) * len(cuts),
        compiler_params=pltpu.CompilerParams(vmem_limit_bytes=12 * MEBI),
        cost_estimate=pl.CostEstimate(
            flops=work, bytes_accessed=0, transcendentals=0
        ),
        name=name,
    )(*flat)


def finish_attention(
    query, fetched, table, lengths, partial, residual, gain, ids, gates, pages_own
):
    count, page_len, kv_width = fetched.shape
    half = kv_width // 2
    tokens = count * page_len
    requests, model_dim = residual.shape
    rows = query.shape[0]
    scaling = 1.0 / math.sqrt(HEAD_DIMENSION)

    def kernel(q_ref, fetched_ref, table_ref, lengths_ref, sum_ref, top_ref, total_ref, residual_ref, gain_ref, ids_ref, gates_ref, attended_ref, merged_ref, normed_ref, heads_ref):
        blocks = head_blocks(q_ref[...])
        held = tokens_of_pages(table_ref[...], lengths_ref, pages_own, page_len)
        bias = token_bias(held, 0, tokens, page_len)
        keys = fetched_ref[:, :, :half].reshape(tokens, half)
        values = fetched_ref[:, :, half:].reshape(tokens, half)
        scores = masked_scores(blocks, keys, bias, scaling)
        before = top_ref[...]
        shed_top = jnp.max(narrowed(scores, jnp.maximum), axis=1, keepdims=True)
        top = jnp.maximum(before, shed_top)
        kept = jnp.exp(before - top)
        weights = jnp.exp(scores - jnp.concatenate([top] * (tokens // 128), axis=1))
        added = jnp.sum(narrowed(weights, jnp.add), axis=1, keepdims=True)
        total = total_ref[...] * kept + added
        summed = own_head(
            jnp.dot(weights.astype(jnp.bfloat16), values, preferred_element_type=jnp.float32)
        )
        heads_ref[...] = (sum_ref[...] * kept + summed) / total
        square = jnp.zeros((requests, 128), jnp.float32)
        for h in range(HEADS):
            columns = slice(h * 128, (h + 1) * 128)
            attended = heads_ref[pl.ds(h, requests, stride=HEADS), :].astype(jnp.bfloat16)
            attended_ref[:, columns] = attended
            merged = (
                residual_ref[:, columns].astype(jnp.float32) + attended.astype(jnp.float32)
            ).astype(jnp.bfloat16)
            merged_ref[:, columns] = merged
            wide = merged.astype(jnp.float32)
            square = square + wide * wide
        mean = jnp.sum(square, axis=1, keepdims=True) * (1.0 / model_dim)
        inverse = lax.rsqrt(mean + epsilon)
        normed_ref[:, model_dim:] = routing_columns(ids_ref[...], gates_ref[...])
        normed_ref[:, :model_dim] = (
            merged_ref[...].astype(jnp.float32) * inverse * gain_ref[...]
        ).astype(jnp.bfloat16)

    shape = jax.ShapeDtypeStruct((requests, model_dim), jnp.bfloat16)
    return pl.pallas_call(
        kernel,
        out_shape=(shape, shape, jax.ShapeDtypeStruct((requests, model_dim + 128), jnp.bfloat16)),
        in_specs=[VMEM] * 3 + [SMEM] + [VMEM] * 7,
        out_specs=(VMEM,) * 3,
        scratch_shapes=[pltpu.VMEM((rows, 128), jnp.float32)],
        compiler_params=pltpu.CompilerParams(vmem_limit_bytes=16 * MEBI),
        cost_estimate=pl.CostEstimate(
            flops=4 * rows * half * tokens, bytes_accessed=4 * MEBI, transcendentals=rows * tokens
        ),
        name="finish_attention",
    )(query, fetched, table, lengths, *partial, residual, gain, ids, gates)


def local(
    queries,
    new_kv,
    kv_pages,
    page_table,
    lengths,
    shed_slots,
    residual,
    norm_gain,
    expert_ids,
    gate_weights,
    w_gate_up,
    w_down,
):
    count_of_rows, model_dim = queries.shape
    top_count = expert_ids.shape[1]
    layout = Layout(lax.axis_size("pool"), lax.axis_size("dev"))
    capacity = 2 * count_of_rows * top_count // (layout.pool * layout.dev)
    planes = layout.planes

    requested = from_behind(shed_slots, "pool", 1)
    fast_pages, _ = in_fast_memory(kv_pages, 4, "pages_in")
    picked = pick_pages(requested, fast_pages)
    fetched = from_behind(picked, "pool", 1)
    queries, expert_ids, picked = lax.optimization_barrier((queries, expert_ids, picked))

    expert = (lax.axis_index("pool") * layout.dev + lax.axis_index("dev")).reshape(1)
    *partial, query = own_attention(queries, new_kv, fast_pages, page_table, lengths)
    attended, merged, normed = finish_attention(
        query,
        fetched,
        page_table,
        lengths,
        partial,
        residual,
        norm_gain.reshape(1, model_dim),
        expert_ids.T,
        gate_weights.T,
        kv_pages.shape[0],
    )

    near = list(range(1, planes // 2 + 1))
    far = [0, *range(planes // 2 + 1, planes)]
    chips = range(0, layout.members, 2)
    blocks = [normed]
    for s in range(1, planes):
        blocks.append(layout.shifted(blocks[s ^ 1], 1) if s & 1 else layout.shifted(normed, s))
    arrived = []
    for s, block in enumerate(blocks):
        ready = [block] * len(chips)
        if 0 < s <= len(near):
            ready = [after(block, part) for part in arrived[0]]
        arrived.append([layout.swapped(rows, chip) for rows, chip in zip(ready, chips)])

    def to_experts(some, tie, *signs):
        pieces = [arrived[s][c] for c in range(len(chips)) for s in some]
        pieces[0] = after(pieces[0], tie)
        own = packed(pieces, *signs)
        return own, layout.swapped(own, 1), layout.members * len(some) * capacity

    def add_cores(mine, over):
        cuts = [count_of_rows] * (mine.shape[0] // count_of_rows)
        return list(add_up([[mine], [over]], cuts, "add_cores"))

    def to_owners(sums, i):
        pieces = len(sums) // len(chips)
        return [layout.swapped(sums[c * pieces + i], chip) for c, chip in enumerate(chips)]

    def total_of(parts):
        return add_up([[part] for part in parts], [count_of_rows], "add_chips")[0]

    down, sign = in_fast_memory(after(w_down[0], blocks[far[-1]]), 4, "weights_in")
    own, other, slots = to_experts(near, blocks[far[-1]], sign)
    mine, over, (up,) = run_experts(own, other, (w_gate_up, down), expert, top_count, slots, True)
    near_mine, near_back = mine, layout.swapped(over, 1)
    own, other, slots = to_experts(far, over)
    near_sums = add_up(
        [[near_mine], [near_back]], [count_of_rows * len(near)] * len(chips), "add_cores"
    )
    other = after(other, near_sums[0])
    mine, over, _ = run_experts(own, other, (up, down), expert, top_count, slots, False)
    parts = to_owners(near_sums, 0)
    over = after(over, parts[1], parts[2])
    far_sums = add_cores(mine, layout.swapped(over, 1))
    totals = add_up([[part] for part in parts], [count_of_rows] * len(near), "add_chips")
    last = to_owners(far_sums, 0)
    others = []
    for total, by in list(zip(totals, near))[::-1]:
        others.append(layout.shifted(after(total, last[1]) if by == 1 else total, by))
    for i, by in list(enumerate(far))[:0:-1]:
        others.append(layout.shifted(total_of(to_owners(far_sums, i)), by))
    merged = add_up(
        [[merged]] + [[part] for part in others], [count_of_rows], "add_first", 10**10
    )[0]
    others = [total_of(last)]
    total = merged.astype(jnp.float32) + sum(part.astype(jnp.float32) for part in others)
    layer_out = total.astype(jnp.bfloat16)
    return (attended, layer_out)


def solution(mesh):
    return jax.shard_map(
        local,
        mesh=mesh,
        in_specs=(
            P(("pool", "dev"), None),
            P(("pool", "dev"), None),
            P(("pool", "dev"), None, None),
            P(("pool", "dev"), None),
            P(("pool", "dev")),
            P(("pool", "dev")),
            P(("pool", "dev"), None),
            P(),
            P(("pool", "dev"), None),
            P(("pool", "dev"), None),
            P(("pool", "dev"), None, None),
            P(("pool", "dev"), None, None),
        ),
        out_specs=(P(("pool", "dev"), None), P(("pool", "dev"), None)),
        check_vma=False,
    )
```

```python
import math

import jax
import jax.numpy as jnp
from jax import lax
from jax.experimental import pallas as pl
from jax.experimental.pallas import tpu as pltpu
from jax.sharding import PartitionSpec as P

HEAD_DIMENSION = 128
KEY_VALUE_HEADS = 2
QUERY_GROUP_SIZE = 16
HEADS = KEY_VALUE_HEADS * QUERY_GROUP_SIZE

masked_score = -1e30
epsilon = 1e-06
AXES = ("pool", "dev")
VMEM = pl.BlockSpec(memory_space=pltpu.VMEM)
SMEM = pl.BlockSpec(memory_space=pltpu.SMEM)
HBM = pl.BlockSpec(memory_space=pltpu.HBM)
MEBI = 1 << 20
EXPERT_LIMIT = 16 * MEBI


def in_hbm(value):
    return pltpu.with_memory_space_constraint(value, pltpu.HBM)


class Layout:
    def __init__(self, pool, dev):
        self.pool, self.dev = pool, dev
        self.inner = math.gcd(dev, 4)
        self.planes = dev // self.inner
        self.members = pool * self.inner
        self.groups = [
            [self.linear(member, plane) for member in range(self.members)]
            for plane in range(self.planes)
        ]

    def linear(self, member, plane):
        return member // self.inner * self.dev + plane * self.inner + member % self.inner

    def shifted(self, value, by):
        if by == 0:
            return value
        pairs = [
            (self.linear(m, z), self.linear(m, z ^ by))
            for z in range(self.planes)
            for m in range(self.members)
        ]
        with jax.named_scope(f"plane_{by}"):
            return lax.ppermute(value, AXES, pairs)

    def swapped(self, value, by):
        if by == 0:
            return value
        pairs = [
            (self.linear(m, z), self.linear(m ^ by, z))
            for z in range(self.planes)
            for m in range(self.members)
        ]
        with jax.named_scope(f"member_{by}"):
            return lax.ppermute(value, AXES, pairs)


def from_behind(value, axis, by):
    length = lax.axis_size(axis)
    return lax.ppermute(value, axis, [(i, (i + by) % length) for i in range(length)])


def pick_pages(slots, pages):
    count = slots.shape[0]
    last = pages.shape[0] - 1

    def kernel(slots_ref, pages_ref, out_ref, sems):
        copies = []
        for i in range(count):
            page = jnp.clip(slots_ref[i], 0, last)
            copies.append(pltpu.make_async_copy(pages_ref.at[page], out_ref.at[i], sems.at[i]))
            copies[-1].start()
        for copy in copies:
            copy.wait()

    return pl.pallas_call(
        kernel,
        out_shape=jax.ShapeDtypeStruct((count,) + pages.shape[1:], pages.dtype),
        in_specs=[SMEM, HBM],
        out_specs=VMEM,
        scratch_shapes=[pltpu.SemaphoreType.DMA((count,))],
        compiler_params=pltpu.CompilerParams(vmem_limit_bytes=4 * MEBI),
        cost_estimate=pl.CostEstimate(flops=0, bytes_accessed=MEBI, transcendentals=0),
        name="pick_pages",
    )(slots, in_hbm(pages))


def head_blocks(query):
    rows = query.shape[0]
    head = lax.broadcasted_iota(jnp.int32, (rows, HEAD_DIMENSION), 0) % HEADS
    nothing = jnp.zeros_like(query)
    low = head < QUERY_GROUP_SIZE
    return jnp.concatenate([jnp.where(low, query, nothing), jnp.where(low, nothing, query)], axis=1)


def own_head(both):
    rows = both.shape[0]
    head = lax.broadcasted_iota(jnp.int32, (rows, HEAD_DIMENSION), 0) % HEADS
    return jnp.where(
        head < QUERY_GROUP_SIZE, both[:, :HEAD_DIMENSION], both[:, HEAD_DIMENSION:]
    )


def tokens_of_pages(table, lengths_ref, first, page_len):
    count_of_rows, width = table.shape
    page = lax.broadcasted_iota(jnp.int32, (count_of_rows, 128), 1) + first
    row = lax.broadcasted_iota(jnp.int32, (count_of_rows, 128), 0)
    lengths = jnp.zeros((count_of_rows, 128), jnp.int32)
    for r in range(count_of_rows):
        lengths = jnp.where(row == r, lengths_ref[r], lengths)
    held = jnp.zeros((count_of_rows, 128), jnp.float32)
    for p in range(width):
        filled = jnp.clip(lengths - p * page_len, 0, page_len).astype(jnp.float32)
        held = held + jnp.where(table[:, p : p + 1] == page, filled, 0.0)
    return held


def token_bias(held, first_page, tokens, page_len):
    page = lax.broadcasted_iota(jnp.int32, (128, tokens), 0)
    token = lax.broadcasted_iota(jnp.int32, (128, tokens), 1)
    widen = (page == token // page_len + first_page).astype(jnp.bfloat16)
    limit = jnp.dot(held.astype(jnp.bfloat16), widen, preferred_element_type=jnp.float32)
    inside = (token[: held.shape[0]] % page_len).astype(jnp.float32)
    return jnp.where(inside < limit, 0.0, masked_score)


def masked_scores(blocks, keys, bias, scaling):
    scores = lax.dot_general(
        blocks, keys, (((1,), (1,)), ((), ())), preferred_element_type=jnp.float32
    )
    requests, tokens = bias.shape
    return (
        (scores * scaling).reshape(requests, HEADS, tokens) + bias[:, None, :]
    ).reshape(requests * HEADS, tokens)


def narrowed(value, join):
    result = value[:, :128]
    for start in range(128, value.shape[1], 128):
        result = join(result, value[:, start : start + 128])
    return result


def own_attention(queries, new_kv, pages, table, lengths):
    page_count, page_len, kv_width = pages.shape
    requests = new_kv.shape[0]
    rows = requests * HEADS
    half = kv_width // 2
    chunk_pages = 128 * (page_count // 128) // 4
    chunk = chunk_pages * page_len
    chunks = page_count // chunk_pages
    scaling = 1.0 / math.sqrt(HEAD_DIMENSION)

    def kernel(
        queries_hbm,
        new_hbm,
        pages_hbm,
        table_hbm,
        lengths_hbm,
        out_ref,
        top_ref,
        sum_ref,
        query_ref,
        s_ref,
        fresh_ref,
        heads_ref,
        flat_ref,
        pages_ref,
        table_ref,
        lengths_ref,
        sems,
    ):
        page_copies = [
            pltpu.make_async_copy(
                pages_hbm.at[pl.ds(c * chunk_pages, chunk_pages)],
                pages_ref.at[pl.ds(c * chunk_pages, chunk_pages)],
                sems.at[4 + c],
            )
            for c in range(chunks)
        ]
        copies = [
            pltpu.make_async_copy(queries_hbm, flat_ref, sems.at[0]),
            pltpu.make_async_copy(table_hbm, table_ref, sems.at[1]),
            pltpu.make_async_copy(lengths_hbm, lengths_ref, sems.at[2]),
            pltpu.make_async_copy(new_hbm, fresh_ref.at[pl.ds(0, requests)], sems.at[3]),
        ]
        fresh_ref[requests:] = jnp.zeros_like(fresh_ref[requests:])
        for copy in copies + page_copies:
            copy.start()
        for copy in copies:
            copy.wait()
        for h in range(HEADS):
            heads_ref[pl.ds(h, requests, stride=HEADS), :] = flat_ref[
                :, h * 128 : (h + 1) * 128
            ].astype(jnp.float32)
        query = heads_ref[...].astype(jnp.bfloat16)
        query_ref[...] = query
        blocks = head_blocks(query)
        held = tokens_of_pages(table_ref[...], lengths_ref, 0, page_len)
        lane = lax.broadcasted_iota(jnp.int32, (requests, 128), 1)
        own = lax.broadcasted_iota(jnp.int32, (requests, 128), 0)
        fresh_bias = jnp.where(lane == own, 0.0, masked_score)
        fresh = masked_scores(blocks, fresh_ref[:, :half], fresh_bias, scaling)
        s_ref[:, chunks * chunk :] = fresh
        top = fresh
        for c in range(chunks):
            page_copies[c].wait()
            keys = pages_ref[c * chunk_pages : (c + 1) * chunk_pages, :, :half].reshape(chunk, half)
            bias = token_bias(held, c * chunk_pages, chunk, page_len)
            scores = masked_scores(blocks, keys, bias, scaling)
            s_ref[:, c * chunk : (c + 1) * chunk] = scores
            top = jnp.maximum(top, narrowed(scores, jnp.maximum))
        top = jnp.max(top, axis=1, keepdims=True)
        weights = jnp.exp(s_ref[:, chunks * chunk :] - top)
        total = weights
        summed = jnp.dot(
            weights.astype(jnp.bfloat16), fresh_ref[:, half:], preferred_element_type=jnp.float32
        )
        for c in range(chunks):
            values = pages_ref[c * chunk_pages : (c + 1) * chunk_pages, :, half:].reshape(chunk, half)
            weights = jnp.exp(s_ref[:, c * chunk : (c + 1) * chunk] - top)
            total = total + narrowed(weights, jnp.add)
            summed = summed + jnp.dot(
                weights.astype(jnp.bfloat16), values, preferred_element_type=jnp.float32
            )
        out_ref[...] = own_head(summed)
        top_ref[...] = jnp.broadcast_to(top, top_ref.shape)
        sum_ref[...] = jnp.broadcast_to(jnp.sum(total, axis=1, keepdims=True), sum_ref.shape)

    shape = jax.ShapeDtypeStruct((rows, 128), jnp.float32)
    return pl.pallas_call(
        kernel,
        out_shape=(shape, shape, shape, jax.ShapeDtypeStruct((rows, 128), jnp.bfloat16)),
        in_specs=[HBM] * 5,
        out_specs=(VMEM,) * 4,
        scratch_shapes=[
            pltpu.VMEM((rows, chunks * chunk + 128), jnp.float32),
            pltpu.VMEM((128, kv_width), jnp.bfloat16),
            pltpu.VMEM((rows, 128), jnp.float32),
            pltpu.VMEM(queries.shape, jnp.bfloat16),
            pltpu.VMEM(pages.shape, jnp.bfloat16),
            pltpu.VMEM(table.shape, jnp.int32),
            pltpu.SMEM(lengths.shape, jnp.int32),
            pltpu.SemaphoreType.DMA((4 + chunks,)),
        ],
        compiler_params=pltpu.CompilerParams(vmem_limit_bytes=24 * MEBI),
        cost_estimate=pl.CostEstimate(
            flops=4 * rows * half * chunks * chunk,
            bytes_accessed=16 * MEBI,
            transcendentals=rows * chunks * chunk,
        ),
        name="own_attention",
    )(*[in_hbm(value) for value in (queries, new_kv, pages, table, lengths)])


def routing_columns(ids, gates):
    top_count = ids.shape[0]
    high = gates.astype(jnp.bfloat16)
    rest = gates - high.astype(jnp.float32)
    middle = rest.astype(jnp.bfloat16)
    low = (rest - middle.astype(jnp.float32)).astype(jnp.bfloat16)
    source = lax.broadcasted_iota(jnp.int32, (top_count, 128), 0)
    lane = lax.broadcasted_iota(jnp.int32, (top_count, 128), 1)
    columns = 0.0
    for i, part in enumerate((ids.astype(jnp.float32).astype(jnp.bfloat16), high, middle, low)):
        place = (lane == source + i * top_count).astype(jnp.bfloat16)
        columns = columns + lax.dot_general(
            part, place, (((0,), (0,)), ((), ())), preferred_element_type=jnp.float32
        )
    return columns.astype(jnp.bfloat16)


def stacked(parts):
    if len(parts) == 1:
        return parts[0]
    return jnp.concatenate(parts, axis=0)


def packed(parts, work=0):
    if len(parts) == 1 and not work:
        return parts[0]
    rows = sum(part.shape[0] for part in parts)
    columns = parts[0].shape[1]

    def kernel(*refs):
        out_ref, offset = refs[-1], 0
        for ref in refs[:-1]:
            out_ref[offset : offset + ref.shape[0]] = ref[...]
            offset += ref.shape[0]

    return pl.pallas_call(
        kernel,
        out_shape=jax.ShapeDtypeStruct((rows, columns), parts[0].dtype),
        in_specs=[VMEM] * len(parts),
        out_specs=VMEM,
        compiler_params=pltpu.CompilerParams(vmem_limit_bytes=12 * MEBI),
        cost_estimate=pl.CostEstimate(flops=work, bytes_accessed=0, transcendentals=0),
        name="packed",
    )(*parts)


def after(value, *others):
    return lax.optimization_barrier((value, *others))[0]


def run_experts(own, other, weights, expert, top_count, slots, keep):
    rows, model_dim = own.shape
    rows, model_dim = 2 * rows, model_dim - 128
    gate_up, down_proj = weights
    double, hidden_dim = gate_up.shape[-1], down_proj.shape[-2]
    width = 256
    up_steps = hidden_dim // width
    out_width = 1024 if rows <= 512 else 512
    out_steps = model_dim // out_width
    strip = 256

    def kernel(expert_ref, own_ref, other_ref, *refs):
        copies = {}
        if keep:
            up_hbm, down_hbm, out_ref, over_ref, up_ref, down_ref, tokens_ref, hidden_ref, sems = refs
            for c in range(up_steps):
                for half in range(2):
                    columns = pl.ds(half * hidden_dim + c * width, width)
                    copies["up", c, half] = pltpu.make_async_copy(
                        up_hbm.at[0, :, columns], up_ref.at[:, columns], sems.at[2 * c + half]
                    )
            for c in range(out_steps):
                columns = pl.ds(c * out_width, out_width)
                copies["down", c] = pltpu.make_async_copy(
                    down_hbm.at[0, :, columns], down_ref.at[:, columns], sems.at[2 * up_steps + c]
                )
            for copy in copies.values():
                copy.start()
        else:
            up_ref, down_ref, out_ref, over_ref, tokens_ref, hidden_ref = refs

        def arrive(*name):
            if keep:
                copies[name].wait()

        token_refs = [own_ref, other_ref]
        routing = stacked([ref[:, model_dim:] for ref in token_refs]).astype(jnp.float32)
        wanted = expert_ref[0].astype(jnp.float32)
        match = jnp.zeros((rows, 1), jnp.float32)
        gates = [jnp.zeros((rows, 1), jnp.float32)] * 3
        for k in range(top_count):
            hit = routing[:, k : k + 1] == wanted
            match = jnp.where(hit, 1.0, match)
            gates = [
                jnp.where(hit, routing[:, i * top_count + k : i * top_count + k + 1], gate)
                for i, gate in enumerate(gates, 1)
            ]
        lane = lax.broadcasted_iota(jnp.int32, (rows, slots), 1)
        match = jnp.broadcast_to(match, (rows, slots))
        earlier = (
            lax.broadcasted_iota(jnp.int32, (strip, strip), 0)
            > lax.broadcasted_iota(jnp.int32, (strip, strip), 1)
        ).astype(jnp.bfloat16)
        ranks, before = [], jnp.zeros((1, slots), jnp.float32)
        for start in range(0, rows, strip):
            piece = match[start : start + strip]
            ranks.append(
                before
                + jnp.dot(earlier, piece.astype(jnp.bfloat16), preferred_element_type=jnp.float32)
            )
            before = before + jnp.sum(piece, axis=0, keepdims=True)
        rank = stacked(ranks)
        choice = jnp.where(rank == lane.astype(jnp.float32), match, 0.0)
        pick = choice.T.astype(jnp.bfloat16)
        place = choice.astype(jnp.bfloat16)
        gate_columns = jnp.where(
            lane == 0, gates[0], jnp.where(lane == 1, gates[1], jnp.where(lane == 2, gates[2], 0.0))
        ).astype(jnp.bfloat16)
        gate = jnp.sum(
            jnp.dot(pick, gate_columns, preferred_element_type=jnp.float32), axis=1, keepdims=True
        )
        for start in range(0, model_dim, out_width):
            columns = slice(start, start + out_width)
            tokens = stacked([ref[:, columns] for ref in token_refs])
            tokens_ref[:, columns] = jnp.dot(
                pick, tokens, preferred_element_type=jnp.float32
            ).astype(jnp.bfloat16)

        for c in range(up_steps):
            arrive("up", c, 0)
            arrive("up", c, 1)
            start = c * width
            tokens = tokens_ref[...]
            gated = jnp.dot(
                tokens, up_ref[:, start : start + width], preferred_element_type=jnp.float32
            )
            up = jnp.dot(
                tokens,
                up_ref[:, hidden_dim + start : hidden_dim + start + width],
                preferred_element_type=jnp.float32,
            )
            hidden_ref[:, start : start + width] = (gated / (1.0 + jnp.exp(-gated)) * up).astype(
                jnp.bfloat16
            )

        for c in range(out_steps):
            arrive("down", c)
            columns = slice(c * out_width, (c + 1) * out_width)
            result = jnp.dot(
                hidden_ref[...], down_ref[:, columns], preferred_element_type=jnp.float32
            )
            result = (result * gate).astype(jnp.bfloat16)
            sums = jnp.dot(place, result, preferred_element_type=jnp.float32).astype(jnp.bfloat16)
            out_ref[:, columns] = sums[: rows // 2]
            over_ref[:, columns] = sums[rows // 2 :]

    shape = jax.ShapeDtypeStruct((rows // 2, model_dim), jnp.bfloat16)
    kept, scratch = (), []
    if keep:
        kept = (
            pltpu.VMEM((model_dim, double), jnp.bfloat16),
            pltpu.VMEM((hidden_dim, model_dim), jnp.bfloat16),
        )
        scratch = [pltpu.SemaphoreType.DMA((2 * up_steps + out_steps,))]
        weights = [in_hbm(gate_up), in_hbm(down_proj)]
    else:
        weights = [pltpu.with_memory_space_constraint(value, pltpu.VMEM) for value in weights]
    results = pl.pallas_call(
        kernel,
        out_shape=(shape, shape) + kept,
        in_specs=[SMEM, VMEM, VMEM] + [HBM if keep else VMEM] * 2,
        out_specs=(VMEM,) * (2 + len(kept)),
        scratch_shapes=[
            pltpu.VMEM((slots, model_dim), jnp.bfloat16),
            pltpu.VMEM((slots, hidden_dim), jnp.bfloat16),
        ]
        + scratch,
        compiler_params=pltpu.CompilerParams(vmem_limit_bytes=EXPERT_LIMIT),
        cost_estimate=pl.CostEstimate(
            flops=6 * slots * model_dim * hidden_dim,
            bytes_accessed=20 * MEBI,
            transcendentals=slots * hidden_dim,
        ),
        name="run_experts",
    )(expert, own, other, *weights)
    return results[0], results[1], results[2:]


def add_up(parts, cuts, name, work=0):
    rows = sum(cuts)
    model_dim = parts[0][0].shape[1]
    flat = [piece for part in parts for piece in part]
    places = []
    for part in parts:
        start = 0
        for piece in part:
            places.append((start, start + piece.shape[0]))
            start += piece.shape[0]

    def kernel(*refs):
        in_refs, out_refs = refs[: len(flat)], refs[len(flat) :]
        step = 1024
        for start in range(0, model_dim, step):
            columns = slice(start, start + step)
            offset = 0
            for out_ref, cut in zip(out_refs, cuts):
                total = 0.0
                for ref, (low, high) in zip(in_refs, places):
                    if low <= offset and offset + cut <= high:
                        rows_of = slice(offset - low, offset - low + cut)
                        total = total + ref[rows_of, columns].astype(jnp.float32)
                out_ref[:, columns] = total.astype(jnp.bfloat16)
                offset += cut

    return pl.pallas_call(
        kernel,
        out_shape=tuple(jax.ShapeDtypeStruct((cut, model_dim), jnp.bfloat16) for cut in cuts),
        in_specs=[VMEM] * len(flat),
        out_specs=(VMEM,) * len(cuts),
        compiler_params=pltpu.CompilerParams(vmem_limit_bytes=12 * MEBI),
        cost_estimate=pl.CostEstimate(
            flops=work, bytes_accessed=0, transcendentals=0
        ),
        name=name,
    )(*flat)


def finish_attention(
    query, fetched, table, lengths, partial, residual, gain, ids, gates, pages_own
):
    count, page_len, kv_width = fetched.shape
    half = kv_width // 2
    tokens = count * page_len
    requests, model_dim = residual.shape
    rows = query.shape[0]
    scaling = 1.0 / math.sqrt(HEAD_DIMENSION)

    def kernel(q_ref, fetched_ref, table_ref, lengths_ref, sum_ref, top_ref, total_ref, residual_ref, gain_ref, ids_ref, gates_ref, attended_ref, merged_ref, normed_ref, heads_ref):
        blocks = head_blocks(q_ref[...])
        held = tokens_of_pages(table_ref[...], lengths_ref, pages_own, page_len)
        bias = token_bias(held, 0, tokens, page_len)
        keys = fetched_ref[:, :, :half].reshape(tokens, half)
        values = fetched_ref[:, :, half:].reshape(tokens, half)
        scores = masked_scores(blocks, keys, bias, scaling)
        before = top_ref[...]
        shed_top = jnp.max(narrowed(scores, jnp.maximum), axis=1, keepdims=True)
        top = jnp.maximum(before, shed_top)
        kept = jnp.exp(before - top)
        weights = jnp.exp(scores - jnp.concatenate([top] * (tokens // 128), axis=1))
        added = jnp.sum(narrowed(weights, jnp.add), axis=1, keepdims=True)
        total = total_ref[...] * kept + added
        summed = own_head(
            jnp.dot(weights.astype(jnp.bfloat16), values, preferred_element_type=jnp.float32)
        )
        heads_ref[...] = (sum_ref[...] * kept + summed) / total
        square = jnp.zeros((requests, 128), jnp.float32)
        for h in range(HEADS):
            columns = slice(h * 128, (h + 1) * 128)
            attended = heads_ref[pl.ds(h, requests, stride=HEADS), :].astype(jnp.bfloat16)
            attended_ref[:, columns] = attended
            merged = (
                residual_ref[:, columns].astype(jnp.float32) + attended.astype(jnp.float32)
            ).astype(jnp.bfloat16)
            merged_ref[:, columns] = merged
            wide = merged.astype(jnp.float32)
            square = square + wide * wide
        mean = jnp.sum(square, axis=1, keepdims=True) * (1.0 / model_dim)
        inverse = lax.rsqrt(mean + epsilon)
        normed_ref[:, model_dim:] = routing_columns(ids_ref[...], gates_ref[...])
        normed_ref[:, :model_dim] = (
            merged_ref[...].astype(jnp.float32) * inverse * gain_ref[...]
        ).astype(jnp.bfloat16)

    shape = jax.ShapeDtypeStruct((requests, model_dim), jnp.bfloat16)
    return pl.pallas_call(
        kernel,
        out_shape=(shape, shape, jax.ShapeDtypeStruct((requests, model_dim + 128), jnp.bfloat16)),
        in_specs=[VMEM] * 3 + [SMEM] + [VMEM] * 7,
        out_specs=(VMEM,) * 3,
        scratch_shapes=[pltpu.VMEM((rows, 128), jnp.float32)],
        compiler_params=pltpu.CompilerParams(vmem_limit_bytes=16 * MEBI),
        cost_estimate=pl.CostEstimate(
            flops=4 * rows * half * tokens, bytes_accessed=4 * MEBI, transcendentals=rows * tokens
        ),
        name="finish_attention",
    )(query, fetched, table, lengths, *partial, residual, gain, ids, gates)


def local(
    queries,
    new_kv,
    kv_pages,
    page_table,
    lengths,
    shed_slots,
    residual,
    norm_gain,
    expert_ids,
    gate_weights,
    w_gate_up,
    w_down,
):
    count_of_rows, model_dim = queries.shape
    top_count = expert_ids.shape[1]
    layout = Layout(lax.axis_size("pool"), lax.axis_size("dev"))
    capacity = 2 * count_of_rows * top_count // (layout.pool * layout.dev)
    planes = layout.planes

    requested = from_behind(shed_slots, "pool", 1)
    picked = pick_pages(requested, kv_pages)
    fetched = from_behind(picked, "pool", 1)
    queries, expert_ids, picked = lax.optimization_barrier((queries, expert_ids, picked))

    expert = (lax.axis_index("pool") * layout.dev + lax.axis_index("dev")).reshape(1)
    *partial, query = own_attention(queries, new_kv, kv_pages, page_table, lengths)
    attended, merged, normed = finish_attention(
        query,
        fetched,
        page_table,
        lengths,
        partial,
        residual,
        norm_gain.reshape(1, model_dim),
        expert_ids.T,
        gate_weights.T,
        kv_pages.shape[0],
    )

    near = list(range(1, planes // 2 + 1))
    far = [0, *range(planes // 2 + 1, planes)]
    chips = range(0, layout.members, 2)
    blocks = [normed]
    for s in range(1, planes):
        blocks.append(layout.shifted(blocks[s ^ 1], 1) if s & 1 else layout.shifted(normed, s))
    arrived = []
    for s, block in enumerate(blocks):
        ready = [block] * len(chips)
        if 0 < s <= len(near):
            ready = [after(block, part) for part in arrived[0]]
        arrived.append([layout.swapped(rows, chip) for rows, chip in zip(ready, chips)])

    def to_experts(some, tie):
        pieces = [arrived[s][c] for c in range(len(chips)) for s in some]
        if tie is not None:
            pieces[0] = after(pieces[0], tie)
        own = packed(pieces)
        return own, layout.swapped(own, 1), layout.members * len(some) * capacity

    def add_cores(mine, over):
        cuts = [count_of_rows] * (mine.shape[0] // count_of_rows)
        return list(add_up([[mine], [over]], cuts, "add_cores"))

    def to_owners(sums, i):
        pieces = len(sums) // len(chips)
        return [layout.swapped(sums[c * pieces + i], chip) for c, chip in enumerate(chips)]

    def total_of(parts):
        return add_up([[part] for part in parts], [count_of_rows], "add_chips")[0]

    own, other, slots = to_experts(near, blocks[far[-1]])
    mine, over, kept = run_experts(own, other, (w_gate_up, w_down), expert, top_count, slots, True)
    near_mine, near_back = mine, layout.swapped(over, 1)
    own, other, slots = to_experts(far, over)
    near_sums = add_up(
        [[near_mine], [near_back]], [count_of_rows * len(near)] * len(chips), "add_cores"
    )
    other = after(other, near_sums[0])
    mine, over, _ = run_experts(own, other, kept, expert, top_count, slots, False)
    parts = to_owners(near_sums, 0)
    over = after(over, parts[1], parts[2])
    far_sums = add_cores(mine, layout.swapped(over, 1))
    totals = add_up([[part] for part in parts], [count_of_rows] * len(near), "add_chips")
    far_totals = [total_of(to_owners(far_sums, i)) for i in range(len(far) - 1, 0, -1)]
    last = to_owners(far_sums, 0)
    others = []
    for total, by in list(zip(totals, near))[::-1]:
        others.append(layout.shifted(total, by))
    others += [layout.shifted(total, by) for total, by in zip(far_totals, far[:0:-1])]
    merged = add_up(
        [[merged]] + [[part] for part in others], [count_of_rows], "add_first", 10**10
    )[0]
    layer_out = add_up([[merged]] + [[part] for part in last], [count_of_rows], "add_last")[0]
    return (attended, layer_out)


def solution(mesh):
    return jax.shard_map(
        local,
        mesh=mesh,
        in_specs=(
            P(("pool", "dev"), None),
            P(("pool", "dev"), None),
            P(("pool", "dev"), None, None),
            P(("pool", "dev"), None),
            P(("pool", "dev")),
            P(("pool", "dev")),
            P(("pool", "dev"), None),
            P(),
            P(("pool", "dev"), None),
            P(("pool", "dev"), None),
            P(("pool", "dev"), None, None),
            P(("pool", "dev"), None, None),
        ),
        out_specs=(P(("pool", "dev"), None), P(("pool", "dev"), None)),
        check_vma=False,
    )
```

```python
import math

import jax
import jax.numpy as jnp
from jax import lax
from jax.experimental import pallas as pl
from jax.experimental.pallas import tpu as pltpu
from jax.sharding import PartitionSpec as P

HEAD_DIMENSION = 128
KEY_VALUE_HEADS = 2
QUERY_GROUP_SIZE = 16
HEADS = KEY_VALUE_HEADS * QUERY_GROUP_SIZE

masked_score = -1e30
epsilon = 1e-06
AXES = ("pool", "dev")
VMEM = pl.BlockSpec(memory_space=pltpu.VMEM)
SMEM = pl.BlockSpec(memory_space=pltpu.SMEM)
HBM = pl.BlockSpec(memory_space=pltpu.HBM)
MEBI = 1 << 20
EXPERT_LIMIT = 16 * MEBI


def in_hbm(value):
    return pltpu.with_memory_space_constraint(value, pltpu.HBM)


class Layout:
    def __init__(self, pool, dev):
        self.pool, self.dev = pool, dev
        self.inner = math.gcd(dev, 4)
        self.planes = dev // self.inner
        self.members = pool * self.inner
        self.groups = [
            [self.linear(member, plane) for member in range(self.members)]
            for plane in range(self.planes)
        ]

    def linear(self, member, plane):
        return member // self.inner * self.dev + plane * self.inner + member % self.inner

    def shifted(self, value, by):
        if by == 0:
            return value
        pairs = [
            (self.linear(m, z), self.linear(m, z ^ by))
            for z in range(self.planes)
            for m in range(self.members)
        ]
        with jax.named_scope(f"plane_{by}"):
            return lax.ppermute(value, AXES, pairs)

    def swapped(self, value, by):
        if by == 0:
            return value
        pairs = [
            (self.linear(m, z), self.linear(m ^ by, z))
            for z in range(self.planes)
            for m in range(self.members)
        ]
        with jax.named_scope(f"member_{by}"):
            return lax.ppermute(value, AXES, pairs)


def from_behind(value, axis, by):
    length = lax.axis_size(axis)
    return lax.ppermute(value, axis, [(i, (i + by) % length) for i in range(length)])


def pick_pages(slots, pages):
    count = slots.shape[0]
    last = pages.shape[0] - 1

    def kernel(slots_ref, pages_ref, out_ref, sems):
        copies = []
        for i in range(count):
            page = jnp.clip(slots_ref[i], 0, last)
            copies.append(pltpu.make_async_copy(pages_ref.at[page], out_ref.at[i], sems.at[i]))
            copies[-1].start()
        for copy in copies:
            copy.wait()

    return pl.pallas_call(
        kernel,
        out_shape=jax.ShapeDtypeStruct((count,) + pages.shape[1:], pages.dtype),
        in_specs=[SMEM, HBM],
        out_specs=VMEM,
        scratch_shapes=[pltpu.SemaphoreType.DMA((count,))],
        compiler_params=pltpu.CompilerParams(vmem_limit_bytes=4 * MEBI),
        cost_estimate=pl.CostEstimate(flops=0, bytes_accessed=MEBI, transcendentals=0),
        name="pick_pages",
    )(slots, in_hbm(pages))


def head_blocks(query):
    rows = query.shape[0]
    head = lax.broadcasted_iota(jnp.int32, (rows, HEAD_DIMENSION), 0) % HEADS
    nothing = jnp.zeros_like(query)
    low = head < QUERY_GROUP_SIZE
    return jnp.concatenate([jnp.where(low, query, nothing), jnp.where(low, nothing, query)], axis=1)


def own_head(both):
    rows = both.shape[0]
    head = lax.broadcasted_iota(jnp.int32, (rows, HEAD_DIMENSION), 0) % HEADS
    return jnp.where(
        head < QUERY_GROUP_SIZE, both[:, :HEAD_DIMENSION], both[:, HEAD_DIMENSION:]
    )


def tokens_of_pages(table, lengths_ref, first, page_len):
    count_of_rows, width = table.shape
    page = lax.broadcasted_iota(jnp.int32, (count_of_rows, 128), 1) + first
    row = lax.broadcasted_iota(jnp.int32, (count_of_rows, 128), 0)
    lengths = jnp.zeros((count_of_rows, 128), jnp.int32)
    for r in range(count_of_rows):
        lengths = jnp.where(row == r, lengths_ref[r], lengths)
    held = jnp.zeros((count_of_rows, 128), jnp.float32)
    for p in range(width):
        filled = jnp.clip(lengths - p * page_len, 0, page_len).astype(jnp.float32)
        held = held + jnp.where(table[:, p : p + 1] == page, filled, 0.0)
    return held


def token_bias(held, first_page, tokens, page_len):
    page = lax.broadcasted_iota(jnp.int32, (128, tokens), 0)
    token = lax.broadcasted_iota(jnp.int32, (128, tokens), 1)
    widen = (page == token // page_len + first_page).astype(jnp.bfloat16)
    limit = jnp.dot(held.astype(jnp.bfloat16), widen, preferred_element_type=jnp.float32)
    inside = (token[: held.shape[0]] % page_len).astype(jnp.float32)
    return jnp.where(inside < limit, 0.0, masked_score)


def masked_scores(blocks, keys, bias, scaling):
    scores = lax.dot_general(
        blocks, keys, (((1,), (1,)), ((), ())), preferred_element_type=jnp.float32
    )
    requests, tokens = bias.shape
    return (
        (scores * scaling).reshape(requests, HEADS, tokens) + bias[:, None, :]
    ).reshape(requests * HEADS, tokens)


def narrowed(value, join):
    result = value[:, :128]
    for start in range(128, value.shape[1], 128):
        result = join(result, value[:, start : start + 128])
    return result


def own_attention(queries, new_kv, pages, table, lengths):
    page_count, page_len, kv_width = pages.shape
    requests = new_kv.shape[0]
    rows = requests * HEADS
    half = kv_width // 2
    chunk_pages = 128 * (page_count // 128) // 4
    chunk = chunk_pages * page_len
    chunks = page_count // chunk_pages
    scaling = 1.0 / math.sqrt(HEAD_DIMENSION)

    def kernel(
        queries_hbm,
        new_hbm,
        pages_hbm,
        table_hbm,
        lengths_hbm,
        out_ref,
        top_ref,
        sum_ref,
        query_ref,
        s_ref,
        fresh_ref,
        heads_ref,
        flat_ref,
        pages_ref,
        table_ref,
        lengths_ref,
        sems,
    ):
        page_copies = [
            pltpu.make_async_copy(
                pages_hbm.at[pl.ds(c * chunk_pages, chunk_pages)],
                pages_ref.at[pl.ds(c * chunk_pages, chunk_pages)],
                sems.at[4 + c],
            )
            for c in range(chunks)
        ]
        copies = [
            pltpu.make_async_copy(queries_hbm, flat_ref, sems.at[0]),
            pltpu.make_async_copy(table_hbm, table_ref, sems.at[1]),
            pltpu.make_async_copy(lengths_hbm, lengths_ref, sems.at[2]),
            pltpu.make_async_copy(new_hbm, fresh_ref.at[pl.ds(0, requests)], sems.at[3]),
        ]
        fresh_ref[requests:] = jnp.zeros_like(fresh_ref[requests:])
        for copy in copies + page_copies:
            copy.start()
        for copy in copies:
            copy.wait()
        for h in range(HEADS):
            heads_ref[pl.ds(h, requests, stride=HEADS), :] = flat_ref[
                :, h * 128 : (h + 1) * 128
            ].astype(jnp.float32)
        query = heads_ref[...].astype(jnp.bfloat16)
        query_ref[...] = query
        blocks = head_blocks(query)
        held = tokens_of_pages(table_ref[...], lengths_ref, 0, page_len)
        lane = lax.broadcasted_iota(jnp.int32, (requests, 128), 1)
        own = lax.broadcasted_iota(jnp.int32, (requests, 128), 0)
        fresh_bias = jnp.where(lane == own, 0.0, masked_score)
        fresh = masked_scores(blocks, fresh_ref[:, :half], fresh_bias, scaling)
        s_ref[:, chunks * chunk :] = fresh
        top = fresh
        for c in range(chunks):
            page_copies[c].wait()
            keys = pages_ref[c * chunk_pages : (c + 1) * chunk_pages, :, :half].reshape(chunk, half)
            bias = token_bias(held, c * chunk_pages, chunk, page_len)
            scores = masked_scores(blocks, keys, bias, scaling)
            s_ref[:, c * chunk : (c + 1) * chunk] = scores
            top = jnp.maximum(top, narrowed(scores, jnp.maximum))
        top = jnp.max(top, axis=1, keepdims=True)
        weights = jnp.exp(s_ref[:, chunks * chunk :] - top)
        total = weights
        summed = jnp.dot(
            weights.astype(jnp.bfloat16), fresh_ref[:, half:], preferred_element_type=jnp.float32
        )
        for c in range(chunks):
            values = pages_ref[c * chunk_pages : (c + 1) * chunk_pages, :, half:].reshape(chunk, half)
            weights = jnp.exp(s_ref[:, c * chunk : (c + 1) * chunk] - top)
            total = total + narrowed(weights, jnp.add)
            summed = summed + jnp.dot(
                weights.astype(jnp.bfloat16), values, preferred_element_type=jnp.float32
            )
        out_ref[...] = own_head(summed)
        top_ref[...] = jnp.broadcast_to(top, top_ref.shape)
        sum_ref[...] = jnp.broadcast_to(jnp.sum(total, axis=1, keepdims=True), sum_ref.shape)

    shape = jax.ShapeDtypeStruct((rows, 128), jnp.float32)
    return pl.pallas_call(
        kernel,
        out_shape=(shape, shape, shape, jax.ShapeDtypeStruct((rows, 128), jnp.bfloat16)),
        in_specs=[HBM] * 5,
        out_specs=(VMEM,) * 4,
        scratch_shapes=[
            pltpu.VMEM((rows, chunks * chunk + 128), jnp.float32),
            pltpu.VMEM((128, kv_width), jnp.bfloat16),
            pltpu.VMEM((rows, 128), jnp.float32),
            pltpu.VMEM(queries.shape, jnp.bfloat16),
            pltpu.VMEM(pages.shape, jnp.bfloat16),
            pltpu.VMEM(table.shape, jnp.int32),
            pltpu.SMEM(lengths.shape, jnp.int32),
            pltpu.SemaphoreType.DMA((4 + chunks,)),
        ],
        compiler_params=pltpu.CompilerParams(vmem_limit_bytes=24 * MEBI),
        cost_estimate=pl.CostEstimate(
            flops=4 * rows * half * chunks * chunk,
            bytes_accessed=16 * MEBI,
            transcendentals=rows * chunks * chunk,
        ),
        name="own_attention",
    )(*[in_hbm(value) for value in (queries, new_kv, pages, table, lengths)])


def routing_columns(ids, gates):
    top_count = ids.shape[0]
    high = gates.astype(jnp.bfloat16)
    rest = gates - high.astype(jnp.float32)
    middle = rest.astype(jnp.bfloat16)
    low = (rest - middle.astype(jnp.float32)).astype(jnp.bfloat16)
    source = lax.broadcasted_iota(jnp.int32, (top_count, 128), 0)
    lane = lax.broadcasted_iota(jnp.int32, (top_count, 128), 1)
    columns = 0.0
    for i, part in enumerate((ids.astype(jnp.float32).astype(jnp.bfloat16), high, middle, low)):
        place = (lane == source + i * top_count).astype(jnp.bfloat16)
        columns = columns + lax.dot_general(
            part, place, (((0,), (0,)), ((), ())), preferred_element_type=jnp.float32
        )
    return columns.astype(jnp.bfloat16)


def stacked(parts):
    if len(parts) == 1:
        return parts[0]
    return jnp.concatenate(parts, axis=0)


def packed(parts, work=0):
    if len(parts) == 1 and not work:
        return parts[0]
    rows = sum(part.shape[0] for part in parts)
    columns = parts[0].shape[1]

    def kernel(*refs):
        out_ref, offset = refs[-1], 0
        for ref in refs[:-1]:
            out_ref[offset : offset + ref.shape[0]] = ref[...]
            offset += ref.shape[0]

    return pl.pallas_call(
        kernel,
        out_shape=jax.ShapeDtypeStruct((rows, columns), parts[0].dtype),
        in_specs=[VMEM] * len(parts),
        out_specs=VMEM,
        compiler_params=pltpu.CompilerParams(vmem_limit_bytes=12 * MEBI),
        cost_estimate=pl.CostEstimate(flops=work, bytes_accessed=0, transcendentals=0),
        name="packed",
    )(*parts)


def after(value, *others):
    return lax.optimization_barrier((value, *others))[0]


def run_experts(own, other, weights, expert, top_count, slots, keep):
    rows, model_dim = own.shape
    rows, model_dim = 2 * rows, model_dim - 128
    gate_up, down_proj = weights
    double, hidden_dim = gate_up.shape[-1], down_proj.shape[-2]
    width = 256
    up_steps = hidden_dim // width
    out_width = 1024 if rows <= 512 else 512
    out_steps = model_dim // out_width
    strip = 256

    def kernel(expert_ref, own_ref, other_ref, *refs):
        copies = {}
        if keep:
            up_hbm, down_hbm, out_ref, over_ref, up_ref, down_ref, tokens_ref, hidden_ref, sems = refs
            for c in range(up_steps):
                for half in range(2):
                    columns = pl.ds(half * hidden_dim + c * width, width)
                    copies["up", c, half] = pltpu.make_async_copy(
                        up_hbm.at[0, :, columns], up_ref.at[:, columns], sems.at[2 * c + half]
                    )
            for c in range(out_steps):
                columns = pl.ds(c * out_width, out_width)
                copies["down", c] = pltpu.make_async_copy(
                    down_hbm.at[0, :, columns], down_ref.at[:, columns], sems.at[2 * up_steps + c]
                )
            for copy in copies.values():
                copy.start()
        else:
            up_ref, down_ref, out_ref, over_ref, tokens_ref, hidden_ref = refs

        def arrive(*name):
            if keep:
                copies[name].wait()

        token_refs = [own_ref, other_ref]
        routing = stacked([ref[:, model_dim:] for ref in token_refs]).astype(jnp.float32)
        wanted = expert_ref[0].astype(jnp.float32)
        match = jnp.zeros((rows, 1), jnp.float32)
        gates = [jnp.zeros((rows, 1), jnp.float32)] * 3
        for k in range(top_count):
            hit = routing[:, k : k + 1] == wanted
            match = jnp.where(hit, 1.0, match)
            gates = [
                jnp.where(hit, routing[:, i * top_count + k : i * top_count + k + 1], gate)
                for i, gate in enumerate(gates, 1)
            ]
        lane = lax.broadcasted_iota(jnp.int32, (rows, slots), 1)
        match = jnp.broadcast_to(match, (rows, slots))
        earlier = (
            lax.broadcasted_iota(jnp.int32, (strip, strip), 0)
            > lax.broadcasted_iota(jnp.int32, (strip, strip), 1)
        ).astype(jnp.bfloat16)
        ranks, before = [], jnp.zeros((1, slots), jnp.float32)
        for start in range(0, rows, strip):
            piece = match[start : start + strip]
            ranks.append(
                before
                + jnp.dot(earlier, piece.astype(jnp.bfloat16), preferred_element_type=jnp.float32)
            )
            before = before + jnp.sum(piece, axis=0, keepdims=True)
        rank = stacked(ranks)
        choice = jnp.where(rank == lane.astype(jnp.float32), match, 0.0)
        pick = choice.T.astype(jnp.bfloat16)
        place = choice.astype(jnp.bfloat16)
        gate_columns = jnp.where(
            lane == 0, gates[0], jnp.where(lane == 1, gates[1], jnp.where(lane == 2, gates[2], 0.0))
        ).astype(jnp.bfloat16)
        gate = jnp.sum(
            jnp.dot(pick, gate_columns, preferred_element_type=jnp.float32), axis=1, keepdims=True
        )
        for start in range(0, model_dim, out_width):
            columns = slice(start, start + out_width)
            tokens = stacked([ref[:, columns] for ref in token_refs])
            tokens_ref[:, columns] = jnp.dot(
                pick, tokens, preferred_element_type=jnp.float32
            ).astype(jnp.bfloat16)

        for c in range(up_steps):
            arrive("up", c, 0)
            arrive("up", c, 1)
            start = c * width
            tokens = tokens_ref[...]
            gated = jnp.dot(
                tokens, up_ref[:, start : start + width], preferred_element_type=jnp.float32
            )
            up = jnp.dot(
                tokens,
                up_ref[:, hidden_dim + start : hidden_dim + start + width],
                preferred_element_type=jnp.float32,
            )
            hidden_ref[:, start : start + width] = (gated / (1.0 + jnp.exp(-gated)) * up).astype(
                jnp.bfloat16
            )

        for c in range(out_steps):
            arrive("down", c)
            columns = slice(c * out_width, (c + 1) * out_width)
            result = jnp.dot(
                hidden_ref[...], down_ref[:, columns], preferred_element_type=jnp.float32
            )
            result = (result * gate).astype(jnp.bfloat16)
            sums = jnp.dot(place, result, preferred_element_type=jnp.float32).astype(jnp.bfloat16)
            out_ref[:, columns] = sums[: rows // 2]
            over_ref[:, columns] = sums[rows // 2 :]

    shape = jax.ShapeDtypeStruct((rows // 2, model_dim), jnp.bfloat16)
    kept, scratch = (), []
    if keep:
        kept = (
            pltpu.VMEM((model_dim, double), jnp.bfloat16),
            pltpu.VMEM((hidden_dim, model_dim), jnp.bfloat16),
        )
        scratch = [pltpu.SemaphoreType.DMA((2 * up_steps + out_steps,))]
        weights = [in_hbm(gate_up), in_hbm(down_proj)]
    else:
        weights = [pltpu.with_memory_space_constraint(value, pltpu.VMEM) for value in weights]
    results = pl.pallas_call(
        kernel,
        out_shape=(shape, shape) + kept,
        in_specs=[SMEM, VMEM, VMEM] + [HBM if keep else VMEM] * 2,
        out_specs=(VMEM,) * (2 + len(kept)),
        scratch_shapes=[
            pltpu.VMEM((slots, model_dim), jnp.bfloat16),
            pltpu.VMEM((slots, hidden_dim), jnp.bfloat16),
        ]
        + scratch,
        compiler_params=pltpu.CompilerParams(vmem_limit_bytes=EXPERT_LIMIT),
        cost_estimate=pl.CostEstimate(
            flops=6 * slots * model_dim * hidden_dim,
            bytes_accessed=20 * MEBI,
            transcendentals=slots * hidden_dim,
        ),
        name="run_experts",
    )(expert, own, other, *weights)
    return results[0], results[1], results[2:]


def add_up(parts, cuts, name, work=0):
    rows = sum(cuts)
    model_dim = parts[0][0].shape[1]
    flat = [piece for part in parts for piece in part]
    places = []
    for part in parts:
        start = 0
        for piece in part:
            places.append((start, start + piece.shape[0]))
            start += piece.shape[0]

    def kernel(*refs):
        in_refs, out_refs = refs[: len(flat)], refs[len(flat) :]
        step = 1024
        for start in range(0, model_dim, step):
            columns = slice(start, start + step)
            offset = 0
            for out_ref, cut in zip(out_refs, cuts):
                total = 0.0
                for ref, (low, high) in zip(in_refs, places):
                    if low <= offset and offset + cut <= high:
                        rows_of = slice(offset - low, offset - low + cut)
                        total = total + ref[rows_of, columns].astype(jnp.float32)
                out_ref[:, columns] = total.astype(jnp.bfloat16)
                offset += cut

    return pl.pallas_call(
        kernel,
        out_shape=tuple(jax.ShapeDtypeStruct((cut, model_dim), jnp.bfloat16) for cut in cuts),
        in_specs=[VMEM] * len(flat),
        out_specs=(VMEM,) * len(cuts),
        compiler_params=pltpu.CompilerParams(vmem_limit_bytes=12 * MEBI),
        cost_estimate=pl.CostEstimate(
            flops=work, bytes_accessed=0, transcendentals=0
        ),
        name=name,
    )(*flat)


def finish_attention(
    query, fetched, table, lengths, partial, residual, gain, ids, gates, pages_own
):
    count, page_len, kv_width = fetched.shape
    half = kv_width // 2
    tokens = count * page_len
    requests, model_dim = residual.shape
    rows = query.shape[0]
    scaling = 1.0 / math.sqrt(HEAD_DIMENSION)

    def kernel(q_ref, fetched_ref, table_ref, lengths_ref, sum_ref, top_ref, total_ref, residual_ref, gain_ref, ids_ref, gates_ref, attended_ref, merged_ref, normed_ref, heads_ref):
        blocks = head_blocks(q_ref[...])
        held = tokens_of_pages(table_ref[...], lengths_ref, pages_own, page_len)
        bias = token_bias(held, 0, tokens, page_len)
        keys = fetched_ref[:, :, :half].reshape(tokens, half)
        values = fetched_ref[:, :, half:].reshape(tokens, half)
        scores = masked_scores(blocks, keys, bias, scaling)
        before = top_ref[...]
        shed_top = jnp.max(narrowed(scores, jnp.maximum), axis=1, keepdims=True)
        top = jnp.maximum(before, shed_top)
        kept = jnp.exp(before - top)
        weights = jnp.exp(scores - jnp.concatenate([top] * (tokens // 128), axis=1))
        added = jnp.sum(narrowed(weights, jnp.add), axis=1, keepdims=True)
        total = total_ref[...] * kept + added
        summed = own_head(
            jnp.dot(weights.astype(jnp.bfloat16), values, preferred_element_type=jnp.float32)
        )
        heads_ref[...] = (sum_ref[...] * kept + summed) / total
        square = jnp.zeros((requests, 128), jnp.float32)
        for h in range(HEADS):
            columns = slice(h * 128, (h + 1) * 128)
            attended = heads_ref[pl.ds(h, requests, stride=HEADS), :].astype(jnp.bfloat16)
            attended_ref[:, columns] = attended
            merged = (
                residual_ref[:, columns].astype(jnp.float32) + attended.astype(jnp.float32)
            ).astype(jnp.bfloat16)
            merged_ref[:, columns] = merged
            wide = merged.astype(jnp.float32)
            square = square + wide * wide
        mean = jnp.sum(square, axis=1, keepdims=True) * (1.0 / model_dim)
        inverse = lax.rsqrt(mean + epsilon)
        normed_ref[:, model_dim:] = routing_columns(ids_ref[...], gates_ref[...])
        normed_ref[:, :model_dim] = (
            merged_ref[...].astype(jnp.float32) * inverse * gain_ref[...]
        ).astype(jnp.bfloat16)

    shape = jax.ShapeDtypeStruct((requests, model_dim), jnp.bfloat16)
    return pl.pallas_call(
        kernel,
        out_shape=(shape, shape, jax.ShapeDtypeStruct((requests, model_dim + 128), jnp.bfloat16)),
        in_specs=[VMEM] * 3 + [SMEM] + [VMEM] * 7,
        out_specs=(VMEM,) * 3,
        scratch_shapes=[pltpu.VMEM((rows, 128), jnp.float32)],
        compiler_params=pltpu.CompilerParams(vmem_limit_bytes=16 * MEBI),
        cost_estimate=pl.CostEstimate(
            flops=4 * rows * half * tokens, bytes_accessed=4 * MEBI, transcendentals=rows * tokens
        ),
        name="finish_attention",
    )(query, fetched, table, lengths, *partial, residual, gain, ids, gates)


def local(
    queries,
    new_kv,
    kv_pages,
    page_table,
    lengths,
    shed_slots,
    residual,
    norm_gain,
    expert_ids,
    gate_weights,
    w_gate_up,
    w_down,
):
    count_of_rows, model_dim = queries.shape
    top_count = expert_ids.shape[1]
    layout = Layout(lax.axis_size("pool"), lax.axis_size("dev"))
    capacity = 2 * count_of_rows * top_count // (layout.pool * layout.dev)
    planes = layout.planes

    requested = from_behind(shed_slots, "pool", 1)
    picked = pick_pages(requested, kv_pages)
    fetched = from_behind(picked, "pool", 1)
    queries, expert_ids, picked = lax.optimization_barrier((queries, expert_ids, picked))

    expert = (lax.axis_index("pool") * layout.dev + lax.axis_index("dev")).reshape(1)
    *partial, query = own_attention(queries, new_kv, kv_pages, page_table, lengths)
    attended, merged, normed = finish_attention(
        query,
        fetched,
        page_table,
        lengths,
        partial,
        residual,
        norm_gain.reshape(1, model_dim),
        expert_ids.T,
        gate_weights.T,
        kv_pages.shape[0],
    )

    near = list(range(1, planes // 2 + 1))
    far = [0, *range(planes // 2 + 1, planes)]
    chips = range(0, layout.members, 2)
    blocks = [normed]
    for s in range(1, planes):
        blocks.append(layout.shifted(blocks[s ^ 1], 1) if s & 1 else layout.shifted(normed, s))
    arrived = []
    for s, block in enumerate(blocks):
        ready = [block] * len(chips)
        if 0 < s <= len(near):
            ready = [after(block, part) for part in arrived[0]]
        arrived.append([layout.swapped(rows, chip) for rows, chip in zip(ready, chips)])

    def to_experts(some, tie):
        pieces = [arrived[s][c] for c in range(len(chips)) for s in some]
        if tie is not None:
            pieces[0] = after(pieces[0], tie)
        own = packed(pieces)
        return own, layout.swapped(own, 1), layout.members * len(some) * capacity

    def add_cores(mine, over):
        cuts = [count_of_rows] * (mine.shape[0] // count_of_rows)
        return list(add_up([[mine], [over]], cuts, "add_cores"))

    def to_owners(sums, i):
        pieces = len(sums) // len(chips)
        return [layout.swapped(sums[c * pieces + i], chip) for c, chip in enumerate(chips)]

    def total_of(parts):
        return add_up([[part] for part in parts], [count_of_rows], "add_chips")[0]

    own, other, slots = to_experts(near, blocks[far[-1]])
    mine, over, kept = run_experts(own, other, (w_gate_up, w_down), expert, top_count, slots, True)
    near_mine, near_back = mine, layout.swapped(over, 1)
    own, other, slots = to_experts(far, over)
    near_sums = add_up(
        [[near_mine], [near_back]], [count_of_rows * len(near)] * len(chips), "add_cores"
    )
    other = after(other, near_sums[0])
    mine, over, _ = run_experts(own, other, kept, expert, top_count, slots, False)
    parts = to_owners(near_sums, 0)
    over = after(over, parts[1], parts[2])
    far_sums = add_cores(mine, layout.swapped(over, 1))
    totals = add_up([[part] for part in parts], [count_of_rows] * len(near), "add_chips")
    others = [layout.shifted(total, by) for total, by in list(zip(totals, near))[::-1]]
    for i, by in list(enumerate(far))[:0:-1]:
        first = total_of(to_owners(far_sums, i))
        others.append(layout.shifted(first, by))
    for c in (1, 2, 3):
        far_sums[c * len(far)] = after(far_sums[c * len(far)], first)
    merged = add_up(
        [[merged]] + [[part] for part in others], [count_of_rows], "add_first", 10**10
    )[0]
    others = [total_of(to_owners(far_sums, 0))]
    total = merged.astype(jnp.float32) + sum(part.astype(jnp.float32) for part in others)
    layer_out = total.astype(jnp.bfloat16)
    return (attended, layer_out)


def solution(mesh):
    return jax.shard_map(
        local,
        mesh=mesh,
        in_specs=(
            P(("pool", "dev"), None),
            P(("pool", "dev"), None),
            P(("pool", "dev"), None, None),
            P(("pool", "dev"), None),
            P(("pool", "dev")),
            P(("pool", "dev")),
            P(("pool", "dev"), None),
            P(),
            P(("pool", "dev"), None),
            P(("pool", "dev"), None),
            P(("pool", "dev"), None, None),
            P(("pool", "dev"), None, None),
        ),
        out_specs=(P(("pool", "dev"), None), P(("pool", "dev"), None)),
        check_vma=False,
    )
```

```python
import math

import jax
import jax.numpy as jnp
from jax import lax
from jax.experimental import pallas as pl
from jax.experimental.pallas import tpu as pltpu
from jax.sharding import PartitionSpec as P

HEAD_DIMENSION = 128
KEY_VALUE_HEADS = 2
QUERY_GROUP_SIZE = 16
HEADS = KEY_VALUE_HEADS * QUERY_GROUP_SIZE

masked_score = -1e30
epsilon = 1e-06
AXES = ("pool", "dev")
VMEM = pl.BlockSpec(memory_space=pltpu.VMEM)
SMEM = pl.BlockSpec(memory_space=pltpu.SMEM)
HBM = pl.BlockSpec(memory_space=pltpu.HBM)
MEBI = 1 << 20
EXPERT_LIMIT = 16 * MEBI


def in_hbm(value):
    return pltpu.with_memory_space_constraint(value, pltpu.HBM)


class Layout:
    def __init__(self, pool, dev):
        self.pool, self.dev = pool, dev
        self.inner = math.gcd(dev, 4)
        self.planes = dev // self.inner
        self.members = pool * self.inner
        self.groups = [
            [self.linear(member, plane) for member in range(self.members)]
            for plane in range(self.planes)
        ]

    def linear(self, member, plane):
        return member // self.inner * self.dev + plane * self.inner + member % self.inner

    def shifted(self, value, by):
        if by == 0:
            return value
        pairs = [
            (self.linear(m, z), self.linear(m, z ^ by))
            for z in range(self.planes)
            for m in range(self.members)
        ]
        with jax.named_scope(f"plane_{by}"):
            return lax.ppermute(value, AXES, pairs)

    def swapped(self, value, by):
        if by == 0:
            return value
        pairs = [
            (self.linear(m, z), self.linear(m ^ by, z))
            for z in range(self.planes)
            for m in range(self.members)
        ]
        with jax.named_scope(f"member_{by}"):
            return lax.ppermute(value, AXES, pairs)


def from_behind(value, axis, by):
    length = lax.axis_size(axis)
    return lax.ppermute(value, axis, [(i, (i + by) % length) for i in range(length)])


def pick_pages(slots, pages):
    count = slots.shape[0]
    last = pages.shape[0] - 1

    def kernel(slots_ref, pages_ref, out_ref, sems):
        copies = []
        for i in range(count):
            page = jnp.clip(slots_ref[i], 0, last)
            copies.append(pltpu.make_async_copy(pages_ref.at[page], out_ref.at[i], sems.at[i]))
            copies[-1].start()
        for copy in copies:
            copy.wait()

    return pl.pallas_call(
        kernel,
        out_shape=jax.ShapeDtypeStruct((count,) + pages.shape[1:], pages.dtype),
        in_specs=[SMEM, HBM],
        out_specs=VMEM,
        scratch_shapes=[pltpu.SemaphoreType.DMA((count,))],
        compiler_params=pltpu.CompilerParams(vmem_limit_bytes=4 * MEBI),
        cost_estimate=pl.CostEstimate(flops=0, bytes_accessed=MEBI, transcendentals=0),
        name="pick_pages",
    )(slots, in_hbm(pages))


def head_blocks(query):
    rows = query.shape[0]
    head = lax.broadcasted_iota(jnp.int32, (rows, HEAD_DIMENSION), 0) % HEADS
    nothing = jnp.zeros_like(query)
    low = head < QUERY_GROUP_SIZE
    return jnp.concatenate([jnp.where(low, query, nothing), jnp.where(low, nothing, query)], axis=1)


def own_head(both):
    rows = both.shape[0]
    head = lax.broadcasted_iota(jnp.int32, (rows, HEAD_DIMENSION), 0) % HEADS
    return jnp.where(
        head < QUERY_GROUP_SIZE, both[:, :HEAD_DIMENSION], both[:, HEAD_DIMENSION:]
    )


def tokens_of_pages(table, lengths_ref, first, page_len):
    count_of_rows, width = table.shape
    page = lax.broadcasted_iota(jnp.int32, (count_of_rows, 128), 1) + first
    row = lax.broadcasted_iota(jnp.int32, (count_of_rows, 128), 0)
    lengths = jnp.zeros((count_of_rows, 128), jnp.int32)
    for r in range(count_of_rows):
        lengths = jnp.where(row == r, lengths_ref[r], lengths)
    held = jnp.zeros((count_of_rows, 128), jnp.float32)
    for p in range(width):
        filled = jnp.clip(lengths - p * page_len, 0, page_len).astype(jnp.float32)
        held = held + jnp.where(table[:, p : p + 1] == page, filled, 0.0)
    return held


def token_bias(held, first_page, tokens, page_len):
    page = lax.broadcasted_iota(jnp.int32, (128, tokens), 0)
    token = lax.broadcasted_iota(jnp.int32, (128, tokens), 1)
    widen = (page == token // page_len + first_page).astype(jnp.bfloat16)
    limit = jnp.dot(held.astype(jnp.bfloat16), widen, preferred_element_type=jnp.float32)
    inside = (token[: held.shape[0]] % page_len).astype(jnp.float32)
    return jnp.where(inside < limit, 0.0, masked_score)


def masked_scores(blocks, keys, bias, scaling):
    scores = lax.dot_general(
        blocks, keys, (((1,), (1,)), ((), ())), preferred_element_type=jnp.float32
    )
    requests, tokens = bias.shape
    return (
        (scores * scaling).reshape(requests, HEADS, tokens) + bias[:, None, :]
    ).reshape(requests * HEADS, tokens)


def narrowed(value, join):
    result = value[:, :128]
    for start in range(128, value.shape[1], 128):
        result = join(result, value[:, start : start + 128])
    return result


def own_attention(queries, new_kv, pages, table, lengths):
    page_count, page_len, kv_width = pages.shape
    requests = new_kv.shape[0]
    rows = requests * HEADS
    half = kv_width // 2
    chunk_pages = 128 * (page_count // 128) // 4
    chunk = chunk_pages * page_len
    chunks = page_count // chunk_pages
    scaling = 1.0 / math.sqrt(HEAD_DIMENSION)

    def kernel(
        queries_hbm,
        new_hbm,
        pages_hbm,
        table_hbm,
        lengths_hbm,
        out_ref,
        top_ref,
        sum_ref,
        query_ref,
        s_ref,
        fresh_ref,
        heads_ref,
        flat_ref,
        pages_ref,
        table_ref,
        lengths_ref,
        sems,
    ):
        page_copies = [
            pltpu.make_async_copy(
                pages_hbm.at[pl.ds(c * chunk_pages, chunk_pages)],
                pages_ref.at[pl.ds(c * chunk_pages, chunk_pages)],
                sems.at[4 + c],
            )
            for c in range(chunks)
        ]
        copies = [
            pltpu.make_async_copy(queries_hbm, flat_ref, sems.at[0]),
            pltpu.make_async_copy(table_hbm, table_ref, sems.at[1]),
            pltpu.make_async_copy(lengths_hbm, lengths_ref, sems.at[2]),
            pltpu.make_async_copy(new_hbm, fresh_ref.at[pl.ds(0, requests)], sems.at[3]),
        ]
        fresh_ref[requests:] = jnp.zeros_like(fresh_ref[requests:])
        for copy in copies + page_copies:
            copy.start()
        for copy in copies:
            copy.wait()
        for h in range(HEADS):
            heads_ref[pl.ds(h, requests, stride=HEADS), :] = flat_ref[
                :, h * 128 : (h + 1) * 128
            ].astype(jnp.float32)
        query = heads_ref[...].astype(jnp.bfloat16)
        query_ref[...] = query
        blocks = head_blocks(query)
        held = tokens_of_pages(table_ref[...], lengths_ref, 0, page_len)
        lane = lax.broadcasted_iota(jnp.int32, (requests, 128), 1)
        own = lax.broadcasted_iota(jnp.int32, (requests, 128), 0)
        fresh_bias = jnp.where(lane == own, 0.0, masked_score)
        fresh = masked_scores(blocks, fresh_ref[:, :half], fresh_bias, scaling)
        s_ref[:, chunks * chunk :] = fresh
        top = fresh
        for c in range(chunks):
            page_copies[c].wait()
            keys = pages_ref[c * chunk_pages : (c + 1) * chunk_pages, :, :half].reshape(chunk, half)
            bias = token_bias(held, c * chunk_pages, chunk, page_len)
            scores = masked_scores(blocks, keys, bias, scaling)
            s_ref[:, c * chunk : (c + 1) * chunk] = scores
            top = jnp.maximum(top, narrowed(scores, jnp.maximum))
        top = jnp.max(top, axis=1, keepdims=True)
        weights = jnp.exp(s_ref[:, chunks * chunk :] - top)
        total = weights
        summed = jnp.dot(
            weights.astype(jnp.bfloat16), fresh_ref[:, half:], preferred_element_type=jnp.float32
        )
        for c in range(chunks):
            values = pages_ref[c * chunk_pages : (c + 1) * chunk_pages, :, half:].reshape(chunk, half)
            weights = jnp.exp(s_ref[:, c * chunk : (c + 1) * chunk] - top)
            total = total + narrowed(weights, jnp.add)
            summed = summed + jnp.dot(
                weights.astype(jnp.bfloat16), values, preferred_element_type=jnp.float32
            )
        out_ref[...] = own_head(summed)
        top_ref[...] = jnp.broadcast_to(top, top_ref.shape)
        sum_ref[...] = jnp.broadcast_to(jnp.sum(total, axis=1, keepdims=True), sum_ref.shape)

    shape = jax.ShapeDtypeStruct((rows, 128), jnp.float32)
    return pl.pallas_call(
        kernel,
        out_shape=(shape, shape, shape, jax.ShapeDtypeStruct((rows, 128), jnp.bfloat16)),
        in_specs=[HBM] * 5,
        out_specs=(VMEM,) * 4,
        scratch_shapes=[
            pltpu.VMEM((rows, chunks * chunk + 128), jnp.float32),
            pltpu.VMEM((128, kv_width), jnp.bfloat16),
            pltpu.VMEM((rows, 128), jnp.float32),
            pltpu.VMEM(queries.shape, jnp.bfloat16),
            pltpu.VMEM(pages.shape, jnp.bfloat16),
            pltpu.VMEM(table.shape, jnp.int32),
            pltpu.SMEM(lengths.shape, jnp.int32),
            pltpu.SemaphoreType.DMA((4 + chunks,)),
        ],
        compiler_params=pltpu.CompilerParams(vmem_limit_bytes=24 * MEBI),
        cost_estimate=pl.CostEstimate(
            flops=4 * rows * half * chunks * chunk,
            bytes_accessed=16 * MEBI,
            transcendentals=rows * chunks * chunk,
        ),
        name="own_attention",
    )(*[in_hbm(value) for value in (queries, new_kv, pages, table, lengths)])


def routing_columns(ids, gates):
    top_count = ids.shape[0]
    high = gates.astype(jnp.bfloat16)
    rest = gates - high.astype(jnp.float32)
    middle = rest.astype(jnp.bfloat16)
    low = (rest - middle.astype(jnp.float32)).astype(jnp.bfloat16)
    source = lax.broadcasted_iota(jnp.int32, (top_count, 128), 0)
    lane = lax.broadcasted_iota(jnp.int32, (top_count, 128), 1)
    columns = 0.0
    for i, part in enumerate((ids.astype(jnp.float32).astype(jnp.bfloat16), high, middle, low)):
        place = (lane == source + i * top_count).astype(jnp.bfloat16)
        columns = columns + lax.dot_general(
            part, place, (((0,), (0,)), ((), ())), preferred_element_type=jnp.float32
        )
    return columns.astype(jnp.bfloat16)


def stacked(parts):
    if len(parts) == 1:
        return parts[0]
    return jnp.concatenate(parts, axis=0)


def packed(parts, work=0):
    if len(parts) == 1 and not work:
        return parts[0]
    rows = sum(part.shape[0] for part in parts)
    columns = parts[0].shape[1]

    def kernel(*refs):
        out_ref, offset = refs[-1], 0
        for ref in refs[:-1]:
            out_ref[offset : offset + ref.shape[0]] = ref[...]
            offset += ref.shape[0]

    return pl.pallas_call(
        kernel,
        out_shape=jax.ShapeDtypeStruct((rows, columns), parts[0].dtype),
        in_specs=[VMEM] * len(parts),
        out_specs=VMEM,
        compiler_params=pltpu.CompilerParams(vmem_limit_bytes=12 * MEBI),
        cost_estimate=pl.CostEstimate(flops=work, bytes_accessed=0, transcendentals=0),
        name="packed",
    )(*parts)


def after(value, *others):
    return lax.optimization_barrier((value, *others))[0]


def run_experts(own, other, weights, expert, top_count, slots, keep):
    rows, model_dim = own.shape
    rows, model_dim = 2 * rows, model_dim - 128
    gate_up, down_proj = weights
    double, hidden_dim = gate_up.shape[-1], down_proj.shape[-2]
    width = 256
    up_steps = hidden_dim // width
    out_width = 1024 if rows <= 512 else 512
    out_steps = model_dim // out_width
    strip = 256
    cuts = 4

    def kernel(expert_ref, own_ref, other_ref, *refs):
        copies = {}
        if keep:
            up_hbm, down_hbm, out_ref, over_ref, up_ref, down_ref, tokens_ref, hidden_ref, sems = refs
            for c in range(up_steps):
                for part in range(2 * cuts):
                    columns = pl.ds(part // cuts * hidden_dim + c * width, width)
                    lines = pl.ds(part % cuts * (model_dim // cuts), model_dim // cuts)
                    copies["up", c, part] = pltpu.make_async_copy(
                        up_hbm.at[0, lines, columns],
                        up_ref.at[lines, columns],
                        sems.at[2 * cuts * c + part],
                    )
            for c in range(out_steps):
                columns = pl.ds(c * out_width, out_width)
                copies["down", c] = pltpu.make_async_copy(
                    down_hbm.at[0, :, columns],
                    down_ref.at[:, columns],
                    sems.at[2 * cuts * up_steps + c],
                )
            for copy in copies.values():
                copy.start()
        else:
            up_ref, down_ref, out_ref, over_ref, tokens_ref, hidden_ref = refs

        def arrive(*name):
            if keep:
                copies[name].wait()

        token_refs = [own_ref, other_ref]
        routing = stacked([ref[:, model_dim:] for ref in token_refs]).astype(jnp.float32)
        wanted = expert_ref[0].astype(jnp.float32)
        match = jnp.zeros((rows, 1), jnp.float32)
        gates = [jnp.zeros((rows, 1), jnp.float32)] * 3
        for k in range(top_count):
            hit = routing[:, k : k + 1] == wanted
            match = jnp.where(hit, 1.0, match)
            gates = [
                jnp.where(hit, routing[:, i * top_count + k : i * top_count + k + 1], gate)
                for i, gate in enumerate(gates, 1)
            ]
        lane = lax.broadcasted_iota(jnp.int32, (rows, slots), 1)
        match = jnp.broadcast_to(match, (rows, slots))
        earlier = (
            lax.broadcasted_iota(jnp.int32, (strip, strip), 0)
            > lax.broadcasted_iota(jnp.int32, (strip, strip), 1)
        ).astype(jnp.bfloat16)
        ranks, before = [], jnp.zeros((1, slots), jnp.float32)
        for start in range(0, rows, strip):
            piece = match[start : start + strip]
            ranks.append(
                before
                + jnp.dot(earlier, piece.astype(jnp.bfloat16), preferred_element_type=jnp.float32)
            )
            before = before + jnp.sum(piece, axis=0, keepdims=True)
        rank = stacked(ranks)
        choice = jnp.where(rank == lane.astype(jnp.float32), match, 0.0)
        pick = choice.T.astype(jnp.bfloat16)
        place = choice.astype(jnp.bfloat16)
        gate_columns = jnp.where(
            lane == 0, gates[0], jnp.where(lane == 1, gates[1], jnp.where(lane == 2, gates[2], 0.0))
        ).astype(jnp.bfloat16)
        gate = jnp.sum(
            jnp.dot(pick, gate_columns, preferred_element_type=jnp.float32), axis=1, keepdims=True
        )
        for start in range(0, model_dim, out_width):
            columns = slice(start, start + out_width)
            tokens = stacked([ref[:, columns] for ref in token_refs])
            tokens_ref[:, columns] = jnp.dot(
                pick, tokens, preferred_element_type=jnp.float32
            ).astype(jnp.bfloat16)

        for c in range(up_steps):
            for part in range(2 * cuts):
                arrive("up", c, part)
            start = c * width
            tokens = tokens_ref[...]
            gated = jnp.dot(
                tokens, up_ref[:, start : start + width], preferred_element_type=jnp.float32
            )
            up = jnp.dot(
                tokens,
                up_ref[:, hidden_dim + start : hidden_dim + start + width],
                preferred_element_type=jnp.float32,
            )
            hidden_ref[:, start : start + width] = (gated / (1.0 + jnp.exp(-gated)) * up).astype(
                jnp.bfloat16
            )

        for c in range(out_steps):
            arrive("down", c)
            columns = slice(c * out_width, (c + 1) * out_width)
            result = jnp.dot(
                hidden_ref[...], down_ref[:, columns], preferred_element_type=jnp.float32
            )
            result = (result * gate).astype(jnp.bfloat16)
            sums = jnp.dot(place, result, preferred_element_type=jnp.float32).astype(jnp.bfloat16)
            out_ref[:, columns] = sums[: rows // 2]
            over_ref[:, columns] = sums[rows // 2 :]

    shape = jax.ShapeDtypeStruct((rows // 2, model_dim), jnp.bfloat16)
    kept, scratch = (), []
    if keep:
        kept = (
            pltpu.VMEM((model_dim, double), jnp.bfloat16),
            pltpu.VMEM((hidden_dim, model_dim), jnp.bfloat16),
        )
        scratch = [pltpu.SemaphoreType.DMA((2 * cuts * up_steps + out_steps,))]
        weights = [in_hbm(gate_up), in_hbm(down_proj)]
    else:
        weights = [pltpu.with_memory_space_constraint(value, pltpu.VMEM) for value in weights]
    results = pl.pallas_call(
        kernel,
        out_shape=(shape, shape) + kept,
        in_specs=[SMEM, VMEM, VMEM] + [HBM if keep else VMEM] * 2,
        out_specs=(VMEM,) * (2 + len(kept)),
        scratch_shapes=[
            pltpu.VMEM((slots, model_dim), jnp.bfloat16),
            pltpu.VMEM((slots, hidden_dim), jnp.bfloat16),
        ]
        + scratch,
        compiler_params=pltpu.CompilerParams(vmem_limit_bytes=EXPERT_LIMIT),
        cost_estimate=pl.CostEstimate(
            flops=6 * slots * model_dim * hidden_dim,
            bytes_accessed=20 * MEBI,
            transcendentals=slots * hidden_dim,
        ),
        name="run_experts",
    )(expert, own, other, *weights)
    return results[0], results[1], results[2:]


def add_up(parts, cuts, name, work=0):
    rows = sum(cuts)
    model_dim = parts[0][0].shape[1]
    flat = [piece for part in parts for piece in part]
    places = []
    for part in parts:
        start = 0
        for piece in part:
            places.append((start, start + piece.shape[0]))
            start += piece.shape[0]

    def kernel(*refs):
        in_refs, out_refs = refs[: len(flat)], refs[len(flat) :]
        step = 1024
        for start in range(0, model_dim, step):
            columns = slice(start, start + step)
            offset = 0
            for out_ref, cut in zip(out_refs, cuts):
                total = 0.0
                for ref, (low, high) in zip(in_refs, places):
                    if low <= offset and offset + cut <= high:
                        rows_of = slice(offset - low, offset - low + cut)
                        total = total + ref[rows_of, columns].astype(jnp.float32)
                out_ref[:, columns] = total.astype(jnp.bfloat16)
                offset += cut

    return pl.pallas_call(
        kernel,
        out_shape=tuple(jax.ShapeDtypeStruct((cut, model_dim), jnp.bfloat16) for cut in cuts),
        in_specs=[VMEM] * len(flat),
        out_specs=(VMEM,) * len(cuts),
        compiler_params=pltpu.CompilerParams(vmem_limit_bytes=12 * MEBI),
        cost_estimate=pl.CostEstimate(
            flops=work, bytes_accessed=0, transcendentals=0
        ),
        name=name,
    )(*flat)


def finish_attention(
    query, fetched, table, lengths, partial, residual, gain, ids, gates, pages_own
):
    count, page_len, kv_width = fetched.shape
    half = kv_width // 2
    tokens = count * page_len
    requests, model_dim = residual.shape
    rows = query.shape[0]
    scaling = 1.0 / math.sqrt(HEAD_DIMENSION)

    def kernel(q_ref, fetched_ref, table_ref, lengths_ref, sum_ref, top_ref, total_ref, residual_ref, gain_ref, ids_ref, gates_ref, attended_ref, merged_ref, normed_ref, heads_ref):
        blocks = head_blocks(q_ref[...])
        held = tokens_of_pages(table_ref[...], lengths_ref, pages_own, page_len)
        bias = token_bias(held, 0, tokens, page_len)
        keys = fetched_ref[:, :, :half].reshape(tokens, half)
        values = fetched_ref[:, :, half:].reshape(tokens, half)
        scores = masked_scores(blocks, keys, bias, scaling)
        before = top_ref[...]
        shed_top = jnp.max(narrowed(scores, jnp.maximum), axis=1, keepdims=True)
        top = jnp.maximum(before, shed_top)
        kept = jnp.exp(before - top)
        weights = jnp.exp(scores - jnp.concatenate([top] * (tokens // 128), axis=1))
        added = jnp.sum(narrowed(weights, jnp.add), axis=1, keepdims=True)
        total = total_ref[...] * kept + added
        summed = own_head(
            jnp.dot(weights.astype(jnp.bfloat16), values, preferred_element_type=jnp.float32)
        )
        heads_ref[...] = (sum_ref[...] * kept + summed) / total
        square = jnp.zeros((requests, 128), jnp.float32)
        for h in range(HEADS):
            columns = slice(h * 128, (h + 1) * 128)
            attended = heads_ref[pl.ds(h, requests, stride=HEADS), :].astype(jnp.bfloat16)
            attended_ref[:, columns] = attended
            merged = (
                residual_ref[:, columns].astype(jnp.float32) + attended.astype(jnp.float32)
            ).astype(jnp.bfloat16)
            merged_ref[:, columns] = merged
            wide = merged.astype(jnp.float32)
            square = square + wide * wide
        mean = jnp.sum(square, axis=1, keepdims=True) * (1.0 / model_dim)
        inverse = lax.rsqrt(mean + epsilon)
        normed_ref[:, model_dim:] = routing_columns(ids_ref[...], gates_ref[...])
        normed_ref[:, :model_dim] = (
            merged_ref[...].astype(jnp.float32) * inverse * gain_ref[...]
        ).astype(jnp.bfloat16)

    shape = jax.ShapeDtypeStruct((requests, model_dim), jnp.bfloat16)
    return pl.pallas_call(
        kernel,
        out_shape=(shape, shape, jax.ShapeDtypeStruct((requests, model_dim + 128), jnp.bfloat16)),
        in_specs=[VMEM] * 3 + [SMEM] + [VMEM] * 7,
        out_specs=(VMEM,) * 3,
        scratch_shapes=[pltpu.VMEM((rows, 128), jnp.float32)],
        compiler_params=pltpu.CompilerParams(vmem_limit_bytes=16 * MEBI),
        cost_estimate=pl.CostEstimate(
            flops=4 * rows * half * tokens, bytes_accessed=4 * MEBI, transcendentals=rows * tokens
        ),
        name="finish_attention",
    )(query, fetched, table, lengths, *partial, residual, gain, ids, gates)


def local(
    queries,
    new_kv,
    kv_pages,
    page_table,
    lengths,
    shed_slots,
    residual,
    norm_gain,
    expert_ids,
    gate_weights,
    w_gate_up,
    w_down,
):
    count_of_rows, model_dim = queries.shape
    top_count = expert_ids.shape[1]
    layout = Layout(lax.axis_size("pool"), lax.axis_size("dev"))
    capacity = 2 * count_of_rows * top_count // (layout.pool * layout.dev)
    planes = layout.planes

    requested = from_behind(shed_slots, "pool", 1)
    picked = pick_pages(requested, kv_pages)
    fetched = from_behind(picked, "pool", 1)
    queries, expert_ids, picked = lax.optimization_barrier((queries, expert_ids, picked))

    expert = (lax.axis_index("pool") * layout.dev + lax.axis_index("dev")).reshape(1)
    *partial, query = own_attention(queries, new_kv, kv_pages, page_table, lengths)
    attended, merged, normed = finish_attention(
        query,
        fetched,
        page_table,
        lengths,
        partial,
        residual,
        norm_gain.reshape(1, model_dim),
        expert_ids.T,
        gate_weights.T,
        kv_pages.shape[0],
    )

    near = list(range(1, planes // 2 + 1))
    far = [0, *range(planes // 2 + 1, planes)]
    chips = range(0, layout.members, 2)
    blocks = [normed]
    for s in range(1, planes):
        blocks.append(layout.shifted(blocks[s ^ 1], 1) if s & 1 else layout.shifted(normed, s))
    arrived = []
    for s, block in enumerate(blocks):
        ready = [block] * len(chips)
        if 0 < s <= len(near):
            ready = [after(block, part) for part in arrived[0]]
        arrived.append([layout.swapped(rows, chip) for rows, chip in zip(ready, chips)])

    def to_experts(some, tie):
        pieces = [arrived[s][c] for c in range(len(chips)) for s in some]
        if tie is not None:
            pieces[0] = after(pieces[0], tie)
        own = packed(pieces)
        return own, layout.swapped(own, 1), layout.members * len(some) * capacity

    def add_cores(mine, over):
        cuts = [count_of_rows] * (mine.shape[0] // count_of_rows)
        return list(add_up([[mine], [over]], cuts, "add_cores"))

    def to_owners(sums, i):
        pieces = len(sums) // len(chips)
        return [layout.swapped(sums[c * pieces + i], chip) for c, chip in enumerate(chips)]

    def total_of(parts):
        return add_up([[part] for part in parts], [count_of_rows], "add_chips")[0]

    own, other, slots = to_experts(near, blocks[far[-1]])
    mine, over, kept = run_experts(own, other, (w_gate_up, w_down), expert, top_count, slots, True)
    near_mine, near_back = mine, layout.swapped(over, 1)
    own, other, slots = to_experts(far, over)
    near_sums = add_up(
        [[near_mine], [near_back]], [count_of_rows * len(near)] * len(chips), "add_cores"
    )
    other = after(other, near_sums[0])
    mine, over, _ = run_experts(own, other, kept, expert, top_count, slots, False)
    parts = to_owners(near_sums, 0)
    over = after(over, parts[1], parts[2])
    far_sums = add_cores(mine, layout.swapped(over, 1))
    totals = add_up([[part] for part in parts], [count_of_rows] * len(near), "add_chips")
    others = [layout.shifted(total, by) for total, by in list(zip(totals, near))[::-1]]
    for i, by in list(enumerate(far))[:0:-1]:
        first = total_of(to_owners(far_sums, i))
        others.append(layout.shifted(first, by))
    for c in (1, 2, 3):
        far_sums[c * len(far)] = after(far_sums[c * len(far)], first)
    merged = add_up(
        [[merged]] + [[part] for part in others], [count_of_rows], "add_first", 10**10
    )[0]
    others = [total_of(to_owners(far_sums, 0))]
    total = merged.astype(jnp.float32) + sum(part.astype(jnp.float32) for part in others)
    layer_out = total.astype(jnp.bfloat16)
    return (attended, layer_out)


def solution(mesh):
    return jax.shard_map(
        local,
        mesh=mesh,
        in_specs=(
            P(("pool", "dev"), None),
            P(("pool", "dev"), None),
            P(("pool", "dev"), None, None),
            P(("pool", "dev"), None),
            P(("pool", "dev")),
            P(("pool", "dev")),
            P(("pool", "dev"), None),
            P(),
            P(("pool", "dev"), None),
            P(("pool", "dev"), None),
            P(("pool", "dev"), None, None),
            P(("pool", "dev"), None, None),
        ),
        out_specs=(P(("pool", "dev"), None), P(("pool", "dev"), None)),
        check_vma=False,
    )
```
